32 devices in a mesh: ctx: 8 (over z, y), mp: 4 (over x, core).
Axes of the slice: x: 2, y: 2, z: 4, core: 2. Of those that a mesh axis runs over, the one named last changes fastest.
Arguments:
- block_in: bfloat16 [2048, 1024], P(('ctx', 'mp')), may hold values from -6 to 6
- attn_gain: float32 [1024], replicated, may hold values from 0.5 to 1.5
- query_weight: bfloat16 [1024, 1024], P(None, 'mp'), may hold values from -0.1875 to 0.1875
- key_weight: bfloat16 [1024, 512], P(None, 'mp'), may hold values from -0.1875 to 0.1875
- value_weight: bfloat16 [1024, 512], P(None, 'mp'), may hold values from -0.1875 to 0.1875
- out_weight: bfloat16 [1024, 1024], P('mp'), may hold values from -2.5 to 2.5
- query_gain: float32 [64], replicated, may hold values from 0.6 to 1.6
- key_gain: float32 [64], replicated, may hold values from 0.6 to 1.6
- ffn_gain: float32 [1024], replicated, may hold values from 0.5 to 1.5
- gate_weight: bfloat16 [1024, 4608], P(None, 'mp'), may hold values from -0.1875 to 0.1875
- up_weight: bfloat16 [1024, 4608], P(None, 'mp'), may hold values from -0.1875 to 0.1875
- down_weight: bfloat16 [4608, 1024], P('mp'), may hold values from -0.09375 to 0.09375
- segments: int32 [2048], replicated, may hold values from 0 to 4, as said below
- positions: int32 [2048], P('ctx'), may hold values from 0 to 1279, as said below
- cotangent: bfloat16 [2048, 1024], P(('ctx', 'mp')), may hold values from -6 to 6
Outputs:
- block_out: bfloat16 [2048, 1024], P(('ctx', 'mp'))
- grad_input: float32 [2048, 1024], P(('ctx', 'mp'))
- query_grad: float32 [1024, 1024], P('ctx', 'mp')
- key_grad: float32 [1024, 512], P('ctx', 'mp')
- value_grad: float32 [1024, 512], P('ctx', 'mp')
- out_grad: float32 [1024, 1024], P('mp', 'ctx')
- gate_grad: float32 [1024, 4608], P('ctx', 'mp')
- up_grad: float32 [1024, 4608], P('ctx', 'mp')
- down_grad: float32 [4608, 1024], P('mp', 'ctx')
- attn_gain_grad: float32 [1024], replicated
- ffn_gain_grad: float32 [1024], replicated
- query_gain_grad: float32 [64], replicated
- key_gain_grad: float32 [64], replicated
The draws below stay inside these ranges and needn't reach their ends.
Inputs may be any that keep to these rules, and one draw needn't show every extreme that they name: `segments`: never falls from a token to the next; every document number occurs; one document holds exactly 1280 tokens, no document more. `positions`: the token's index minus the index of the first token of its document.
All inputs are finite; a program needn't handle non-finite values.
Results may differ from the reference program's by a relative error of at most 0.023.
Values may be sent and summed in bfloat16 or wider, within the bound.
No kernel may reach another device: no remote copies, remote signals or barrier semaphores. Data moves between devices by JAX's collectives and lax.ppermute only.
A program may use at most 192 MiB of HBM per device.

```python
import jax
import jax.numpy as jnp
from jax import lax

D = 1024
HEADS = 16
KV_HEADS = 8
HD = 64
FF = 4608
NDOC = 5
TOK_DEV = 256
TOKENS = 2048


def document_layout(key):
    longest = TOKENS // 2 + TOK_DEV
    rest = TOKENS - longest
    others = NDOC - 1
    spread = rest // (4 * others)
    inner = jnp.arange(1, others, dtype=jnp.int32)
    jitter = jax.random.randint(jax.random.fold_in(key, 5), (others - 1,), -spread, spread + 1, dtype=jnp.int32)
    cuts = (inner * rest // others + jitter).astype(jnp.int32)
    bounds = jnp.concatenate([jnp.zeros((1,), jnp.int32), cuts, jnp.full((1,), rest, jnp.int32)])
    pieces = (bounds[1:] - bounds[:-1]).astype(jnp.int32)
    place = jax.random.randint(jax.random.fold_in(key, 7), (), 0, NDOC, dtype=jnp.int32)
    slot = jnp.arange(NDOC, dtype=jnp.int32)
    before = pieces[jnp.minimum(slot, others - 1)]
    later = pieces[jnp.maximum(slot - 1, 0)]
    lengths = jnp.where(slot == place, longest, jnp.where(slot < place, before, later)).astype(jnp.int32)
    starts = (jnp.cumsum(lengths) - lengths).astype(jnp.int32)
    index = jnp.arange(TOKENS, dtype=jnp.int32)
    after = index[:, None] >= starts[None, 1:]
    segment = jnp.sum(after.astype(jnp.int32), axis=1).astype(jnp.int32)
    begins = jnp.max(jnp.where(after, starts[None, 1:], 0), axis=1).astype(jnp.int32)
    return (segment, index - begins)


def draw_segments(key, part):
    return document_layout(key)[0]


def draw_positions(key, part):
    return document_layout(key)[1]


def head_gain(key, salt):
    return jax.random.uniform(jax.random.fold_in(key, salt), (HD,), jnp.float32, 0.6, 1.6)


def draw_query_gain(key, part):
    return head_gain(key, 3)


def draw_key_gain(key, part):
    return head_gain(key, 11)


def raised(result, key, source, target, parts, factor):
    owner, partner = [(jnp.arange(result.shape[position]) // (result.shape[position] // parts)).reshape([-1 if axis == position else 1 for axis in range(result.ndim)]) for position in (source, target)]
    chosen = jax.random.permutation(key, parts)[partner]
    strong = (owner == chosen) | (owner == (partner + parts // 2) % parts)
    return jnp.where(strong, factor * result, result)


def shard_levels(own_key, dims, split, smallest, high):
    loudness = 1.0
    for dim, shards_of in split:
        heights = jax.random.uniform(jax.random.fold_in(jax.random.fold_in(own_key, 6), dim), (shards_of,), jnp.float32, smallest / len(split), high / len(split))
        loudness = loudness * jnp.repeat(jnp.exp(heights), dims[dim] // shards_of).reshape((-1,) + (1,) * (len(dims) - 1 - dim))
    return loudness


def noise(own_key, extent, width, reach, cuts=(), kind=jnp.bfloat16):
    loudness = shard_levels(own_key, extent, cuts, -0.22, 0.18) if cuts else 1.0
    values = jax.random.normal(own_key, extent, jnp.float32) * width * loudness
    return jnp.minimum(jnp.maximum(values, -reach), reach).astype(kind)


def noise_with(rng, shape, width, reach, shards, heavy, held_as=jnp.bfloat16):
    values = width * jax.random.normal(rng, shape, jnp.float32)
    if shards:
        values = values * shard_levels(rng, shape, shards, -0.22, 0.18)
    return jnp.clip(raised(values, jax.random.fold_in(rng, 3), *heavy), -reach, reach).astype(held_as)


def setup_inputs(seed: int = 0) -> dict:
    splits = jax.random.split(jax.random.key(seed), 16)
    block_in = noise(splits[0], (TOKENS, D), 1.0, 6.0, ((0, 32),))
    attn_gain = jnp.clip(1.0 + 0.1 * jax.random.normal(splits[1], (D,), jnp.float32), 0.5, 1.5)
    query_weight = noise(splits[2], (D, HEADS * HD), D ** -0.5, 0.1875, ((1, 4),))
    key_weight = noise(splits[3], (D, KV_HEADS * HD), D ** -0.5, 0.1875, ((1, 4),))
    value_weight = noise(splits[4], (D, KV_HEADS * HD), D ** -0.5, 0.1875, ((1, 4),))
    out_weight = noise(splits[5], (HEADS * HD, D), (max(1, 2 * NDOC * HEADS * HD // TOKENS)) ** -0.5, 2.5, ((0, 4),))
    query_gain = draw_query_gain(jax.random.fold_in(splits[15], 71), 0)
    key_gain = draw_key_gain(jax.random.fold_in(splits[15], 71), 0)
    ffn_gain = jnp.clip(1.0 + 0.1 * jax.random.normal(splits[8], (D,), jnp.float32), 0.5, 1.5)
    gate_weight = noise(splits[9], (D, FF), D ** -0.5, 0.1875, ((1, 4),))
    up_weight = noise(splits[10], (D, FF), D ** -0.5, 0.1875, ((1, 4),))
    down_weight = noise(splits[11], (FF, D), FF ** -0.5, 0.09375, ((0, 4),))
    segments = draw_segments(jax.random.fold_in(splits[15], 71), 0)
    positions = draw_positions(jax.random.fold_in(splits[15], 71), 0)
    cotangent = noise_with(splits[14], (TOKENS, D), 1.0, 6.0, ((0, 32),), (0, 1, 32, 2.75))
    return {"block_in": block_in, "attn_gain": attn_gain, "query_weight": query_weight, "key_weight": key_weight, "value_weight": value_weight, "out_weight": out_weight, "query_gain": query_gain, "key_gain": key_gain, "ffn_gain": ffn_gain, "gate_weight": gate_weight, "up_weight": up_weight, "down_weight": down_weight, "segments": segments, "positions": positions, "cotangent": cotangent}


EPS = 1e-05
ROPE_BASE = 1000000.0
MASKED_SCORE = -1e+30

def norm_forward(values, gain):
    scale_row = lax.rsqrt(lax.optimization_barrier(jnp.mean(values * values, axis=-1, keepdims=True)) + EPS)
    return (values * scale_row * gain, scale_row)

def norm_backward(values, scale_row, gain, grad_out):
    normed = values * scale_row
    grad_normed = grad_out * gain
    grad_in = scale_row * (grad_normed - normed * lax.optimization_barrier(jnp.mean(grad_normed * normed, axis=-1, keepdims=True)))
    return (grad_in, grad_out * normed)

def rope_tables(positions):
    middle = HD // 2
    freqs = ROPE_BASE ** (-2.0 * jnp.arange(middle).astype(jnp.float32) / HD)
    angles = positions.astype(jnp.float32)[:, None] * freqs[None, :]
    return (jnp.cos(angles)[:, None, :], jnp.sin(angles)[:, None, :])

def rotate(values, cos_table, sin_table):
    middle = values.shape[-1] // 2
    front_part, back_part = (values[..., :middle], values[..., middle:])
    return jnp.concatenate([front_part * cos_table - back_part * sin_table, back_part * cos_table + front_part * sin_table], axis=-1)

def rotate_back(grads, cos_table, sin_table):
    middle = grads.shape[-1] // 2
    front_part, back_part = (grads[..., :middle], grads[..., middle:])
    return jnp.concatenate([front_part * cos_table + back_part * sin_table, back_part * cos_table - front_part * sin_table], axis=-1)

def widen(array):
    return lax.optimization_barrier(array.astype(jnp.bfloat16)).astype(jnp.float32)

def reference(block_in, attn_gain, query_weight, key_weight, value_weight, out_weight, query_gain, key_gain, ffn_gain, gate_weight, up_weight, down_weight, segments, positions, cotangent):
    group_size = HEADS // KV_HEADS
    softmax_scale = HD ** (-0.5)
    block_rows = min(512, TOKENS)
    block_count = TOKENS // block_rows
    inputs = block_in.astype(jnp.float32)
    normed_attn, scale_attn = norm_forward(inputs, attn_gain)
    act_attn = normed_attn.astype(jnp.bfloat16)
    queries = jnp.dot(act_attn, query_weight, preferred_element_type=jnp.float32).reshape(TOKENS, HEADS, HD)
    keys_pre = jnp.dot(act_attn, key_weight, preferred_element_type=jnp.float32).reshape(TOKENS, KV_HEADS, HD)
    value_rows = jnp.dot(act_attn, value_weight, preferred_element_type=jnp.float32).astype(jnp.bfloat16)
    query_normed, query_scale = norm_forward(queries, query_gain)
    key_normed, key_scale = norm_forward(keys_pre, key_gain)
    cos_table, sin_table = rope_tables(positions)
    query_rot = rotate(query_normed, cos_table, sin_table).astype(jnp.bfloat16)
    key_rot = rotate(key_normed, cos_table, sin_table).astype(jnp.bfloat16)
    key_wide = key_rot.astype(jnp.float32)
    value_wide = value_rows.astype(jnp.float32).reshape(TOKENS, KV_HEADS, HD)
    token_index = jnp.arange(TOKENS, dtype=jnp.int32)
    query_blocks = query_rot.astype(jnp.float32).reshape(block_count, block_rows, KV_HEADS, group_size, HD)
    index_blocks = token_index.reshape(block_count, block_rows)
    segment_blocks = segments.reshape(block_count, block_rows)

    def visible_of(query_index, query_segment):
        return (query_segment[:, None] == segments[None, :]) & (query_index[:, None] >= token_index[None, :])

    def forward_block(operands):
        query_block, query_index, query_segment = operands
        visible = visible_of(query_index, query_segment)
        scores = jnp.einsum('qkgd,tkd->kgqt', query_block, key_wide) * softmax_scale
        row_max = lax.optimization_barrier(jnp.max(jnp.where(visible, scores, MASKED_SCORE), axis=-1, keepdims=True))
        attn_prob = jnp.exp(jnp.where(visible, scores - row_max, MASKED_SCORE))
        row_sum = lax.optimization_barrier(jnp.sum(attn_prob, axis=-1, keepdims=True))
        mixed = jnp.einsum('kgqt,tkd->qkgd', widen(attn_prob), value_wide) / jnp.transpose(row_sum, (2, 0, 1, 3))
        return (mixed, (row_max + jnp.log(row_sum))[..., 0])
    attn_out, log_sums = lax.map(forward_block, (query_blocks, index_blocks, segment_blocks))
    attn_flat = attn_out.reshape(TOKENS, HEADS * HD)
    attn_b = attn_flat.astype(jnp.bfloat16)
    resid = inputs + jnp.dot(attn_b, out_weight, preferred_element_type=jnp.float32)
    normed_ffn, scale_ffn = norm_forward(resid, ffn_gain)
    act_ffn = normed_ffn.astype(jnp.bfloat16)
    gate_pre = jnp.dot(act_ffn, gate_weight, preferred_element_type=jnp.float32)
    up_proj = jnp.dot(act_ffn, up_weight, preferred_element_type=jnp.float32)
    sigmoid_gate = jax.nn.sigmoid(gate_pre)
    hidden = (gate_pre * sigmoid_gate * up_proj).astype(jnp.bfloat16)
    block_out = (resid + jnp.dot(hidden, down_weight, preferred_element_type=jnp.float32)).astype(jnp.bfloat16)
    down_grad = jnp.dot(hidden.T, cotangent, preferred_element_type=jnp.float32)
    grad_hidden = jnp.dot(cotangent, down_weight.T, preferred_element_type=jnp.float32)
    grad_gate = (grad_hidden * up_proj * sigmoid_gate * (1.0 + gate_pre * (1.0 - sigmoid_gate))).astype(jnp.bfloat16)
    grad_up = (grad_hidden * gate_pre * sigmoid_gate).astype(jnp.bfloat16)
    gate_grad = jnp.dot(act_ffn.T, grad_gate, preferred_element_type=jnp.float32)
    up_grad = jnp.dot(act_ffn.T, grad_up, preferred_element_type=jnp.float32)
    grad_act_ffn = jnp.dot(grad_gate, gate_weight.T, preferred_element_type=jnp.float32) + jnp.dot(grad_up, up_weight.T, preferred_element_type=jnp.float32)
    grad_norm_ffn, gain_terms_ffn = norm_backward(resid, scale_ffn, ffn_gain, grad_act_ffn)
    ffn_gain_grad = lax.optimization_barrier(jnp.sum(gain_terms_ffn, axis=0))
    grad_resid = cotangent.astype(jnp.float32) + grad_norm_ffn
    grad_resid_b = grad_resid.astype(jnp.bfloat16)
    out_grad = jnp.dot(attn_b.T, grad_resid_b, preferred_element_type=jnp.float32)
    grad_attn = jnp.dot(grad_resid_b, out_weight.T, preferred_element_type=jnp.float32).reshape(TOKENS, KV_HEADS, group_size, HD)
    delta = lax.optimization_barrier(jnp.sum(grad_attn * attn_flat.reshape(TOKENS, KV_HEADS, group_size, HD), axis=-1))
    grad_blocks = widen(grad_attn).reshape(block_count, block_rows, KV_HEADS, group_size, HD)
    delta_blocks = delta.reshape(block_count, block_rows, KV_HEADS, group_size)

    def backward_block(carried, operands):
        key_acc, value_acc = carried
        query_block, query_index, query_segment, grad_block, delta_block, lse_block = operands
        visible = visible_of(query_index, query_segment)
        scores = jnp.einsum('qkgd,tkd->kgqt', query_block, key_wide) * softmax_scale
        attn_prob = jnp.exp(jnp.where(visible, scores - lse_block[..., None], MASKED_SCORE))
        grad_prob = jnp.einsum('qkgd,tkd->kgqt', grad_block, value_wide)
        grad_scores = widen(attn_prob * (grad_prob - jnp.transpose(delta_block, (1, 2, 0))[..., None]) * softmax_scale)
        grad_query = jnp.einsum('kgqt,tkd->qkgd', grad_scores, key_wide)
        key_acc = key_acc + jnp.einsum('kgqt,qkgd->tkd', grad_scores, query_block)
        value_acc = value_acc + jnp.einsum('kgqt,qkgd->tkd', widen(attn_prob), grad_block)
        return ((key_acc, value_acc), grad_query)
    zero_keys = jnp.zeros((TOKENS, KV_HEADS, HD), jnp.float32)
    (grad_key_rot, grad_value), grad_query_rot = lax.scan(backward_block, (zero_keys, zero_keys), (query_blocks, index_blocks, segment_blocks, grad_blocks, delta_blocks, log_sums))
    grad_query_rot = grad_query_rot.reshape(TOKENS, HEADS, HD)
    grad_queries, gain_terms_query = norm_backward(queries, query_scale, query_gain, rotate_back(grad_query_rot, cos_table, sin_table))
    grad_keys, gain_terms_key = norm_backward(keys_pre, key_scale, key_gain, rotate_back(grad_key_rot, cos_table, sin_table))
    query_gain_grad = lax.optimization_barrier(jnp.sum(gain_terms_query, axis=(0, 1)))
    key_gain_grad = lax.optimization_barrier(jnp.sum(gain_terms_key, axis=(0, 1)))
    grad_query_b = grad_queries.reshape(TOKENS, HEADS * HD).astype(jnp.bfloat16)
    grad_key_b = grad_keys.reshape(TOKENS, KV_HEADS * HD).astype(jnp.bfloat16)
    grad_value_b = grad_value.reshape(TOKENS, KV_HEADS * HD).astype(jnp.bfloat16)
    query_grad = jnp.dot(act_attn.T, grad_query_b, preferred_element_type=jnp.float32)
    key_grad = jnp.dot(act_attn.T, grad_key_b, preferred_element_type=jnp.float32)
    value_grad = jnp.dot(act_attn.T, grad_value_b, preferred_element_type=jnp.float32)
    grad_act_attn = jnp.dot(grad_query_b, query_weight.T, preferred_element_type=jnp.float32) + jnp.dot(grad_key_b, key_weight.T, preferred_element_type=jnp.float32) + jnp.dot(grad_value_b, value_weight.T, preferred_element_type=jnp.float32)
    grad_norm_attn, gain_terms_attn = norm_backward(inputs, scale_attn, attn_gain, grad_act_attn)
    attn_gain_grad = lax.optimization_barrier(jnp.sum(gain_terms_attn, axis=0))
    grad_input = grad_resid + grad_norm_attn
    return (block_out, grad_input, query_grad, key_grad, value_grad, out_grad, gate_grad, up_grad, down_grad, attn_gain_grad, ffn_gain_grad, query_gain_grad, key_gain_grad)
```

```python
import jax
import jax.numpy as jnp
from jax import lax
from jax.sharding import PartitionSpec as P

HEADS = 16
KV_HEADS = 8
HD = 64
EPS = 1e-05
ROPE_BASE = 1000000.0
MASKED_SCORE = -1e30
LONGEST = {2048: 1280, 8192: 4352}
BF = jnp.bfloat16
F32 = jnp.float32
ROWS = (((0,), (0,)), ((), ()))
COLS = (((1,), (1,)), ((), ()))


def dot(a, b, dims=(((1,), (0,)), ((), ()))):
    return lax.dot_general(a, b, dims, preferred_element_type=F32)


def norm_forward(values, gain):
    scale_row = lax.rsqrt(jnp.mean(values * values, axis=-1, keepdims=True) + EPS)
    return (values * scale_row * gain, scale_row)


def norm_backward(values, scale_row, gain, grad_out):
    normed = values * scale_row
    grad_normed = grad_out * gain
    grad_in = scale_row * (
        grad_normed - normed * jnp.mean(grad_normed * normed, axis=-1, keepdims=True)
    )
    return (grad_in, grad_out * normed)


def rope_tables(positions):
    middle = HD // 2
    freqs = ROPE_BASE ** (-2.0 * jnp.arange(middle).astype(F32) / HD)
    angles = positions.astype(F32)[:, None] * freqs[None, :]
    return (jnp.cos(angles)[:, None, :], jnp.sin(angles)[:, None, :])


def rotate(values, cos_table, sin_table):
    middle = values.shape[-1] // 2
    front_part, back_part = (values[..., :middle], values[..., middle:])
    return jnp.concatenate(
        [
            front_part * cos_table - back_part * sin_table,
            back_part * cos_table + front_part * sin_table,
        ],
        axis=-1,
    )


def xor(values, axis, mask):
    n = lax.axis_size(axis)
    return lax.ppermute(values, axis, [(i, i ^ mask) for i in range(n)])


def up(values, step):
    n = lax.axis_size("ctx")
    return lax.ppermute(values, "ctx", [(i, i + step) for i in range(n - step)])


def down(values, step):
    n = lax.axis_size("ctx")
    return lax.ppermute(values, "ctx", [(i, i - step) for i in range(step, n)])


def mp_gather(values):
    other = xor(values, "mp", 2)
    core = xor(values, "mp", 1)
    return jnp.concatenate([values, other, core, xor(other, "mp", 1)], axis=0)


def mp_reduce(partial):
    half = partial.shape[0] // 2
    kept = partial[:half] + xor(partial[half:].astype(BF), "mp", 1).astype(F32)
    own = half // 2
    return kept[:own] + xor(kept[own:].astype(BF), "mp", 2).astype(F32)


def mp_allreduce(partial):
    half = partial.shape[0] // 2
    kept = (partial[:half] + xor(partial[half:].astype(BF), "mp", 1).astype(F32)).astype(BF)
    other = xor(kept, "mp", 2)
    own = half // 2
    other = jnp.concatenate([other[own:], other[:own]], axis=0)
    both = (kept.astype(F32) + other.astype(F32)).astype(BF)
    return jnp.concatenate([both, xor(both, "mp", 1)], axis=0).astype(F32)


def mp_order(values):
    rank = lax.axis_index("mp")
    parts = values.reshape(2, 2, -1)
    parts = jnp.swapaxes(parts, 0, 1)
    parts = jnp.where(rank % 2 == 1, parts[::-1], parts)
    parts = jnp.where(rank // 2 == 1, parts[:, ::-1], parts)
    return parts.reshape(values.shape)


def split_columns(values):
    n = lax.axis_size("ctx")
    index = lax.axis_index("ctx")
    rows, columns = values.shape
    parts = values.reshape((rows,) + (2,) * (n.bit_length() - 1) + (columns // n,))
    bits = n.bit_length() - 1
    for bit in range(bits):
        axis = bits - bit
        parts = jnp.where((index >> bit) % 2 == 1, jnp.flip(parts, axis), parts)
    parts = jnp.moveaxis(parts, bits, 1)
    order = [0, 1] + [bits - b + 1 for b in range(1, bits)] + [bits + 1]
    parts = jnp.transpose(parts, order)
    parts = parts.reshape(rows, 2, columns // 2)
    return parts[:, 0], parts[:, 1]


def halve(make, size, axis):
    n = lax.axis_size("ctx")
    mask = 2
    arrived = xor(make(size // 2, size).astype(BF), "ctx", mask)
    total = make(0, size // 2) + arrived.astype(F32)
    while mask * 2 < n:
        size //= 2
        mask *= 2
        front = lax.slice_in_dim(total, 0, size // 2, axis=axis)
        back = lax.slice_in_dim(total, size // 2, size, axis=axis)
        total = front + xor(back.astype(BF), "ctx", mask).astype(F32)
    return total


def body(
    block_in,
    attn_gain,
    query_weight,
    key_weight,
    value_weight,
    out_weight,
    query_gain,
    key_gain,
    ffn_gain,
    gate_weight,
    up_weight,
    down_weight,
    segments,
    positions,
    cotangent,
):
    group_size = HEADS // KV_HEADS
    key_heads = key_weight.shape[1] // HD
    query_heads = query_weight.shape[1] // HD
    softmax_scale = HD ** (-0.5)
    n_ctx = lax.axis_size("ctx")
    ctx_rank = lax.axis_index("ctx")
    own_rows = block_in.shape[0]
    rows = positions.shape[0]
    total_tokens = rows * n_ctx
    longest = LONGEST.get(total_tokens, total_tokens)
    window = min(n_ctx - 1, -(-(longest - 1) // rows))
    slots = (window + 1) // 2

    inputs = mp_gather(block_in).astype(F32)
    cot = mp_gather(cotangent)
    place = mp_order(jnp.arange(rows, dtype=jnp.int32))
    positions = mp_order(positions)
    normed_attn, scale_attn = norm_forward(inputs, attn_gain)
    act_attn = normed_attn.astype(BF)

    keys_pre = dot(act_attn, key_weight).reshape(rows, key_heads, HD)
    value_rows = dot(act_attn, value_weight).astype(BF)
    queries = dot(act_attn, query_weight).reshape(rows, query_heads, HD)
    key_normed, key_scale = norm_forward(keys_pre, key_gain)
    cos_table, sin_table = rope_tables(positions)
    key_rot = rotate(key_normed, cos_table, sin_table).astype(BF).reshape(rows, key_heads * HD)
    pair = jnp.concatenate([key_rot, value_rows], axis=1)

    odd_rank = ctx_rank % 2 == 1
    items = [pair] + [up(pair, 2 * k) for k in range(1, slots + 1) if 2 * k < n_ctx]
    while len(items) < slots + 1:
        items.append(jnp.zeros_like(pair))
    blocks = {0: pair}
    for k in range(1, slots + 1):
        if 2 * k <= window:
            blocks[2 * k] = items[k]
    for j in range(slots):
        blocks[2 * j + 1] = xor(jnp.where(odd_rank, items[j + 1], items[j]), "ctx", 1)
    count = window + 1
    keys = jnp.concatenate([blocks[d] for d in range(count)], axis=0)

    query_normed, query_scale = norm_forward(queries, query_gain)
    query_rot = (
        rotate(query_normed, cos_table, sin_table)
        .astype(BF)
        .reshape(rows, key_heads, group_size, HD)
    )
    query_index = ctx_rank * rows + place
    first_seen = query_index - positions
    key_index = (
        (ctx_rank - jnp.arange(count, dtype=jnp.int32))[:, None] * rows + place[None, :]
    ).reshape(-1)
    visible = (key_index[None, :] <= query_index[:, None]) & (
        key_index[None, :] >= first_seen[:, None]
    )
    key_block = keys[:, : key_heads * HD].reshape(count * rows, key_heads, HD)
    value_block = keys[:, key_heads * HD :].reshape(count * rows, key_heads, HD)
    scores = (
        jnp.einsum("qkgd,tkd->kgqt", query_rot, key_block, preferred_element_type=F32)
        * softmax_scale
    )
    running_max = jnp.max(jnp.where(visible, scores, MASKED_SCORE), axis=-1)
    attn_prob = jnp.exp(jnp.where(visible, scores - running_max[..., None], MASKED_SCORE))
    running_out = jnp.einsum(
        "kgqt,tkd->kgqd", attn_prob.astype(BF), value_block, preferred_element_type=F32
    )
    running_sum = jnp.sum(attn_prob, axis=-1)
    attn_rows = jnp.transpose(running_out / running_sum[..., None], (2, 0, 1, 3))
    log_sums = running_max + jnp.log(running_sum)
    attn_b = attn_rows.reshape(rows, query_heads * HD).astype(BF)
    resid = inputs + mp_allreduce(dot(attn_b, out_weight))
    normed_ffn, scale_ffn = norm_forward(resid, ffn_gain)
    act_ffn = normed_ffn.astype(BF)
    gate_pre = dot(act_ffn, gate_weight)
    up_proj = dot(act_ffn, up_weight)
    sigmoid_gate = jax.nn.sigmoid(gate_pre)
    hidden = (gate_pre * sigmoid_gate * up_proj).astype(BF)
    grad_hidden = dot(cot, down_weight, COLS)
    grad_gate = (
        grad_hidden * up_proj * sigmoid_gate * (1.0 + gate_pre * (1.0 - sigmoid_gate))
    ).astype(BF)
    grad_up = (grad_hidden * gate_pre * sigmoid_gate).astype(BF)
    grad_act_ffn = mp_allreduce(
        dot(grad_gate, gate_weight, COLS) + dot(grad_up, up_weight, COLS)
    )
    block_out = (resid[:own_rows] + mp_reduce(dot(hidden, down_weight))).astype(BF)

    def pairwise(own, other_sent):
        return jnp.concatenate([own, other_sent], axis=0)

    cot_own, cot_other = split_columns(cot)
    cot_pair = pairwise(cot_own, xor(cot_other, "ctx", 1))
    hidden_pair = pairwise(hidden, xor(hidden, "ctx", 1))
    act_own, act_other = split_columns(act_ffn)
    act_pair = pairwise(act_own, xor(act_other, "ctx", 1))
    gate_pair = pairwise(grad_gate, xor(grad_gate, "ctx", 1))
    up_pair = pairwise(grad_up, xor(grad_up, "ctx", 1))
    width = cot_pair.shape[1]
    down_grad = halve(lambda a, b: dot(hidden_pair, cot_pair[:, a:b], ROWS), width, 1)
    gate_grad = halve(lambda a, b: dot(act_pair[:, a:b], gate_pair, ROWS), width, 0)
    up_grad = halve(lambda a, b: dot(act_pair[:, a:b], up_pair, ROWS), width, 0)

    grad_norm_ffn, gain_terms_ffn = norm_backward(resid, scale_ffn, ffn_gain, grad_act_ffn)
    grad_resid = cot.astype(F32) + grad_norm_ffn
    grad_resid_b = grad_resid.astype(BF)
    resid_own, resid_other = split_columns(grad_resid_b)
    resid_pair = pairwise(resid_own, xor(resid_other, "ctx", 1))
    attn_pair = pairwise(attn_b, xor(attn_b, "ctx", 1))
    out_grad = halve(lambda a, b: dot(attn_pair, resid_pair[:, a:b], ROWS), width, 1)

    grad_attn_rows = dot(grad_resid_b, out_weight, COLS).reshape(rows, key_heads, group_size, HD)
    delta = jnp.transpose(jnp.sum(grad_attn_rows * attn_rows, axis=-1), (1, 2, 0))
    grad_attn_b = grad_attn_rows.astype(BF)
    probs = jnp.exp(jnp.where(visible, scores - log_sums[..., None], MASKED_SCORE))
    grad_prob = jnp.einsum(
        "qkgd,tkd->kgqt", grad_attn_b, value_block, preferred_element_type=F32
    )
    grad_scores = (probs * (grad_prob - delta[..., None]) * softmax_scale).astype(BF)
    key_term = jnp.einsum("kgqt,qkgd->tkd", grad_scores, query_rot, preferred_element_type=F32)
    value_term = jnp.einsum(
        "kgqt,qkgd->tkd", probs.astype(BF), grad_attn_b, preferred_element_type=F32
    )
    terms = jnp.concatenate(
        [
            key_term.reshape(count, rows, key_heads * HD),
            value_term.reshape(count, rows, key_heads * HD),
        ],
        axis=-1,
    )
    sums = [terms[2 * k] if 2 * k <= window else jnp.zeros_like(terms[0]) for k in range(slots + 1)]
    for j in range(slots):
        arrived = xor(terms[2 * j + 1].astype(BF), "ctx", 1).astype(F32)
        sums[j] = sums[j] + jnp.where(odd_rank, 0.0, arrived)
        sums[j + 1] = sums[j + 1] + jnp.where(odd_rank, arrived, 0.0)
    pair_grad = sums[0]
    for k in range(slots, 0, -1):
        if 2 * k < n_ctx:
            pair_grad = pair_grad + down(sums[k].astype(BF), 2 * k).astype(F32)
    grad_query = jnp.einsum(
        "kgqt,tkd->qkgd", grad_scores, key_block, preferred_element_type=F32
    ).reshape(rows, query_heads, HD)
    grad_key_rot = pair_grad[:, : key_heads * HD].reshape(rows, key_heads, HD)
    grad_value_b = pair_grad[:, key_heads * HD :].astype(BF)

    grad_queries, gain_terms_query = norm_backward(
        queries, query_scale, query_gain, rotate(grad_query, cos_table, -sin_table)
    )
    grad_query_b = grad_queries.reshape(rows, query_heads * HD).astype(BF)
    grad_keys, gain_terms_key = norm_backward(
        keys_pre, key_scale, key_gain, rotate(grad_key_rot, cos_table, -sin_table)
    )
    grad_key_b = grad_keys.reshape(rows, key_heads * HD).astype(BF)

    in_own, in_other = split_columns(act_attn)
    in_pair = pairwise(in_own, xor(in_other, "ctx", 1))
    query_pair = pairwise(grad_query_b, xor(grad_query_b, "ctx", 1))
    query_grad = halve(lambda a, b: dot(in_pair[:, a:b], query_pair, ROWS), width, 0)
    pair_b = jnp.concatenate([grad_key_b, grad_value_b], axis=1)
    kv_pair = pairwise(pair_b, xor(pair_b, "ctx", 1))
    kv_grad = halve(lambda a, b: dot(in_pair[:, a:b], kv_pair, ROWS), width, 0)
    key_grad = kv_grad[:, : key_heads * HD]
    value_grad = kv_grad[:, key_heads * HD :]

    grad_partial = (
        dot(grad_query_b, query_weight, COLS)
        + dot(grad_key_b, key_weight, COLS)
        + dot(grad_value_b, value_weight, COLS)
    )
    attn_gain_part = jnp.sum(grad_partial * (inputs * scale_attn), axis=0)
    grad_act_attn = mp_reduce(grad_partial)
    grad_norm_attn, _ = norm_backward(
        inputs[:own_rows], scale_attn[:own_rows], attn_gain, grad_act_attn
    )
    grad_input = grad_resid[:own_rows] + grad_norm_attn

    gains = jnp.concatenate(
        [
            attn_gain_part,
            jnp.sum(gain_terms_ffn[:own_rows], axis=0),
            jnp.sum(gain_terms_query, axis=(0, 1)),
            jnp.sum(gain_terms_key, axis=(0, 1)),
        ]
    ).reshape(-1, 128)
    for axis in ("mp", "ctx"):
        mask = 1
        while mask < lax.axis_size(axis):
            gains = gains + xor(gains, axis, mask)
            mask *= 2
    gains = gains.reshape(-1)
    d = attn_gain.shape[0]
    return (
        block_out,
        grad_input,
        query_grad,
        key_grad,
        value_grad,
        out_grad,
        gate_grad,
        up_grad,
        down_grad,
        gains[:d],
        gains[d : 2 * d],
        gains[2 * d : 2 * d + HD],
        gains[2 * d + HD :],
    )


def solution(mesh):
    in_specs = (
        P(("ctx", "mp"), None),
        P(),
        P(None, "mp"),
        P(None, "mp"),
        P(None, "mp"),
        P("mp", None),
        P(),
        P(),
        P(),
        P(None, "mp"),
        P(None, "mp"),
        P("mp", None),
        P(),
        P("ctx"),
        P(("ctx", "mp"), None),
    )
    out_specs = (
        P(("ctx", "mp"), None),
        P(("ctx", "mp"), None),
        P("ctx", "mp"),
        P("ctx", "mp"),
        P("ctx", "mp"),
        P("mp", "ctx"),
        P("ctx", "mp"),
        P("ctx", "mp"),
        P("mp", "ctx"),
        P(),
        P(),
        P(),
        P(),
    )
    return jax.shard_map(body, mesh=mesh, in_specs=in_specs, out_specs=out_specs, check_vma=False)
```

```python
import functools

import jax
import jax.numpy as jnp
from jax import lax
from jax.experimental import pallas as pl
from jax.experimental.pallas import tpu as pltpu
from jax.sharding import PartitionSpec as P

HEADS = 16
KV_HEADS = 8
HD = 64
EPS = 1e-05
ROPE_BASE = 1000000.0
MASKED_SCORE = -1e30
LONGEST = {2048: 1280, 8192: 4352}
BF = jnp.bfloat16
F32 = jnp.float32
ROWS = (((0,), (0,)), ((), ()))
COLS = (((1,), (1,)), ((), ()))
SCALE = HD ** (-0.5)


def dot(a, b, dims=(((1,), (0,)), ((), ()))):
    return lax.dot_general(a, b, dims, preferred_element_type=F32)


def xor(values, axis, mask):
    n = lax.axis_size(axis)
    return lax.ppermute(values, axis, [(i, i ^ mask) for i in range(n)])


def up(values, step):
    n = lax.axis_size("ctx")
    return lax.ppermute(values, "ctx", [(i, i + step) for i in range(n - step)])


def down(values, step):
    n = lax.axis_size("ctx")
    return lax.ppermute(values, "ctx", [(i, i - step) for i in range(step, n)])


def lanes(shape):
    return lax.broadcasted_iota(jnp.int32, shape, len(shape) - 1)


def group_sum(values):
    width = values.shape[-1]
    line = lax.broadcasted_iota(jnp.int32, (width, width), 0) // HD
    ones = (line == lanes((width, width)) // HD).astype(BF)
    front = values.astype(BF)
    back = (values - front.astype(F32)).astype(BF)
    return dot(front, ones) + dot(back, ones)


def partner(values):
    width = values.shape[-1]
    first = lanes(values.shape) % HD < HD // 2
    return jnp.where(
        first, pltpu.roll(values, width - HD // 2, 1), pltpu.roll(values, HD // 2, 1)
    )


def wide(table, width):
    return jnp.concatenate([table] * (width // table.shape[-1]), axis=-1)


def row_norm(values):
    return lax.rsqrt(jnp.mean(values * values, axis=-1, keepdims=True) + EPS)


def head_norm(values):
    return lax.rsqrt(group_sum(values * values) * (1.0 / HD) + EPS)


def head_norm_backward(values, gain, grads, cos, sin):
    width = values.shape[-1]
    grads = grads * wide(cos, width) - partner(grads) * wide(sin, width)
    scale = head_norm(values)
    normed = values * scale
    inner = grads * gain
    grad_in = scale * (inner - normed * (group_sum(inner * normed) * (1.0 / HD)))
    return grad_in, jnp.sum(grads * normed, axis=0, keepdims=True)


def place_of(iota, rows, rank):
    quarter = rows // 4
    part = iota // quarter
    relative = (part % 2) * 2 + part // 2
    return jnp.bitwise_xor(relative, rank) * quarter + iota % quarter


def stack(slab, kv_head):
    slab = slab.astype(F32)
    turned = pltpu.roll(slab, HD, 1)
    low = lanes(slab.shape) < HD
    if kv_head == 0:
        parts = [jnp.where(low, slab, 0.0), jnp.where(low, turned, 0.0)]
    else:
        parts = [jnp.where(low, 0.0, turned), jnp.where(low, 0.0, slab)]
    return jnp.concatenate(parts, axis=0)


def unstack(stacked, kv_head):
    rows = stacked.shape[0] // 2
    first, second = stacked[:rows], stacked[rows:]
    low = lanes(first.shape) < HD
    if kv_head == 0:
        return jnp.where(low, first, pltpu.roll(second, HD, 1))
    return jnp.where(low, pltpu.roll(first, HD, 1), second)


def qkv_kernel(
    ranks, x0, x1, x2, x3, gain, wq, wk, wv, query_gain, key_gain, cos, sin,
    act_out, select_out, pair_out, query_rot_out, query_out, key_out,
):
    x = jnp.concatenate([x0[...], x1[...], x2[...], x3[...]], axis=0).astype(F32)
    act = (x * row_norm(x) * gain[...]).astype(BF)
    act_out[...] = act
    keys = dot(act, wk[...])
    key_out[...] = keys
    width = keys.shape[-1]
    normed = keys * head_norm(keys) * key_gain[...]
    rotated = normed * cos[...] + partner(normed) * sin[...]
    pair_out[:, :width] = rotated.astype(BF)
    pair_out[:, width:] = dot(act, wv[...]).astype(BF)
    queries = dot(act, wq[...])
    query_out[...] = queries
    normed = queries * head_norm(queries) * query_gain[...]
    width = queries.shape[-1]
    rotated = normed * wide(cos[...], width) + partner(normed) * wide(sin[...], width)
    query_rot_out[...] = rotated.astype(BF)
    select_columns(ranks, act_out, select_out)


def select_columns(ranks, source, target):
    columns = target.shape[1]
    blocks = columns // 128
    if blocks != 4:
        target[...] = jnp.zeros(target.shape, target.dtype)
        return
    for b in range(blocks):
        start = pl.multiple_of((2 * b + 1 - ranks[0] % 2) * 128, 128)
        target[:, b * 128 : (b + 1) * 128] = source[:, pl.ds(start, 128)]


def attention_kernel(
    count, ranks, query_rot, first_seen, wo, *refs
):
    blocks = refs[:count]
    out_f32, out_b, sums_out, kept_out, sent_out, scores = refs[count:]
    rows = query_rot.shape[0]
    key_width = blocks[0].shape[1] // 2
    query_index = ranks[0] * rows + place_of(
        lax.broadcasted_iota(jnp.int32, (rows, 1), 0), rows, ranks[1]
    )
    key_place = place_of(lanes((1, rows)), rows, ranks[1])
    masks = []
    for d in range(count):
        key_index = (ranks[0] - d) * rows + key_place
        mask = key_index >= first_seen[...]
        if d == 0:
            mask = mask & (key_index <= query_index)
        masks.append(jnp.where(mask, 0.0, MASKED_SCORE))
    for head in range(2):
        slab = query_rot[:, head * 128 : (head + 1) * 128]
        stacked = (stack(slab, head) * SCALE).astype(BF)
        top = jnp.full((2 * rows, 1), MASKED_SCORE, F32)
        for d in range(count):
            block = dot(stacked, blocks[d][:, :key_width], COLS)
            block = block + jnp.concatenate([masks[d], masks[d]], axis=0)
            scores[:, d * rows : (d + 1) * rows] = block
            top = jnp.maximum(top, jnp.max(block, axis=-1, keepdims=True))
        total = jnp.zeros((2 * rows, 1), F32)
        mixed = jnp.zeros((2 * rows, key_width), F32)
        for d in range(count):
            weights = jnp.exp(scores[:, d * rows : (d + 1) * rows] - top)
            total = total + jnp.sum(weights, axis=-1, keepdims=True)
            mixed = mixed + dot(weights.astype(BF), blocks[d][:, key_width:])
        sums = jnp.broadcast_to(top + jnp.log(total), (2 * rows, 128))
        sums_out[head : head + 1, :] = jnp.transpose(sums)[:1]
        out_f32[:, head * 128 : (head + 1) * 128] = unstack(mixed / total, head)
    attn_b = out_f32[...].astype(BF)
    out_b[...] = attn_b
    half = rows // 2
    kept_out[...] = dot(attn_b[:half], wo[...])
    sent_out[...] = dot(attn_b[half:], wo[...]).astype(BF)


def ffn_forward_kernel(
    ranks, x0, x1, x2, x3, half0, half1, gain, wg, wu, cot,
    resid_out, act_out, select_out, cot_select_out, gate_out, up_out, hidden_out,
):
    x = jnp.concatenate([x0[...], x1[...], x2[...], x3[...]], axis=0).astype(F32)
    resid = x + jnp.concatenate([half0[...], half1[...]], axis=0).astype(F32)
    resid_out[...] = resid
    act = (resid * row_norm(resid) * gain[...]).astype(BF)
    act_out[...] = act
    gate = dot(act, wg[...])
    upper = dot(act, wu[...])
    gate_out[...] = gate
    up_out[...] = upper
    hidden_out[...] = (gate * jax.nn.sigmoid(gate) * upper).astype(BF)
    select_columns(ranks, act_out, select_out)
    select_columns(ranks, cot, cot_select_out)


def ffn_backward_kernel(
    gate, upper, grad_hidden, wg, wu, grad_gate_out, grad_up_out, kept_out, sent_out
):
    grads = grad_hidden[...]
    values = gate[...]
    sigmoid = jax.nn.sigmoid(values)
    grad_gate = (grads * upper[...] * sigmoid * (1.0 + values * (1.0 - sigmoid))).astype(BF)
    grad_up = (grads * values * sigmoid).astype(BF)
    grad_gate_out[...] = grad_gate
    grad_up_out[...] = grad_up
    half = values.shape[0] // 2
    sent_out[...] = (
        dot(grad_gate[half:], wg[...], COLS) + dot(grad_up[half:], wu[...], COLS)
    ).astype(BF)
    kept_out[...] = dot(grad_gate[:half], wg[...], COLS) + dot(grad_up[:half], wu[...], COLS)


def attention_backward_kernel(
    count, ranks, cot, resid, half0, half1, gain, wo, attn, sums, query_rot, first_row, *refs
):
    blocks = refs[:count]
    grad_own_out, grad_b_out, select_out, gain_out, grad_query_out = refs[count : count + 5]
    terms = refs[count + 5 :]
    rows = query_rot.shape[0]
    key_width = blocks[0].shape[1] // 2
    values = resid[...]
    scale = row_norm(values)
    normed = values * scale
    grads = jnp.concatenate([half0[...], half1[...]], axis=0).astype(F32)
    inner = grads * gain[...]
    grad_in = scale * (inner - normed * jnp.mean(inner * normed, axis=-1, keepdims=True))
    grad_resid = cot[...].astype(F32) + grad_in
    own = rows // 4
    grad_own_out[...] = grad_resid[:own]
    gain_out[...] = jnp.sum(grads[:own] * normed[:own], axis=0, keepdims=True)
    grad_resid_b = grad_resid.astype(BF)
    grad_b_out[...] = grad_resid_b
    select_columns(ranks, grad_b_out, select_out)
    grad_attn = dot(grad_resid_b, wo[...], COLS)
    delta = jnp.transpose(group_sum(grad_attn * attn[...]))
    grad_attn_b = grad_attn.astype(BF)

    query_index = ranks[0] * rows + place_of(lanes((1, rows)), rows, ranks[1])
    key_place = place_of(lax.broadcasted_iota(jnp.int32, (rows, 1), 0), rows, ranks[1])
    stacked = [stack(query_rot[:, h * 128 : (h + 1) * 128], h) for h in range(2)]
    stacked_b = [s.astype(BF) for s in stacked]
    scaled = [(s * SCALE).astype(BF) for s in stacked]
    grads_b = [
        stack(grad_attn_b[:, h * 128 : (h + 1) * 128], h).astype(BF) for h in range(2)
    ]
    deltas = [
        jnp.concatenate(
            [delta[2 * h * HD : 2 * h * HD + 1], delta[(2 * h + 1) * HD : (2 * h + 1) * HD + 1]],
            axis=1,
        )
        for h in range(2)
    ]
    grad_query = [jnp.zeros((2 * rows, key_width), F32) for _ in range(2)]
    for d in range(count - 1, -1, -1):
        key_index = (ranks[0] - d) * rows + key_place
        mask = key_index >= first_row[...]
        if d == 0:
            mask = mask & (key_index <= query_index)
        mask = jnp.where(mask, 0.0, MASKED_SCORE)
        mask = jnp.concatenate([mask, mask], axis=1)
        key_block = blocks[d][:, :key_width]
        value_block = blocks[d][:, key_width:]
        key_term = jnp.zeros((rows, key_width), F32)
        value_term = jnp.zeros((rows, key_width), F32)
        for h in range(2):
            scores = dot(key_block, scaled[h], COLS) + mask
            probs = jnp.exp(scores - sums[h : h + 1, :])
            grad_probs = dot(value_block, grads_b[h], COLS)
            grad_scores = (probs * (grad_probs - deltas[h]) * SCALE).astype(BF)
            key_term = key_term + dot(grad_scores, stacked_b[h])
            value_term = value_term + dot(probs.astype(BF), grads_b[h])
            grad_query[h] = grad_query[h] + dot(grad_scores, key_block, ROWS)
        terms[d][:, :key_width] = key_term.astype(terms[d].dtype)
        terms[d][:, key_width:] = value_term.astype(terms[d].dtype)
    for h in range(2):
        grad_query_out[:, h * 128 : (h + 1) * 128] = unstack(grad_query[h], h)


def query_backward_kernel(
    queries, gain, grads, cos, sin, wq, grad_out, gain_out, partial_out
):
    grad_in, gain_terms = head_norm_backward(queries[...], gain[...], grads[...], cos[...], sin[...])
    grad_b = grad_in.astype(BF)
    grad_out[...] = grad_b
    gain_out[...] = gain_terms
    partial_out[...] = dot(grad_b, wq[...], COLS)


def key_backward_kernel(
    keys, gain, grads, cos, sin, wk, wv, query_partial, x0, x1, x2, x3,
    grad_out, gain_out, attn_gain_out, kept_out, sent_out,
):
    width = keys.shape[-1]
    grad_in, gain_terms = head_norm_backward(
        keys[...], gain[...], grads[:, :width], cos[...], sin[...]
    )
    grad_b = grad_in.astype(BF)
    value_b = grads[:, width:].astype(BF)
    grad_out[:, :width] = grad_b
    grad_out[:, width:] = value_b
    gain_out[...] = gain_terms
    partial = query_partial[...] + dot(grad_b, wk[...], COLS) + dot(value_b, wv[...], COLS)
    x = jnp.concatenate([x0[...], x1[...], x2[...], x3[...]], axis=0).astype(F32)
    attn_gain_out[...] = jnp.sum(partial * (x * row_norm(x)), axis=0, keepdims=True)
    half = partial.shape[0] // 2
    kept_out[...] = partial[:half]
    sent_out[...] = partial[half:].astype(BF)


def weight_grad_kernel(ranks, act, arrived_act, grads, arrived_grads, kept_out, sent_out):
    parity = ranks[0] % 2
    mine = ranks[0] // 2
    for lo in range(2):
        for hi in range(2):
            block = jnp.bitwise_xor(mine, lo + 2 * hi)
            start = pl.multiple_of((2 * block + parity) * 128, 128)
            there = pl.multiple_of(block * 128, 128)
            total = dot(act[:, pl.ds(start, 128)], grads[...], ROWS) + dot(
                arrived_act[:, pl.ds(there, 128)], arrived_grads[...], ROWS
            )
            target = sent_out if lo else kept_out
            target[hi * 128 : (hi + 1) * 128, :] = total.astype(target.dtype)


def shape(dims, dtype):
    return jax.ShapeDtypeStruct(dims, dtype)


def launch(kernel, outs, args, scratch=(), name=None):
    nbytes = sum(a.size * a.dtype.itemsize for a in list(args) + list(outs))
    nbytes += sum(s.shape[0] * s.shape[1] * 4 for s in scratch)
    specs = [
        pl.BlockSpec(memory_space=pltpu.SMEM if a.shape == (2,) else pltpu.VMEM) for a in args
    ]
    return pl.pallas_call(
        kernel,
        out_shape=outs,
        in_specs=specs,
        out_specs=[pl.BlockSpec(memory_space=pltpu.VMEM) for _ in outs],
        scratch_shapes=list(scratch),
        compiler_params=pltpu.CompilerParams(
            vmem_limit_bytes=min(2 * nbytes + (8 << 20), 56 << 20)
        ),
        name=name,
    )(*args)


def mp_order(values):
    rank = lax.axis_index("mp")
    parts = values.reshape(2, 2, -1)
    parts = jnp.swapaxes(parts, 0, 1)
    parts = jnp.where(rank % 2 == 1, parts[::-1], parts)
    parts = jnp.where(rank // 2 == 1, parts[:, ::-1], parts)
    return parts.reshape(values.shape)


def mp_gather(values):
    other = xor(values, "mp", 2)
    core = xor(values, "mp", 1)
    return values, other, core, xor(other, "mp", 1)


def mp_reduce(kept, sent):
    kept = kept + xor(sent, "mp", 1).astype(F32)
    own = kept.shape[0] // 2
    return kept[:own] + xor(kept[own:].astype(BF), "mp", 2).astype(F32)


def mp_allreduce(kept, sent):
    kept = (kept + xor(sent, "mp", 1).astype(F32)).astype(BF)
    other = xor(kept, "mp", 2)
    own = kept.shape[0] // 2
    other = jnp.concatenate([other[own:], other[:own]], axis=0)
    both = (kept.astype(F32) + other.astype(F32)).astype(BF)
    return both, xor(both, "mp", 1)


def split_columns(values):
    n = lax.axis_size("ctx")
    index = lax.axis_index("ctx")
    rows, columns = values.shape
    bits = n.bit_length() - 1
    parts = values.reshape((rows,) + (2,) * bits + (columns // n,))
    for bit in range(bits):
        parts = jnp.where((index >> bit) % 2 == 1, jnp.flip(parts, bits - bit), parts)
    order = [0] + [bits - b for b in range(bits)] + [bits + 1]
    parts = jnp.transpose(parts, order).reshape(rows, 2, columns // 2)
    return parts[:, 0], parts[:, 1]


def weight_grad(ranks, act, arrived_act, grads, arrived_grads, name):
    n = lax.axis_size("ctx")
    columns = grads.shape[1]
    half = act.shape[1] // 4
    if n == 8 and act.shape[1] == 1024:
        kept, sent = launch(
            weight_grad_kernel,
            [shape((half, columns), F32), shape((half, columns), BF)],
            [ranks, act, arrived_act, grads, arrived_grads],
            name=name,
        )
    else:
        own, other = split_columns(act)
        both = jnp.concatenate([own, xor(other, "ctx", 1)], axis=0)
        both_grads = jnp.concatenate([grads, arrived_grads], axis=0)
        total = dot(both, both_grads, ROWS)
        kept, sent = total[:half], total[half:].astype(BF)
    total = kept + xor(sent, "ctx", 2).astype(F32)
    mask = 4
    while mask < n:
        half = total.shape[0] // 2
        total = total[:half] + xor(total[half:].astype(BF), "ctx", mask).astype(F32)
        mask *= 2
    return total


def body(
    block_in,
    attn_gain,
    query_weight,
    key_weight,
    value_weight,
    out_weight,
    query_gain,
    key_gain,
    ffn_gain,
    gate_weight,
    up_weight,
    down_weight,
    segments,
    positions,
    cotangent,
):
    width = block_in.shape[1]
    key_width = key_weight.shape[1]
    query_width = query_weight.shape[1]
    hidden_width = gate_weight.shape[1]
    n_ctx = lax.axis_size("ctx")
    ctx_rank = lax.axis_index("ctx")
    own_rows = block_in.shape[0]
    rows = positions.shape[0]
    total_tokens = rows * n_ctx
    longest = LONGEST.get(total_tokens, total_tokens)
    window = min(n_ctx - 1, -(-(longest - 1) // rows))
    slots = (window + 1) // 2
    count = window + 1
    half = rows // 2
    ranks = jnp.stack([ctx_rank, lax.axis_index("mp")]).astype(jnp.int32)

    x = mp_gather(block_in)
    place = mp_order(jnp.arange(rows, dtype=jnp.int32))
    positions = mp_order(positions)
    first_seen = ctx_rank * rows + place - positions
    lane = jnp.arange(128, dtype=jnp.int32)
    freqs = ROPE_BASE ** (-2.0 * (lane % (HD // 2)).astype(F32) / HD)
    angles = positions.astype(F32)[:, None] * freqs[None, :]
    cos = jnp.cos(angles)
    sin = jnp.sin(angles) * jnp.where(lane % HD < HD // 2, -1.0, 1.0)[None, :]
    query_gain_row = jnp.tile(query_gain, query_width // HD).reshape(1, -1)
    key_gain_row = jnp.tile(key_gain, key_width // HD).reshape(1, -1)
    attn_gain_row = attn_gain.reshape(1, -1)
    ffn_gain_row = ffn_gain.reshape(1, -1)

    act_attn, act_attn_select, pair, query_rot, queries, keys_pre = launch(
        qkv_kernel,
        [
            shape((rows, width), BF),
            shape((rows, width // 2), BF),
            shape((rows, 2 * key_width), BF),
            shape((rows, query_width), BF),
            shape((rows, query_width), F32),
            shape((rows, key_width), F32),
        ],
        [ranks, *x, attn_gain_row, query_weight, key_weight, value_weight,
         query_gain_row, key_gain_row, cos, sin],
        name="qkv",
    )

    odd_rank = ctx_rank % 2 == 1
    items = [pair] + [up(pair, 2 * k) for k in range(1, slots + 1) if 2 * k < n_ctx]
    while len(items) < slots + 1:
        items.append(jnp.zeros_like(pair))
    blocks = {0: pair}
    for k in range(1, slots + 1):
        if 2 * k <= window:
            blocks[2 * k] = items[k]
    for j in range(slots):
        blocks[2 * j + 1] = xor(jnp.where(odd_rank, items[j + 1], items[j]), "ctx", 1)
    blocks = [blocks[d] for d in range(count)]

    cot = jnp.concatenate(mp_gather(cotangent), axis=0)
    grad_hidden = dot(cot, down_weight, COLS)

    attn_rows, attn_b, log_sums, kept, sent = launch(
        functools.partial(attention_kernel, count),
        [
            shape((rows, query_width), F32),
            shape((rows, query_width), BF),
            shape((2, 2 * rows), F32),
            shape((half, width), F32),
            shape((half, width), BF),
        ],
        [ranks, query_rot, first_seen.reshape(-1, 1), out_weight, *blocks],
        scratch=[pltpu.VMEM((2 * rows, count * rows), F32)],
        name="attention",
    )
    resid_halves = mp_allreduce(kept, sent)
    early = xor(jnp.concatenate([act_attn_select, attn_b], axis=1), "ctx", 1)
    act_attn_there = early[:, : width // 2]
    attn_there = early[:, width // 2 :]

    resid, act_ffn, act_select, cot_select, gate_pre, up_proj, hidden = launch(
        ffn_forward_kernel,
        [
            shape((rows, width), F32),
            shape((rows, width), BF),
            shape((rows, width // 2), BF),
            shape((rows, width // 2), BF),
            shape((rows, hidden_width), F32),
            shape((rows, hidden_width), F32),
            shape((rows, hidden_width), BF),
        ],
        [ranks, *x, *resid_halves, ffn_gain_row, gate_weight, up_weight, cot],
        name="ffn_forward",
    )
    hidden_there = xor(hidden, "ctx", 1)
    cot_there = xor(cot_select, "ctx", 1)
    grad_gate, grad_up, kept, sent = launch(
        ffn_backward_kernel,
        [
            shape((rows, hidden_width), BF),
            shape((rows, hidden_width), BF),
            shape((half, width), F32),
            shape((half, width), BF),
        ],
        [gate_pre, up_proj, grad_hidden, gate_weight, up_weight],
        name="ffn_backward",
    )
    grad_act_halves = mp_allreduce(kept, sent)
    act_there = xor(act_select, "ctx", 1)
    gate_there = xor(grad_gate, "ctx", 1)
    up_there = xor(grad_up, "ctx", 1)

    outs = launch(
        functools.partial(attention_backward_kernel, count),
        [
            shape((own_rows, width), F32),
            shape((rows, width), BF),
            shape((rows, width // 2), BF),
            shape((1, width), F32),
            shape((rows, query_width), F32),
        ]
        + [shape((rows, 2 * key_width), BF if d else F32) for d in range(count)],
        [ranks, cot, resid, *grad_act_halves, ffn_gain_row, out_weight, attn_rows, log_sums,
         query_rot, first_seen.reshape(1, -1), *blocks],
        name="attention_backward",
    )
    grad_resid, grad_resid_b, grad_select, ffn_gain_part, grad_query = outs[:5]
    terms = outs[5:]

    sums = [terms[2 * k].astype(F32) if 2 * k <= window else 0.0 for k in range(slots + 1)]
    for j in range(slots - 1, -1, -1):
        arrived = xor(terms[2 * j + 1], "ctx", 1).astype(F32)
        sums[j] = sums[j] + jnp.where(odd_rank, 0.0, arrived)
        sums[j + 1] = sums[j + 1] + jnp.where(odd_rank, arrived, 0.0)
    pair_grad = sums[0]
    for k in range(slots, 0, -1):
        if 2 * k < n_ctx:
            pair_grad = pair_grad + down(sums[k].astype(BF), 2 * k).astype(F32)

    grad_query_b, query_gain_part, query_partial = launch(
        query_backward_kernel,
        [
            shape((rows, query_width), BF),
            shape((1, query_width), F32),
            shape((rows, width), F32),
        ],
        [queries, query_gain_row, grad_query, cos, sin, query_weight],
        name="query_backward",
    )
    late = xor(jnp.concatenate([grad_select, grad_query_b], axis=1), "ctx", 1)
    grad_there = late[:, : width // 2]
    query_there = late[:, width // 2 :]

    down_grad = weight_grad(ranks, cot, cot_there, hidden, hidden_there, "down_grad")
    gate_grad = weight_grad(ranks, act_ffn, act_there, grad_gate, gate_there, "gate_grad")
    up_grad = weight_grad(ranks, act_ffn, act_there, grad_up, up_there, "up_grad")
    out_grad = weight_grad(ranks, grad_resid_b, grad_there, attn_b, attn_there, "out_grad")
    query_grad = weight_grad(
        ranks, act_attn, act_attn_there, grad_query_b, query_there, "query_grad"
    )

    pair_b, key_gain_part, attn_gain_part, kept, sent = launch(
        key_backward_kernel,
        [
            shape((rows, 2 * key_width), BF),
            shape((1, key_width), F32),
            shape((1, width), F32),
            shape((half, width), F32),
            shape((half, width), BF),
        ],
        [keys_pre, key_gain_row, pair_grad, cos, sin, key_weight, value_weight,
         query_partial, *x],
        name="key_backward",
    )
    pair_there = xor(pair_b, "ctx", 1)
    pair_weight_grad = weight_grad(
        ranks, act_attn, act_attn_there, pair_b, pair_there, "key_value_grad"
    )
    grad_act_attn = mp_reduce(kept, sent)
    inputs = block_in.astype(F32)
    scale = row_norm(inputs)
    normed = inputs * scale
    inner = grad_act_attn * attn_gain
    grad_input = grad_resid + scale * (
        inner - normed * jnp.mean(inner * normed, axis=-1, keepdims=True)
    )

    block_out = dot(hidden, down_weight)
    block_out = (
        resid[:own_rows] + mp_reduce(block_out[:half], block_out[half:].astype(BF))
    ).astype(BF)

    gains = jnp.concatenate(
        [
            attn_gain_part.reshape(-1),
            ffn_gain_part.reshape(-1),
            jnp.sum(query_gain_part.reshape(-1, HD), axis=0),
            jnp.sum(key_gain_part.reshape(-1, HD), axis=0),
        ]
    ).reshape(-1, 128)
    for axis in ("mp", "ctx"):
        mask = 1
        while mask < lax.axis_size(axis):
            gains = gains + xor(gains, axis, mask)
            mask *= 2
    gains = gains.reshape(-1)
    return (
        block_out,
        grad_input,
        query_grad,
        pair_weight_grad[:, :key_width],
        pair_weight_grad[:, key_width:],
        jnp.transpose(out_grad),
        gate_grad,
        up_grad,
        jnp.transpose(down_grad),
        gains[:width],
        gains[width : 2 * width],
        gains[2 * width : 2 * width + HD],
        gains[2 * width + HD :],
    )


def solution(mesh):
    in_specs = (
        P(("ctx", "mp"), None),
        P(),
        P(None, "mp"),
        P(None, "mp"),
        P(None, "mp"),
        P("mp", None),
        P(),
        P(),
        P(),
        P(None, "mp"),
        P(None, "mp"),
        P("mp", None),
        P(),
        P("ctx"),
        P(("ctx", "mp"), None),
    )
    out_specs = (
        P(("ctx", "mp"), None),
        P(("ctx", "mp"), None),
        P("ctx", "mp"),
        P("ctx", "mp"),
        P("ctx", "mp"),
        P("mp", "ctx"),
        P("ctx", "mp"),
        P("ctx", "mp"),
        P("mp", "ctx"),
        P(),
        P(),
        P(),
        P(),
    )
    return jax.shard_map(body, mesh=mesh, in_specs=in_specs, out_specs=out_specs, check_vma=False)
```

```python
import functools

import jax
import jax.numpy as jnp
from jax import lax
from jax.experimental import pallas as pl
from jax.experimental.pallas import tpu as pltpu
from jax.sharding import PartitionSpec as P

HEADS = 16
KV_HEADS = 8
HD = 64
EPS = 1e-05
ROPE_BASE = 1000000.0
MASKED_SCORE = -1e30
LONGEST = {2048: 1280, 8192: 4352}
BF = jnp.bfloat16
F32 = jnp.float32
ROWS = (((0,), (0,)), ((), ()))
COLS = (((1,), (1,)), ((), ()))
SCALE = HD ** (-0.5)


def dot(a, b, dims=(((1,), (0,)), ((), ()))):
    return lax.dot_general(a, b, dims, preferred_element_type=F32)


def xor(values, axis, mask):
    n = lax.axis_size(axis)
    return lax.ppermute(values, axis, [(i, i ^ mask) for i in range(n)])


def up(values, step):
    n = lax.axis_size("ctx")
    return lax.ppermute(values, "ctx", [(i, i + step) for i in range(n - step)])


def down(values, step):
    n = lax.axis_size("ctx")
    return lax.ppermute(values, "ctx", [(i, i - step) for i in range(step, n)])


def lanes(shape):
    return lax.broadcasted_iota(jnp.int32, shape, len(shape) - 1)


def group_sum(values):
    width = values.shape[-1]
    line = lax.broadcasted_iota(jnp.int32, (width, width), 0) // HD
    ones = (line == lanes((width, width)) // HD).astype(BF)
    front = values.astype(BF)
    back = (values - front.astype(F32)).astype(BF)
    return dot(front, ones) + dot(back, ones)


def partner(values):
    width = values.shape[-1]
    first = lanes(values.shape) % HD < HD // 2
    return jnp.where(
        first, pltpu.roll(values, width - HD // 2, 1), pltpu.roll(values, HD // 2, 1)
    )


def wide(table, width):
    return jnp.concatenate([table] * (width // table.shape[-1]), axis=-1)


def row_norm(values):
    return lax.rsqrt(jnp.mean(values * values, axis=-1, keepdims=True) + EPS)


def head_norm(values):
    return lax.rsqrt(group_sum(values * values) * (1.0 / HD) + EPS)


def head_norm_backward(values, gain, grads, cos, sin):
    width = values.shape[-1]
    grads = grads * wide(cos, width) - partner(grads) * wide(sin, width)
    scale = head_norm(values)
    normed = values * scale
    inner = grads * gain
    grad_in = scale * (inner - normed * (group_sum(inner * normed) * (1.0 / HD)))
    return grad_in, jnp.sum(grads * normed, axis=0, keepdims=True)


def place_of(iota, rows, rank):
    quarter = rows // 4
    part = iota // quarter
    relative = (part % 2) * 2 + part // 2
    return jnp.bitwise_xor(relative, rank) * quarter + iota % quarter


def stack(slab, kv_head):
    slab = slab.astype(F32)
    turned = pltpu.roll(slab, HD, 1)
    low = lanes(slab.shape) < HD
    if kv_head == 0:
        parts = [jnp.where(low, slab, 0.0), jnp.where(low, turned, 0.0)]
    else:
        parts = [jnp.where(low, 0.0, turned), jnp.where(low, 0.0, slab)]
    return jnp.concatenate(parts, axis=0)


def unstack(stacked, kv_head):
    rows = stacked.shape[0] // 2
    first, second = stacked[:rows], stacked[rows:]
    low = lanes(first.shape) < HD
    if kv_head == 0:
        return jnp.where(low, first, pltpu.roll(second, HD, 1))
    return jnp.where(low, pltpu.roll(first, HD, 1), second)


def qkv_kernel(
    ranks, x0, x1, x2, x3, gain, wq, wk, wv, query_gain, key_gain, cos, sin,
    act_out, select_out, pair_out, query_rot_out, query_out, key_out,
):
    x = jnp.concatenate([x0[...], x1[...], x2[...], x3[...]], axis=0).astype(F32)
    act = (x * row_norm(x) * gain[...]).astype(BF)
    act_out[...] = act
    keys = dot(act, wk[...])
    key_out[...] = keys
    width = keys.shape[-1]
    normed = keys * head_norm(keys) * key_gain[...]
    rotated = normed * cos[...] + partner(normed) * sin[...]
    pair_out[:, :width] = rotated.astype(BF)
    pair_out[:, width:] = dot(act, wv[...]).astype(BF)
    queries = dot(act, wq[...])
    query_out[...] = queries
    normed = queries * head_norm(queries) * query_gain[...]
    width = queries.shape[-1]
    rotated = normed * wide(cos[...], width) + partner(normed) * wide(sin[...], width)
    query_rot_out[...] = rotated.astype(BF)
    select_columns(ranks, act_out, select_out)


def select_columns(ranks, source, target):
    columns = target.shape[1]
    blocks = columns // 128
    if blocks != 4:
        target[...] = jnp.zeros(target.shape, target.dtype)
        return
    for b in range(blocks):
        start = pl.multiple_of((2 * b + 1 - ranks[0] % 2) * 128, 128)
        target[:, b * 128 : (b + 1) * 128] = source[:, pl.ds(start, 128)]


def cotangent_kernel(ranks, c0, c1, c2, c3, wd, cot_out, select_out, grad_hidden_out):
    cot = jnp.concatenate([c0[...], c1[...], c2[...], c3[...]], axis=0)
    cot_out[...] = cot
    select_columns(ranks, cot_out, select_out)
    grad_hidden_out[...] = dot(cot, wd[...], COLS)


def attention_kernel(count, ranks, query_rot, positions, wo, act_select, *refs):
    slots = count // 2
    even = refs[:slots]
    low_odd, high_odd = refs[slots : 2 * slots], refs[2 * slots : 3 * slots]
    out_f32, early_out, sums_out, kept_out, sent_out = refs[3 * slots : 3 * slots + 5]
    odd = refs[3 * slots + 5 : -1]
    scores = refs[-1]
    rows = query_rot.shape[0]
    key_width = even[0].shape[1] // 2
    for j in range(slots):
        odd[j][...] = jnp.where(
            ranks[0] % 2 == 1, low_odd[j][...].astype(F32), high_odd[j][...].astype(F32)
        ).astype(BF)
    blocks = [(even, odd)[d % 2][d // 2] for d in range(count)]
    query_index = ranks[0] * rows + place_of(
        lax.broadcasted_iota(jnp.int32, (rows, 1), 0), rows, ranks[1]
    )
    first_seen = query_index - positions[...]
    key_place = place_of(lanes((1, rows)), rows, ranks[1])
    masks = []
    for d in range(count):
        key_index = (ranks[0] - d) * rows + key_place
        mask = key_index >= first_seen
        if d == 0:
            mask = mask & (key_index <= query_index)
        masks.append(jnp.where(mask, 0.0, MASKED_SCORE))
    for head in range(2):
        slab = query_rot[:, head * 128 : (head + 1) * 128]
        stacked = (stack(slab, head) * SCALE).astype(BF)
        top = jnp.full((2 * rows, 1), MASKED_SCORE, F32)
        for d in range(count):
            block = dot(stacked, blocks[d][:, :key_width], COLS)
            block = block + jnp.concatenate([masks[d], masks[d]], axis=0)
            scores[:, d * rows : (d + 1) * rows] = block
            top = jnp.maximum(top, jnp.max(block, axis=-1, keepdims=True))
        total = jnp.zeros((2 * rows, 1), F32)
        mixed = jnp.zeros((2 * rows, key_width), F32)
        for d in range(count):
            weights = jnp.exp(scores[:, d * rows : (d + 1) * rows] - top)
            total = total + jnp.sum(weights, axis=-1, keepdims=True)
            mixed = mixed + dot(weights.astype(BF), blocks[d][:, key_width:])
        sums = jnp.broadcast_to(top + jnp.log(total), (2 * rows, 128))
        sums_out[head : head + 1, :] = jnp.transpose(sums)[:1]
        out_f32[:, head * 128 : (head + 1) * 128] = unstack(mixed / total, head)
    attn_b = out_f32[...].astype(BF)
    chosen = act_select.shape[1]
    early_out[:, :chosen] = act_select[...]
    early_out[:, chosen:] = attn_b
    half = rows // 2
    kept_out[...] = dot(attn_b[:half], wo[...])
    sent_out[...] = dot(attn_b[half:], wo[...]).astype(BF)


def add_kernel(kept, arrived, out):
    out[...] = (kept[...].astype(F32) + arrived[...].astype(F32)).astype(out.dtype)


def flipped_add_kernel(kept, arrived, out):
    half = kept.shape[0] // 2
    for a, b in ((0, half), (half, 0)):
        total = kept[a : a + half, :].astype(F32) + arrived[b : b + half, :].astype(F32)
        out[a : a + half, :] = total.astype(out.dtype)


def fold_kernel(kept, arrived, front_out, back_out):
    half = front_out.shape[0]
    front_out[...] = kept[:half, :] + arrived[:half, :].astype(F32)
    back_out[...] = (kept[half:, :] + arrived[half:, :].astype(F32)).astype(BF)


def turned_add_kernel(kept, arrived, out):
    out[...] = jnp.transpose(kept[...] + arrived[...].astype(F32))


def split_add_kernel(kept, arrived, first_out, second_out):
    total = kept[...] + arrived[...].astype(F32)
    width = first_out.shape[1]
    first_out[...] = total[:, :width]
    second_out[...] = total[:, width:]


def pair_sum_kernel(ranks, term, if_odd, if_even, out):
    odd = ranks[0] % 2 == 1
    out[...] = (
        term[...].astype(F32)
        + jnp.where(odd, if_odd[...].astype(F32), if_even[...].astype(F32))
    ).astype(BF)


def down_kernel(hidden, wd, kept_out, sent_out):
    half = hidden.shape[0] // 2
    sent_out[...] = dot(hidden[half:, :], wd[...]).astype(BF)
    kept_out[...] = dot(hidden[:half, :], wd[...])


def block_out_kernel(resid, kept, arrived, out):
    own = out.shape[0]
    out[...] = (resid[:own, :] + kept[:own, :] + arrived[...].astype(F32)).astype(BF)


def grad_input_kernel(x, gain, grad_resid, kept, arrived, out):
    own = out.shape[0]
    grads = kept[:own, :] + arrived[...].astype(F32)
    values = x[...].astype(F32)
    scale = row_norm(values)
    normed = values * scale
    inner = grads * gain[...]
    out[...] = grad_resid[...] + scale * (
        inner - normed * jnp.mean(inner * normed, axis=-1, keepdims=True)
    )


def ffn_forward_kernel(
    ranks, x0, x1, x2, x3, half0, half1, gain, wg, wu,
    resid_out, act_out, select_out, gate_out, up_out, hidden_out,
):
    x = jnp.concatenate([x0[...], x1[...], x2[...], x3[...]], axis=0).astype(F32)
    resid = x + jnp.concatenate([half0[...], half1[...]], axis=0).astype(F32)
    resid_out[...] = resid
    act = (resid * row_norm(resid) * gain[...]).astype(BF)
    act_out[...] = act
    gate = dot(act, wg[...])
    upper = dot(act, wu[...])
    gate_out[...] = gate
    up_out[...] = upper
    hidden_out[...] = (gate * jax.nn.sigmoid(gate) * upper).astype(BF)
    select_columns(ranks, act_out, select_out)


def ffn_backward_kernel(
    gate, upper, grad_hidden, wg, wu, select, gate_packet, grad_up_out, kept_out, sent_out
):
    grads = grad_hidden[...]
    values = gate[...]
    sigmoid = jax.nn.sigmoid(values)
    grad_gate = (grads * upper[...] * sigmoid * (1.0 + values * (1.0 - sigmoid))).astype(BF)
    grad_up = (grads * values * sigmoid).astype(BF)
    chosen = select.shape[1]
    gate_packet[:, :chosen] = select[...]
    gate_packet[:, chosen:] = grad_gate
    grad_up_out[...] = grad_up
    half = values.shape[0] // 2
    sent_out[...] = (
        dot(grad_gate[half:], wg[...], COLS) + dot(grad_up[half:], wu[...], COLS)
    ).astype(BF)
    kept_out[...] = dot(grad_gate[:half], wg[...], COLS) + dot(grad_up[:half], wu[...], COLS)


def attention_backward_kernel(
    count, ranks, cot, resid, half0, half1, gain, wo, attn, sums, query_rot, positions, *refs
):
    blocks = refs[:count]
    grad_own_out, grad_b_out, select_out, gain_out, grad_query_out = refs[count : count + 5]
    terms = refs[count + 5 :]
    rows = query_rot.shape[0]
    key_width = blocks[0].shape[1] // 2
    values = resid[...]
    scale = row_norm(values)
    normed = values * scale
    grads = jnp.concatenate([half0[...], half1[...]], axis=0).astype(F32)
    inner = grads * gain[...]
    grad_in = scale * (inner - normed * jnp.mean(inner * normed, axis=-1, keepdims=True))
    grad_resid = cot[...].astype(F32) + grad_in
    own = rows // 4
    grad_own_out[...] = grad_resid[:own]
    gain_out[...] = jnp.sum(grads[:own] * normed[:own], axis=0, keepdims=True)
    grad_resid_b = grad_resid.astype(BF)
    grad_b_out[...] = grad_resid_b
    select_columns(ranks, grad_b_out, select_out)
    grad_attn = dot(grad_resid_b, wo[...], COLS)
    delta = jnp.transpose(group_sum(grad_attn * attn[...]))
    grad_attn_b = grad_attn.astype(BF)

    query_index = ranks[0] * rows + place_of(lanes((1, rows)), rows, ranks[1])
    first_row = query_index - positions[...]
    key_place = place_of(lax.broadcasted_iota(jnp.int32, (rows, 1), 0), rows, ranks[1])
    stacked = [stack(query_rot[:, h * 128 : (h + 1) * 128], h) for h in range(2)]
    stacked_b = [s.astype(BF) for s in stacked]
    scaled = [(s * SCALE).astype(BF) for s in stacked]
    grads_b = [
        stack(grad_attn_b[:, h * 128 : (h + 1) * 128], h).astype(BF) for h in range(2)
    ]
    deltas = [
        jnp.concatenate(
            [delta[2 * h * HD : 2 * h * HD + 1], delta[(2 * h + 1) * HD : (2 * h + 1) * HD + 1]],
            axis=1,
        )
        for h in range(2)
    ]
    grad_query = [jnp.zeros((2 * rows, key_width), F32) for _ in range(2)]
    for d in range(count - 1, -1, -1):
        key_index = (ranks[0] - d) * rows + key_place
        mask = key_index >= first_row
        if d == 0:
            mask = mask & (key_index <= query_index)
        mask = jnp.where(mask, 0.0, MASKED_SCORE)
        mask = jnp.concatenate([mask, mask], axis=1)
        key_block = blocks[d][:, :key_width]
        value_block = blocks[d][:, key_width:]
        key_term = jnp.zeros((rows, key_width), F32)
        value_term = jnp.zeros((rows, key_width), F32)
        for h in range(2):
            scores = dot(key_block, scaled[h], COLS) + mask
            probs = jnp.exp(scores - sums[h : h + 1, :])
            grad_probs = dot(value_block, grads_b[h], COLS)
            grad_scores = (probs * (grad_probs - deltas[h]) * SCALE).astype(BF)
            key_term = key_term + dot(grad_scores, stacked_b[h])
            value_term = value_term + dot(probs.astype(BF), grads_b[h])
            grad_query[h] = grad_query[h] + dot(grad_scores, key_block, ROWS)
        terms[d][:, :key_width] = key_term.astype(terms[d].dtype)
        terms[d][:, key_width:] = value_term.astype(terms[d].dtype)
    for h in range(2):
        grad_query_out[:, h * 128 : (h + 1) * 128] = unstack(grad_query[h], h)


def query_backward_kernel(
    queries, gain, grads, cos, sin, wq, select, late_out, gain_out, partial_out
):
    grad_in, gain_terms = head_norm_backward(queries[...], gain[...], grads[...], cos[...], sin[...])
    grad_b = grad_in.astype(BF)
    chosen = select.shape[1]
    late_out[:, :chosen] = select[...]
    late_out[:, chosen:] = grad_b
    gain_out[...] = gain_terms
    partial_out[...] = dot(grad_b, wq[...], COLS)


def key_backward_kernel(
    ranks, keys, gain, cos, sin, wk, wv, query_partial, x0, x1, x2, x3,
    ffn_gain_part, query_gain_part, term, arrived, *refs,
):
    shifted = refs[:-4]
    grad_out, gains_out, kept_out, sent_out = refs[-4:]
    width = keys.shape[-1]
    grads = term[...] + jnp.where(ranks[0] % 2 == 1, 0.0, arrived[...].astype(F32))
    for other in shifted:
        grads = grads + other[...].astype(F32)
    grad_in, gain_terms = head_norm_backward(
        keys[...], gain[...], grads[:, :width], cos[...], sin[...]
    )
    grad_b = grad_in.astype(BF)
    value_b = grads[:, width:].astype(BF)
    grad_out[:, :width] = grad_b
    grad_out[:, width:] = value_b
    partial = query_partial[...] + dot(grad_b, wk[...], COLS) + dot(value_b, wv[...], COLS)
    half = partial.shape[0] // 2
    kept_out[...] = partial[:half]
    sent_out[...] = partial[half:].astype(BF)
    x = jnp.concatenate([x0[...], x1[...], x2[...], x3[...]], axis=0).astype(F32)
    features = x.shape[1]
    parts = [
        jnp.sum(partial * (x * row_norm(x)), axis=0, keepdims=True),
        ffn_gain_part[...],
    ]
    row = 0
    for part in parts:
        for c in range(features // 128):
            gains_out[row : row + 1, :] = part[:, c * 128 : (c + 1) * 128]
            row += 1
    queries = query_gain_part[...]
    queries = sum(queries[:, c * 128 : (c + 1) * 128] for c in range(queries.shape[1] // 128))
    gains_out[row : row + 1, :] = queries
    gains_out[row + 1 : row + 2, :] = gain_terms


def weight_grad_kernel(
    offsets, ranks, act, arrived_act, grads, arrived_grads, kept_out, sent_out
):
    parity = ranks[0] % 2
    mine = ranks[0] // 2
    own, there_at = offsets
    width = kept_out.shape[1]
    mine_grads = grads[:, own : own + width]
    other_grads = arrived_grads[:, there_at : there_at + width]
    for lo in (1, 0):
        for hi in range(2):
            block = jnp.bitwise_xor(mine, lo + 2 * hi)
            start = pl.multiple_of((2 * block + parity) * 128, 128)
            there = pl.multiple_of(block * 128, 128)
            total = dot(act[:, pl.ds(start, 128)], mine_grads, ROWS) + dot(
                arrived_act[:, pl.ds(there, 128)], other_grads, ROWS
            )
            target = sent_out if lo else kept_out
            target[hi * 128 : (hi + 1) * 128, :] = total.astype(target.dtype)


def shape(dims, dtype):
    return jax.ShapeDtypeStruct(dims, dtype)


def launch(kernel, outs, args, scratch=(), name=None, after=()):
    nbytes = sum(s.shape[0] * s.shape[1] * 4 for s in scratch)
    n_in, n_after = len(args), len(after)

    def run(*refs):
        kernel(*refs[:n_in], *refs[n_in + n_after :])

    return pl.pallas_call(
        run,
        out_shape=outs,
        in_specs=[
            pl.BlockSpec(memory_space=pltpu.SMEM if a.shape == (2,) else pltpu.VMEM) for a in args
        ]
        + [pl.BlockSpec(memory_space=pl.ANY)] * n_after,
        out_specs=[pl.BlockSpec(memory_space=pltpu.VMEM) for _ in outs],
        scratch_shapes=list(scratch),
        compiler_params=pltpu.CompilerParams(vmem_limit_bytes=nbytes + (12 << 20)),
        name=name,
    )(*args, *after)


def add(kept, arrived, dtype, name, kernel=add_kernel, after=()):
    return launch(kernel, [shape(kept.shape, dtype)], [kept, arrived], name=name, after=after)[0]


def mp_order(values):
    rank = lax.axis_index("mp")
    parts = values.reshape(2, 2, -1)
    parts = jnp.swapaxes(parts, 0, 1)
    parts = jnp.where(rank % 2 == 1, parts[::-1], parts)
    parts = jnp.where(rank // 2 == 1, parts[:, ::-1], parts)
    return parts.reshape(values.shape)


def mp_gather(values):
    other = xor(values, "mp", 2)
    core = xor(values, "mp", 1)
    return values, other, core, xor(other, "mp", 1)


def mp_reduce_start(kept, sent, name):
    own = kept.shape[0] // 2
    kept, back = launch(
        fold_kernel,
        [shape((own, kept.shape[1]), F32), shape((own, kept.shape[1]), BF)],
        [kept, xor(sent, "mp", 1)],
        name=name,
    )
    return kept, xor(back, "mp", 2)


def mp_allreduce(kept, sent, name):
    kept = add(kept, xor(sent, "mp", 1), BF, name + "_core")
    both = add(kept, xor(kept, "mp", 2), BF, name + "_chip", kernel=flipped_add_kernel)
    return both, xor(both, "mp", 1)


def split_columns(values):
    n = lax.axis_size("ctx")
    index = lax.axis_index("ctx")
    rows, columns = values.shape
    bits = n.bit_length() - 1
    parts = values.reshape((rows,) + (2,) * bits + (columns // n,))
    for bit in range(bits):
        parts = jnp.where((index >> bit) % 2 == 1, jnp.flip(parts, bits - bit), parts)
    order = [0] + [bits - b for b in range(bits)] + [bits + 1]
    parts = jnp.transpose(parts, order).reshape(rows, 2, columns // 2)
    return parts[:, 0], parts[:, 1]


def weight_grad(ranks, act, arrived_act, grads, arrived_grads, offsets, columns, name, after=()):
    n = lax.axis_size("ctx")
    half = act.shape[1] // 4
    if n == 8 and act.shape[1] == 1024:
        return launch(
            functools.partial(weight_grad_kernel, offsets),
            [shape((half, columns), F32), shape((half, columns), BF)],
            [ranks, act, arrived_act, grads, arrived_grads],
            name=name,
            after=after,
        )
    own, other = split_columns(act)
    grads = grads[:, offsets[0] : offsets[0] + columns]
    arrived_grads = arrived_grads[:, offsets[1] : offsets[1] + columns]
    both = jnp.concatenate([own, xor(other, "ctx", 1)], axis=0)
    total = dot(both, jnp.concatenate([grads, arrived_grads], axis=0), ROWS)
    return total[:half], total[half:].astype(BF)


def halve(kept, sent, name, after=()):
    n = lax.axis_size("ctx")
    arrived = xor(sent, "ctx", 2)
    mask = 4
    while mask < n:
        half, columns = kept.shape[0] // 2, kept.shape[1]
        kept, back = launch(
            fold_kernel,
            [shape((half, columns), F32), shape((half, columns), BF)],
            [kept, arrived],
            name=name + "_fold",
            after=after,
        )
        arrived = xor(back, "ctx", mask)
        mask *= 2
    return kept, arrived


def body(
    block_in,
    attn_gain,
    query_weight,
    key_weight,
    value_weight,
    out_weight,
    query_gain,
    key_gain,
    ffn_gain,
    gate_weight,
    up_weight,
    down_weight,
    segments,
    positions,
    cotangent,
):
    width = block_in.shape[1]
    key_width = key_weight.shape[1]
    query_width = query_weight.shape[1]
    hidden_width = gate_weight.shape[1]
    n_ctx = lax.axis_size("ctx")
    ctx_rank = lax.axis_index("ctx")
    own_rows = block_in.shape[0]
    rows = positions.shape[0]
    total_tokens = rows * n_ctx
    longest = LONGEST.get(total_tokens, total_tokens)
    window = min(n_ctx - 1, -(-(longest - 1) // rows))
    slots = (window + 1) // 2
    count = window + 1
    half = rows // 2
    ranks = jnp.stack([ctx_rank, lax.axis_index("mp")]).astype(jnp.int32)

    x = mp_gather(block_in)
    positions = mp_order(positions)
    lane = jnp.arange(128, dtype=jnp.int32)
    freqs = ROPE_BASE ** (-2.0 * (lane % (HD // 2)).astype(F32) / HD)
    angles = positions.astype(F32)[:, None] * freqs[None, :]
    cos = jnp.cos(angles)
    sin = jnp.sin(angles) * jnp.where(lane % HD < HD // 2, -1.0, 1.0)[None, :]
    query_gain_row = jnp.tile(query_gain, query_width // HD).reshape(1, -1)
    key_gain_row = jnp.tile(key_gain, key_width // HD).reshape(1, -1)
    attn_gain_row = attn_gain.reshape(1, -1)
    ffn_gain_row = ffn_gain.reshape(1, -1)
    position_column = positions.reshape(-1, 1)
    position_row = positions.reshape(1, -1)

    act_attn, act_attn_select, pair, query_rot, queries, keys_pre = launch(
        qkv_kernel,
        [
            shape((rows, width), BF),
            shape((rows, width // 2), BF),
            shape((rows, 2 * key_width), BF),
            shape((rows, query_width), BF),
            shape((rows, query_width), F32),
            shape((rows, key_width), F32),
        ],
        [ranks, *x, attn_gain_row, query_weight, key_weight, value_weight,
         query_gain_row, key_gain_row, cos, sin],
        name="qkv",
        after=[position_column, position_row],
    )

    def cross(values, odd):
        return lax.ppermute(values, "ctx", [(i, i ^ 1) for i in range(odd, n_ctx, 2)])

    def climb(step):
        if step >= n_ctx:
            return jnp.zeros_like(pair)
        only_odd = step > window
        pairs = [(i, i + step) for i in range(n_ctx - step) if i % 2 == 1 or not only_odd]
        return lax.ppermute(pair, "ctx", pairs)

    items = [pair] + [climb(2 * k) for k in range(1, slots + 1)]
    low_odd = [cross(items[j], 0) for j in range(slots)]
    high_odd = [cross(items[j + 1], 1) for j in range(slots)]
    even = items[:slots]

    cot, cot_select, grad_hidden = launch(
        cotangent_kernel,
        [
            shape((rows, width), BF),
            shape((rows, width // 2), BF),
            shape((rows, hidden_width), F32),
        ],
        [ranks, *mp_gather(cotangent), down_weight],
        name="cotangent",
    )
    cot_there = xor(cot_select, "ctx", 1)

    outs = launch(
        functools.partial(attention_kernel, count),
        [
            shape((rows, query_width), F32),
            shape((rows, width // 2 + query_width), BF),
            shape((2, 2 * rows), F32),
            shape((half, width), F32),
            shape((half, width), BF),
        ]
        + [shape((rows, 2 * key_width), BF) for _ in range(slots)],
        [ranks, query_rot, position_column, out_weight, act_attn_select,
         *even, *low_odd, *high_odd],
        scratch=[pltpu.VMEM((2 * rows, count * rows), F32)],
        name="attention",
        after=[grad_hidden],
    )
    attn_rows, early, log_sums, kept, sent = outs[:5]
    blocks = [(even, outs[5:])[d % 2][d // 2] for d in range(count)]
    resid_halves = mp_allreduce(kept, sent, "resid")
    early_there = xor(early, "ctx", 1)
    chosen = width // 2

    resid, act_ffn, act_select, gate_pre, up_proj, hidden = launch(
        ffn_forward_kernel,
        [
            shape((rows, width), F32),
            shape((rows, width), BF),
            shape((rows, width // 2), BF),
            shape((rows, hidden_width), F32),
            shape((rows, hidden_width), F32),
            shape((rows, hidden_width), BF),
        ],
        [ranks, *x, *resid_halves, ffn_gain_row, gate_weight, up_weight],
        name="ffn_forward",
    )
    hidden_there = xor(hidden, "ctx", 1)
    gate_packet, grad_up, kept, sent = launch(
        ffn_backward_kernel,
        [
            shape((rows, chosen + hidden_width), BF),
            shape((rows, hidden_width), BF),
            shape((half, width), F32),
            shape((half, width), BF),
        ],
        [gate_pre, up_proj, grad_hidden, gate_weight, up_weight, act_select],
        name="ffn_backward",
        after=[early_there, cot_there],
    )
    grad_act_halves = mp_allreduce(kept, sent, "grad_act")
    gate_there = xor(gate_packet, "ctx", 1)
    up_there = xor(grad_up, "ctx", 1)

    down_kept, down_sent = weight_grad(
        ranks, cot, cot_there, hidden, hidden_there, (0, 0), hidden_width, "down_grad",
        after=[grad_act_halves[1]],
    )

    outs = launch(
        functools.partial(attention_backward_kernel, count),
        [
            shape((own_rows, width), F32),
            shape((rows, width), BF),
            shape((rows, width // 2), BF),
            shape((1, width), F32),
            shape((rows, query_width), F32),
        ]
        + [shape((rows, 2 * key_width), BF if d else F32) for d in range(count)],
        [ranks, cot, resid, *grad_act_halves, ffn_gain_row, out_weight, attn_rows, log_sums,
         query_rot, position_row, *blocks],
        name="attention_backward",
        after=[down_sent],
    )
    grad_resid, grad_resid_b, grad_select, ffn_gain_part, grad_query = outs[:5]
    terms = outs[5:]

    arrived = [xor(terms[2 * j + 1], "ctx", 1) for j in range(slots)]
    shifted = []
    if 2 * slots < n_ctx:
        pairs = [(i, i - 2 * slots) for i in range(2 * slots, n_ctx) if i % 2 == 1]
        shifted.append(lax.ppermute(arrived[slots - 1], "ctx", pairs))
    for k in range(slots - 1, 0, -1):
        total = launch(
            pair_sum_kernel,
            [shape(terms[0].shape, BF)],
            [ranks, terms[2 * k], arrived[k - 1], arrived[k]],
            name="pair_sum",
        )[0]
        shifted.append(down(total, 2 * k))

    late, query_gain_part, query_partial = launch(
        query_backward_kernel,
        [
            shape((rows, chosen + query_width), BF),
            shape((1, query_width), F32),
            shape((rows, width), F32),
        ],
        [queries, query_gain_row, grad_query, cos, sin, query_weight, grad_select],
        name="query_backward",
        after=[total],
    )
    late_there = xor(late, "ctx", 1)
    out_kept, out_sent = launch(
        down_kernel,
        [shape((half, width), F32), shape((half, width), BF)],
        [hidden, down_weight],
        name="down",
        after=[query_partial],
    )
    gate_kept, gate_sent = weight_grad(
        ranks, act_ffn, gate_there, gate_packet, gate_there, (chosen, chosen), hidden_width,
        "gate_grad", after=[query_partial],
    )
    pair_b, gains, kept, sent = launch(
        key_backward_kernel,
        [
            shape((rows, 2 * key_width), BF),
            shape((2 * width // 128 + 2, 128), F32),
            shape((half, width), F32),
            shape((half, width), BF),
        ],
        [ranks, keys_pre, key_gain_row, cos, sin, key_weight, value_weight, query_partial, *x,
         ffn_gain_part, query_gain_part, terms[0], arrived[0], *shifted],
        name="key_backward",
        after=[gate_sent, out_sent],
    )
    pair_there = xor(pair_b, "ctx", 1)
    kept, across = mp_reduce_start(kept, sent, "grad_input_core")
    grad_input = launch(
        grad_input_kernel,
        [shape((own_rows, width), F32)],
        [x[0], attn_gain_row, grad_resid, kept, across],
        name="grad_input",
    )[0]
    up_kept, up_sent = weight_grad(
        ranks, act_ffn, gate_there, grad_up, up_there, (0, 0), hidden_width, "up_grad",
        after=[kept],
    )
    out_w_kept, out_w_sent = weight_grad(
        ranks, grad_resid_b, late_there, early, early_there, (chosen, chosen), query_width,
        "out_grad", after=[kept],
    )
    query_kept, query_sent = weight_grad(
        ranks, act_attn, early_there, late, late_there, (chosen, chosen), query_width,
        "query_grad", after=[kept],
    )
    pair_kept, pair_sent = weight_grad(
        ranks, act_attn, early_there, pair_b, pair_there, (0, 0), 2 * key_width,
        "key_value_grad", after=[query_sent],
    )

    def finish(halves, name, kernel=add_kernel, turned=False):
        kept, arrived = halves
        dims = kept.shape[::-1] if turned else kept.shape
        return launch(kernel, [shape(dims, F32)], [kept, arrived], name=name)[0]

    down_grad = finish(halve(down_kept, down_sent, "down"), "down_last", turned_add_kernel, True)
    gate_grad = finish(halve(gate_kept, gate_sent, "gate"), "gate_last")
    up_grad = finish(halve(up_kept, up_sent, "up"), "up_last")
    out_grad = finish(halve(out_w_kept, out_w_sent, "out"), "out_last", turned_add_kernel, True)
    query_grad = finish(halve(query_kept, query_sent, "query"), "query_last")
    pair_kept, pair_arrived = halve(pair_kept, pair_sent, "key_value")
    key_grad, value_grad = launch(
        split_add_kernel,
        [shape((pair_kept.shape[0], key_width), F32)] * 2,
        [pair_kept, pair_arrived],
        name="key_value_last",
    )

    out_kept, out_across = mp_reduce_start(out_kept, out_sent, "block_out_core")
    block_out = launch(
        block_out_kernel,
        [shape((own_rows, width), BF)],
        [resid, out_kept, out_across],
        name="block_out",
    )[0]

    for axis in ("mp", "ctx"):
        mask = 1
        while mask < lax.axis_size(axis):
            gains = add(gains, xor(gains, axis, mask), F32, "gains")
            mask *= 2
    gains = gains.reshape(-1)
    heads = gains[2 * width :].reshape(2, -1, HD).sum(axis=1)
    query_gains, key_gains = heads[0], heads[1]
    return (
        block_out,
        grad_input,
        query_grad,
        key_grad,
        value_grad,
        out_grad,
        gate_grad,
        up_grad,
        down_grad,
        gains[:width],
        gains[width : 2 * width],
        query_gains,
        key_gains,
    )


def solution(mesh):
    in_specs = (
        P(("ctx", "mp"), None),
        P(),
        P(None, "mp"),
        P(None, "mp"),
        P(None, "mp"),
        P("mp", None),
        P(),
        P(),
        P(),
        P(None, "mp"),
        P(None, "mp"),
        P("mp", None),
        P(),
        P("ctx"),
        P(("ctx", "mp"), None),
    )
    out_specs = (
        P(("ctx", "mp"), None),
        P(("ctx", "mp"), None),
        P("ctx", "mp"),
        P("ctx", "mp"),
        P("ctx", "mp"),
        P("mp", "ctx"),
        P("ctx", "mp"),
        P("ctx", "mp"),
        P("mp", "ctx"),
        P(),
        P(),
        P(),
        P(),
    )
    return jax.shard_map(body, mesh=mesh, in_specs=in_specs, out_specs=out_specs, check_vma=False)
```

```python
import functools
import math

import jax
import jax.numpy as jnp
from jax import lax
from jax.experimental import pallas as pl
from jax.experimental.pallas import tpu as pltpu
from jax.sharding import PartitionSpec as P

HEADS = 16
KV_HEADS = 8
HD = 64
EPS = 1e-05
ROPE_BASE = 1000000.0
MASKED_SCORE = -1e30
LONGEST = {2048: 1280, 8192: 4352}
BF = jnp.bfloat16
F32 = jnp.float32
ROWS = (((0,), (0,)), ((), ()))
COLS = (((1,), (1,)), ((), ()))
SCALE = HD ** (-0.5)


def dot(a, b, dims=(((1,), (0,)), ((), ()))):
    return lax.dot_general(a, b, dims, preferred_element_type=F32)


def xor(values, axis, mask):
    n = lax.axis_size(axis)
    return lax.ppermute(values, axis, [(i, i ^ mask) for i in range(n)])


def up(values, step):
    n = lax.axis_size("ctx")
    return lax.ppermute(values, "ctx", [(i, i + step) for i in range(n - step)])


def down(values, step):
    n = lax.axis_size("ctx")
    return lax.ppermute(values, "ctx", [(i, i - step) for i in range(step, n)])


def lanes(shape):
    return lax.broadcasted_iota(jnp.int32, shape, len(shape) - 1)


def group_sum(values):
    width = values.shape[-1]
    line = lax.broadcasted_iota(jnp.int32, (width, width), 0) // HD
    ones = (line == lanes((width, width)) // HD).astype(BF)
    front = values.astype(BF)
    back = (values - front.astype(F32)).astype(BF)
    return dot(front, ones) + dot(back, ones)


def partner(values):
    width = values.shape[-1]
    first = lanes(values.shape) % HD < HD // 2
    return jnp.where(
        first, pltpu.roll(values, width - HD // 2, 1), pltpu.roll(values, HD // 2, 1)
    )


def wide(table, width):
    return jnp.concatenate([table] * (width // table.shape[-1]), axis=-1)


def row_norm(values):
    return lax.rsqrt(jnp.mean(values * values, axis=-1, keepdims=True) + EPS)


def head_norm(values):
    return lax.rsqrt(group_sum(values * values) * (1.0 / HD) + EPS)


def head_norm_backward(values, gain, grads, cos, sin):
    width = values.shape[-1]
    grads = grads * wide(cos, width) - partner(grads) * wide(sin, width)
    scale = head_norm(values)
    normed = values * scale
    inner = grads * gain
    grad_in = scale * (inner - normed * (group_sum(inner * normed) * (1.0 / HD)))
    return grad_in, jnp.sum(grads * normed, axis=0, keepdims=True)


def place_of(iota, rows, rank):
    quarter = rows // 4
    part = iota // quarter
    relative = (part % 2) * 2 + part // 2
    return jnp.bitwise_xor(relative, rank) * quarter + iota % quarter


def stack(slab, kv_head):
    slab = slab.astype(F32)
    turned = pltpu.roll(slab, HD, 1)
    low = lanes(slab.shape) < HD
    if kv_head == 0:
        parts = [jnp.where(low, slab, 0.0), jnp.where(low, turned, 0.0)]
    else:
        parts = [jnp.where(low, 0.0, turned), jnp.where(low, 0.0, slab)]
    return jnp.concatenate(parts, axis=0)


def unstack(stacked, kv_head):
    rows = stacked.shape[0] // 2
    first, second = stacked[:rows], stacked[rows:]
    low = lanes(first.shape) < HD
    if kv_head == 0:
        return jnp.where(low, first, pltpu.roll(second, HD, 1))
    return jnp.where(low, pltpu.roll(first, HD, 1), second)


def qkv_kernel(
    ranks, x0, x1, x2, x3, gain, wq, wk, wv, query_gain, key_gain, positions,
    act_out, select_out, pair_out, query_rot_out, query_out, key_out,
    cos_out, sin_out, column_out, row_out,
):
    rows = act_out.shape[0]
    line = lax.broadcasted_iota(jnp.int32, (rows, rows), 0)
    picked = place_of(line, rows, ranks[1]) == lanes((rows, rows))
    column = jnp.sum(
        jnp.where(picked, positions[...].astype(F32), 0.0), axis=1, keepdims=True
    )
    column_out[...] = column.astype(jnp.int32)
    row = jnp.sum(jnp.where(line == lanes((rows, rows)), column, 0.0), axis=0, keepdims=True)
    row_out[...] = row.astype(jnp.int32)
    lane = lanes((1, 128))
    power = (lane % (HD // 2)).astype(F32) * (-2.0 / HD)
    angles = column * jnp.exp(power * math.log(ROPE_BASE))
    cos = jnp.cos(angles)
    sin = jnp.sin(angles) * jnp.where(lane % HD < HD // 2, -1.0, 1.0)
    cos_out[...] = cos
    sin_out[...] = sin

    x = jnp.concatenate([x0[...], x1[...], x2[...], x3[...]], axis=0).astype(F32)
    act = (x * row_norm(x) * gain[...]).astype(BF)
    act_out[...] = act
    keys = dot(act, wk[...])
    key_out[...] = keys
    width = keys.shape[-1]
    normed = keys * head_norm(keys) * wide(key_gain[...], width)
    rotated = normed * wide(cos, width) + partner(normed) * wide(sin, width)
    pair_out[:, :width] = rotated.astype(BF)
    pair_out[:, width:] = dot(act, wv[...]).astype(BF)
    queries = dot(act, wq[...])
    query_out[...] = queries
    width = queries.shape[-1]
    normed = queries * head_norm(queries) * wide(query_gain[...], width)
    rotated = normed * wide(cos, width) + partner(normed) * wide(sin, width)
    query_rot_out[...] = rotated.astype(BF)
    select_columns(ranks, act_out, select_out)


def select_columns(ranks, source, target):
    columns = target.shape[1]
    blocks = columns // 128
    if blocks != 4:
        target[...] = jnp.zeros(target.shape, target.dtype)
        return
    for b in range(blocks):
        start = pl.multiple_of((2 * b + 1 - ranks[0] % 2) * 128, 128)
        target[:, b * 128 : (b + 1) * 128] = source[:, pl.ds(start, 128)]


def cotangent_kernel(ranks, c0, c1, c2, c3, wd, cot_out, select_out, grad_hidden_out):
    cot = jnp.concatenate([c0[...], c1[...], c2[...], c3[...]], axis=0)
    cot_out[...] = cot
    select_columns(ranks, cot_out, select_out)
    grad_hidden_out[...] = dot(cot, wd[...], COLS)


def attention_kernel(count, ranks, query_rot, positions, wo, act_select, *refs):
    slots = count // 2
    even = refs[:slots]
    low_odd, high_odd = refs[slots : 2 * slots], refs[2 * slots : 3 * slots]
    out_f32, early_out, sums_out, kept_out, sent_out = refs[3 * slots : 3 * slots + 5]
    odd = refs[3 * slots + 5 : -1]
    scores = refs[-1]
    rows = query_rot.shape[0]
    key_width = even[0].shape[1] // 2
    for j in range(slots):
        odd[j][...] = jnp.where(
            ranks[0] % 2 == 1, low_odd[j][...].astype(F32), high_odd[j][...].astype(F32)
        ).astype(BF)
    blocks = [(even, odd)[d % 2][d // 2] for d in range(count)]
    query_index = ranks[0] * rows + place_of(
        lax.broadcasted_iota(jnp.int32, (rows, 1), 0), rows, ranks[1]
    )
    first_seen = query_index - positions[...]
    key_place = place_of(lanes((1, rows)), rows, ranks[1])
    masks = []
    for d in range(count):
        key_index = (ranks[0] - d) * rows + key_place
        mask = key_index >= first_seen
        if d == 0:
            mask = mask & (key_index <= query_index)
        masks.append(jnp.where(mask, 0.0, MASKED_SCORE))
    for head in range(2):
        slab = query_rot[:, head * 128 : (head + 1) * 128]
        stacked = (stack(slab, head) * SCALE).astype(BF)
        top = jnp.full((2 * rows, 1), MASKED_SCORE, F32)
        for d in range(count):
            block = dot(stacked, blocks[d][:, :key_width], COLS)
            block = block + jnp.concatenate([masks[d], masks[d]], axis=0)
            scores[:, d * rows : (d + 1) * rows] = block
            top = jnp.maximum(top, jnp.max(block, axis=-1, keepdims=True))
        total = jnp.zeros((2 * rows, 1), F32)
        mixed = jnp.zeros((2 * rows, key_width), F32)
        for d in range(count):
            weights = jnp.exp(scores[:, d * rows : (d + 1) * rows] - top)
            total = total + jnp.sum(weights, axis=-1, keepdims=True)
            mixed = mixed + dot(weights.astype(BF), blocks[d][:, key_width:])
        sums = jnp.broadcast_to(top + jnp.log(total), (2 * rows, 128))
        sums_out[head : head + 1, :] = jnp.transpose(sums)[:1]
        out_f32[:, head * 128 : (head + 1) * 128] = unstack(mixed / total, head)
    attn_b = out_f32[...].astype(BF)
    chosen = act_select.shape[1]
    early_out[:, :chosen] = act_select[...]
    early_out[:, chosen:] = attn_b
    half = rows // 2
    kept_out[...] = dot(attn_b[:half], wo[...])
    sent_out[...] = dot(attn_b[half:], wo[...]).astype(BF)


def add_kernel(kept, arrived, out):
    out[...] = (kept[...].astype(F32) + arrived[...].astype(F32)).astype(out.dtype)


def flipped_add_kernel(kept, arrived, out):
    half = kept.shape[0] // 2
    for a, b in ((0, half), (half, 0)):
        total = kept[a : a + half, :].astype(F32) + arrived[b : b + half, :].astype(F32)
        out[a : a + half, :] = total.astype(out.dtype)


def fold_kernel(kept, arrived, front_out, back_out):
    half = front_out.shape[0]
    front_out[...] = kept[:half, :] + arrived[:half, :].astype(F32)
    back_out[...] = (kept[half:, :] + arrived[half:, :].astype(F32)).astype(BF)


def turned_add_kernel(kept, arrived, out):
    out[...] = jnp.transpose(kept[...] + arrived[...].astype(F32))


def attention_last_kernel(kept, arrived, out_grad, query_grad, key_grad, value_grad):
    total = kept[...] + arrived[...].astype(F32)
    turned = out_grad.shape[0]
    out_grad[...] = jnp.transpose(total[:, :turned])
    start = turned
    for out in (query_grad, key_grad, value_grad):
        width = out.shape[1]
        out[...] = total[:, start : start + width]
        start += width


def pair_sum_kernel(ranks, term, if_odd, if_even, out):
    odd = ranks[0] % 2 == 1
    out[...] = (
        term[...].astype(F32)
        + jnp.where(odd, if_odd[...].astype(F32), if_even[...].astype(F32))
    ).astype(BF)


def down_kernel(hidden, wd, kept_out, sent_out):
    half = hidden.shape[0] // 2
    sent_out[...] = dot(hidden[half:, :], wd[...]).astype(BF)
    kept_out[...] = dot(hidden[:half, :], wd[...])


def block_out_kernel(resid, kept, arrived, out):
    own = out.shape[0]
    out[...] = (resid[:own, :] + kept[:own, :] + arrived[...].astype(F32)).astype(BF)


def grad_input_kernel(x, gain, grad_resid, kept, arrived, out):
    own = out.shape[0]
    grads = kept[:own, :] + arrived[...].astype(F32)
    values = x[...].astype(F32)
    scale = row_norm(values)
    normed = values * scale
    inner = grads * gain[...]
    out[...] = grad_resid[...] + scale * (
        inner - normed * jnp.mean(inner * normed, axis=-1, keepdims=True)
    )


def ffn_forward_kernel(
    ranks, x0, x1, x2, x3, half0, half1, gain, wg, wu,
    resid_out, act_out, select_out, gate_out, up_out, hidden_out,
):
    x = jnp.concatenate([x0[...], x1[...], x2[...], x3[...]], axis=0).astype(F32)
    resid = x + jnp.concatenate([half0[...], half1[...]], axis=0).astype(F32)
    resid_out[...] = resid
    act = (resid * row_norm(resid) * gain[...]).astype(BF)
    act_out[...] = act
    gate = dot(act, wg[...])
    upper = dot(act, wu[...])
    gate_out[...] = gate
    up_out[...] = upper
    hidden_out[...] = (gate * jax.nn.sigmoid(gate) * upper).astype(BF)
    select_columns(ranks, act_out, select_out)


def ffn_backward_kernel(
    gate, upper, grad_hidden, wg, wu, select, gate_packet, grad_up_out, kept_out, sent_out
):
    grads = grad_hidden[...]
    values = gate[...]
    sigmoid = jax.nn.sigmoid(values)
    grad_gate = (grads * upper[...] * sigmoid * (1.0 + values * (1.0 - sigmoid))).astype(BF)
    grad_up = (grads * values * sigmoid).astype(BF)
    chosen = select.shape[1]
    gate_packet[:, :chosen] = select[...]
    gate_packet[:, chosen:] = grad_gate
    grad_up_out[...] = grad_up
    half = values.shape[0] // 2
    sent_out[...] = (
        dot(grad_gate[half:], wg[...], COLS) + dot(grad_up[half:], wu[...], COLS)
    ).astype(BF)
    kept_out[...] = dot(grad_gate[:half], wg[...], COLS) + dot(grad_up[:half], wu[...], COLS)


def attention_backward_kernel(
    count, ranks, cot, resid, half0, half1, gain, wo, attn, sums, query_rot, positions, *refs
):
    blocks = refs[:count]
    grad_own_out, grad_b_out, select_out, gain_out, grad_query_out = refs[count : count + 5]
    terms = refs[count + 5 :]
    rows = query_rot.shape[0]
    key_width = blocks[0].shape[1] // 2
    values = resid[...]
    scale = row_norm(values)
    normed = values * scale
    grads = jnp.concatenate([half0[...], half1[...]], axis=0).astype(F32)
    inner = grads * gain[...]
    grad_in = scale * (inner - normed * jnp.mean(inner * normed, axis=-1, keepdims=True))
    grad_resid = cot[...].astype(F32) + grad_in
    own = rows // 4
    grad_own_out[...] = grad_resid[:own]
    gain_out[...] = jnp.sum(grads[:own] * normed[:own], axis=0, keepdims=True)
    grad_resid_b = grad_resid.astype(BF)
    grad_b_out[...] = grad_resid_b
    select_columns(ranks, grad_b_out, select_out)
    grad_attn = dot(grad_resid_b, wo[...], COLS)
    delta = jnp.transpose(group_sum(grad_attn * attn[...]))
    grad_attn_b = grad_attn.astype(BF)

    query_index = ranks[0] * rows + place_of(lanes((1, rows)), rows, ranks[1])
    first_row = query_index - positions[...]
    key_place = place_of(lax.broadcasted_iota(jnp.int32, (rows, 1), 0), rows, ranks[1])
    stacked = [stack(query_rot[:, h * 128 : (h + 1) * 128], h) for h in range(2)]
    stacked_b = [s.astype(BF) for s in stacked]
    scaled = [(s * SCALE).astype(BF) for s in stacked]
    grads_b = [
        stack(grad_attn_b[:, h * 128 : (h + 1) * 128], h).astype(BF) for h in range(2)
    ]
    deltas = [
        jnp.concatenate(
            [delta[2 * h * HD : 2 * h * HD + 1], delta[(2 * h + 1) * HD : (2 * h + 1) * HD + 1]],
            axis=1,
        )
        for h in range(2)
    ]
    grad_query = [jnp.zeros((2 * rows, key_width), F32) for _ in range(2)]
    for d in range(count - 1, -1, -1):
        key_index = (ranks[0] - d) * rows + key_place
        mask = key_index >= first_row
        if d == 0:
            mask = mask & (key_index <= query_index)
        mask = jnp.where(mask, 0.0, MASKED_SCORE)
        mask = jnp.concatenate([mask, mask], axis=1)
        key_block = blocks[d][:, :key_width]
        value_block = blocks[d][:, key_width:]
        key_term = jnp.zeros((rows, key_width), F32)
        value_term = jnp.zeros((rows, key_width), F32)
        for h in range(2):
            scores = dot(key_block, scaled[h], COLS) + mask
            probs = jnp.exp(scores - sums[h : h + 1, :])
            grad_probs = dot(value_block, grads_b[h], COLS)
            grad_scores = (probs * (grad_probs - deltas[h]) * SCALE).astype(BF)
            key_term = key_term + dot(grad_scores, stacked_b[h])
            value_term = value_term + dot(probs.astype(BF), grads_b[h])
            grad_query[h] = grad_query[h] + dot(grad_scores, key_block, ROWS)
        terms[d][:, :key_width] = key_term.astype(terms[d].dtype)
        terms[d][:, key_width:] = value_term.astype(terms[d].dtype)
    for h in range(2):
        grad_query_out[:, h * 128 : (h + 1) * 128] = unstack(grad_query[h], h)


def query_backward_kernel(
    queries, gain, grads, cos, sin, wq, select, late_out, gain_out, partial_out
):
    grad_in, gain_terms = head_norm_backward(queries[...], wide(gain[...], queries.shape[-1]), grads[...], cos[...], sin[...])
    grad_b = grad_in.astype(BF)
    chosen = select.shape[1]
    late_out[:, :chosen] = select[...]
    late_out[:, chosen:] = grad_b
    gain_out[...] = gain_terms
    partial_out[...] = dot(grad_b, wq[...], COLS)


def key_backward_kernel(
    ranks, keys, gain, cos, sin, wk, wv, query_partial, x0, x1, x2, x3,
    ffn_gain_part, query_gain_part, term, arrived, *refs,
):
    shifted = refs[:-4]
    grad_out, gains_out, kept_out, sent_out = refs[-4:]
    width = keys.shape[-1]
    grads = term[...] + jnp.where(ranks[0] % 2 == 1, 0.0, arrived[...].astype(F32))
    for other in shifted:
        grads = grads + other[...].astype(F32)
    grad_in, gain_terms = head_norm_backward(
        keys[...], wide(gain[...], width), grads[:, :width], cos[...], sin[...]
    )
    grad_b = grad_in.astype(BF)
    value_b = grads[:, width:].astype(BF)
    grad_out[:, :width] = grad_b
    grad_out[:, width:] = value_b
    partial = query_partial[...] + dot(grad_b, wk[...], COLS) + dot(value_b, wv[...], COLS)
    half = partial.shape[0] // 2
    kept_out[...] = partial[:half]
    sent_out[...] = partial[half:].astype(BF)
    x = jnp.concatenate([x0[...], x1[...], x2[...], x3[...]], axis=0).astype(F32)
    features = x.shape[1]
    parts = [
        jnp.sum(partial * (x * row_norm(x)), axis=0, keepdims=True),
        ffn_gain_part[...],
    ]
    row = 0
    for part in parts:
        for c in range(features // 128):
            gains_out[row : row + 1, :] = part[:, c * 128 : (c + 1) * 128]
            row += 1
    queries = query_gain_part[...]
    queries = sum(queries[:, c * 128 : (c + 1) * 128] for c in range(queries.shape[1] // 128))
    gains_out[row : row + 1, :] = queries
    gains_out[row + 1 : row + 2, :] = gain_terms


def weight_grad_kernel(parts, ranks, *refs):
    kept_out, sent_out = refs[-2:]
    parity = ranks[0] % 2
    mine = ranks[0] // 2
    place = 0
    for p, (own, there_at, width) in enumerate(parts):
        act, arrived_act, grads, arrived_grads = refs[4 * p : 4 * p + 4]
        mine_grads = grads[:, own : own + width]
        other_grads = arrived_grads[:, there_at : there_at + width]
        for lo in (1, 0):
            for hi in range(2):
                block = jnp.bitwise_xor(mine, lo + 2 * hi)
                start = pl.multiple_of((2 * block + parity) * 128, 128)
                there = pl.multiple_of(block * 128, 128)
                total = dot(act[:, pl.ds(start, 128)], mine_grads, ROWS) + dot(
                    arrived_act[:, pl.ds(there, 128)], other_grads, ROWS
                )
                target = sent_out if lo else kept_out
                target[hi * 128 : (hi + 1) * 128, place : place + width] = total.astype(
                    target.dtype
                )
        place += width


def shape(dims, dtype):
    return jax.ShapeDtypeStruct(dims, dtype)


def launch(kernel, outs, args, scratch=(), name=None, after=(), carry=()):
    nbytes = sum(s.shape[0] * s.shape[1] * 4 for s in scratch)
    n_in, n_out, n_unused = len(args), len(outs), len(after) + len(carry)

    def run(*refs):
        results = refs[n_in + n_unused :]
        kernel(*refs[:n_in], *results[:n_out], *results[n_out + len(carry) :])

    any_spec = pl.BlockSpec(memory_space=pl.ANY)
    return pl.pallas_call(
        run,
        out_shape=list(outs) + [shape(c.shape, c.dtype) for c in carry],
        in_specs=[
            pl.BlockSpec(memory_space=pltpu.SMEM if a.shape == (2,) else pltpu.VMEM) for a in args
        ]
        + [any_spec] * n_unused,
        out_specs=[pl.BlockSpec(memory_space=pltpu.VMEM) for _ in outs] + [any_spec] * len(carry),
        scratch_shapes=list(scratch),
        input_output_aliases={n_in + len(after) + i: n_out + i for i in range(len(carry))},
        compiler_params=pltpu.CompilerParams(vmem_limit_bytes=nbytes + (12 << 20)),
        name=name,
    )(*args, *after, *carry)


def add(kept, arrived, dtype, name, kernel=add_kernel, after=(), carry=()):
    out = launch(
        kernel, [shape(kept.shape, dtype)], [kept, arrived], name=name, after=after, carry=carry
    )
    return out if carry else out[0]


def mp_gather(values):
    other = xor(values, "mp", 2)
    core = xor(values, "mp", 1)
    return values, other, core, xor(other, "mp", 1)


def mp_reduce_start(kept, sent, name, after=()):
    own = kept.shape[0] // 2
    kept, back = launch(
        fold_kernel,
        [shape((own, kept.shape[1]), F32), shape((own, kept.shape[1]), BF)],
        [kept, xor(sent, "mp", 1)],
        name=name,
        after=after,
    )
    return kept, xor(back, "mp", 2)


def split_columns(values):
    n = lax.axis_size("ctx")
    index = lax.axis_index("ctx")
    rows, columns = values.shape
    bits = n.bit_length() - 1
    parts = values.reshape((rows,) + (2,) * bits + (columns // n,))
    for bit in range(bits):
        parts = jnp.where((index >> bit) % 2 == 1, jnp.flip(parts, bits - bit), parts)
    order = [0] + [bits - b for b in range(bits)] + [bits + 1]
    parts = jnp.transpose(parts, order).reshape(rows, 2, columns // 2)
    return parts[:, 0], parts[:, 1]


def weight_grad(ranks, parts, name, after=()):
    n = lax.axis_size("ctx")
    act = parts[0][0]
    half = act.shape[1] // 4
    columns = sum(part[5] for part in parts)
    if n == 8 and act.shape[1] == 1024:
        return launch(
            functools.partial(weight_grad_kernel, [part[4] + (part[5],) for part in parts]),
            [shape((half, columns), F32), shape((half, columns), BF)],
            [ranks] + [a for part in parts for a in part[:4]],
            name=name,
            after=after,
        )
    totals = []
    for act, _, grads, arrived_grads, offsets, width in parts:
        own, other = split_columns(act)
        grads = grads[:, offsets[0] : offsets[0] + width]
        arrived_grads = arrived_grads[:, offsets[1] : offsets[1] + width]
        both = jnp.concatenate([own, xor(other, "ctx", 1)], axis=0)
        totals.append(dot(both, jnp.concatenate([grads, arrived_grads], axis=0), ROWS))
    total = jnp.concatenate(totals, axis=1)
    return total[:half], total[half:].astype(BF)


def halve(kept, arrived, name, after=()):
    n = lax.axis_size("ctx")
    mask = 4
    while mask < n:
        half, columns = kept.shape[0] // 2, kept.shape[1]
        kept, back = launch(
            fold_kernel,
            [shape((half, columns), F32), shape((half, columns), BF)],
            [kept, arrived],
            name=name,
            after=after,
        )
        arrived = xor(back, "ctx", mask)
        mask *= 2
    return kept, arrived, back


def body(
    block_in,
    attn_gain,
    query_weight,
    key_weight,
    value_weight,
    out_weight,
    query_gain,
    key_gain,
    ffn_gain,
    gate_weight,
    up_weight,
    down_weight,
    segments,
    positions,
    cotangent,
):
    width = block_in.shape[1]
    key_width = key_weight.shape[1]
    query_width = query_weight.shape[1]
    hidden_width = gate_weight.shape[1]
    n_ctx = lax.axis_size("ctx")
    ctx_rank = lax.axis_index("ctx")
    own_rows = block_in.shape[0]
    rows = positions.shape[0]
    total_tokens = rows * n_ctx
    longest = LONGEST.get(total_tokens, total_tokens)
    window = min(n_ctx - 1, -(-(longest - 1) // rows))
    slots = (window + 1) // 2
    count = window + 1
    half = rows // 2
    ranks = jnp.stack([ctx_rank, lax.axis_index("mp")]).astype(jnp.int32)

    x = mp_gather(block_in)
    query_gain_row = query_gain.reshape(1, -1)
    key_gain_row = key_gain.reshape(1, -1)
    attn_gain_row = attn_gain.reshape(1, -1)
    ffn_gain_row = ffn_gain.reshape(1, -1)

    (
        act_attn, act_attn_select, pair, query_rot, queries, keys_pre,
        cos, sin, position_column, position_row,
    ) = launch(
        qkv_kernel,
        [
            shape((rows, width), BF),
            shape((rows, width // 2), BF),
            shape((rows, 2 * key_width), BF),
            shape((rows, query_width), BF),
            shape((rows, query_width), F32),
            shape((rows, key_width), F32),
            shape((rows, 128), F32),
            shape((rows, 128), F32),
            shape((rows, 1), jnp.int32),
            shape((1, rows), jnp.int32),
        ],
        [ranks, *x, attn_gain_row, query_weight, key_weight, value_weight,
         query_gain_row, key_gain_row, positions.reshape(1, -1)],
        name="qkv",
    )

    def cross(values, odd):
        return lax.ppermute(values, "ctx", [(i, i ^ 1) for i in range(odd, n_ctx, 2)])

    def climb(step):
        if step >= n_ctx:
            return jnp.zeros_like(pair)
        only_odd = step > window
        pairs = [(i, i + step) for i in range(n_ctx - step) if i % 2 == 1 or not only_odd]
        return lax.ppermute(pair, "ctx", pairs)

    items = [pair] + [climb(2 * k) for k in range(1, slots + 1)]
    low_odd = [cross(items[j], 0) for j in range(slots)]
    high_odd = [cross(items[j + 1], 1) for j in range(slots)]
    even = items[:slots]

    outs = launch(
        functools.partial(attention_kernel, count),
        [
            shape((rows, query_width), F32),
            shape((rows, width // 2 + query_width), BF),
            shape((2, 2 * rows), F32),
            shape((half, width), F32),
            shape((half, width), BF),
        ]
        + [shape((rows, 2 * key_width), BF) for _ in range(slots)],
        [ranks, query_rot, position_column, out_weight, act_attn_select,
         *even, *low_odd, *high_odd],
        scratch=[pltpu.VMEM((2 * rows, count * rows), F32)],
        name="attention",
    )
    attn_rows, early, log_sums, kept, sent = outs[:5]
    blocks = [(even, outs[5:])[d % 2][d // 2] for d in range(count)]
    chosen = width // 2

    kept = add(kept, xor(sent, "mp", 1), BF, "resid_core")
    cot, cot_select, grad_hidden = launch(
        cotangent_kernel,
        [
            shape((rows, width), BF),
            shape((rows, chosen), BF),
            shape((rows, hidden_width), F32),
        ],
        [ranks, *mp_gather(cotangent), down_weight],
        name="cotangent",
        after=[kept],
    )
    both = add(
        kept, xor(kept, "mp", 2), BF, "resid_chip", kernel=flipped_add_kernel, after=[grad_hidden]
    )
    early_there = xor(early, "ctx", 1)
    cot_there = xor(cot_select, "ctx", 1)

    resid, act_ffn, act_select, gate_pre, up_proj, hidden = launch(
        ffn_forward_kernel,
        [
            shape((rows, width), F32),
            shape((rows, width), BF),
            shape((rows, chosen), BF),
            shape((rows, hidden_width), F32),
            shape((rows, hidden_width), F32),
            shape((rows, hidden_width), BF),
        ],
        [ranks, *x, both, xor(both, "mp", 1), ffn_gain_row, gate_weight, up_weight],
        name="ffn_forward",
    )
    hidden_there = xor(hidden, "ctx", 1)
    gate_packet, grad_up, kept, sent = launch(
        ffn_backward_kernel,
        [
            shape((rows, chosen + hidden_width), BF),
            shape((rows, hidden_width), BF),
            shape((half, width), F32),
            shape((half, width), BF),
        ],
        [gate_pre, up_proj, grad_hidden, gate_weight, up_weight, act_select],
        name="ffn_backward",
    )
    kept, gate_packet = add(kept, xor(sent, "mp", 1), BF, "grad_act_core", carry=[gate_packet])
    gate_there = xor(gate_packet, "ctx", 1)
    both = add(kept, xor(kept, "mp", 2), BF, "grad_act_chip", kernel=flipped_add_kernel)
    down_kept, down_sent = weight_grad(
        ranks, [(cot, cot_there, hidden, hidden_there, (0, 0), hidden_width)], "down_grad",
        after=[both],
    )

    outs = launch(
        functools.partial(attention_backward_kernel, count),
        [
            shape((own_rows, width), F32),
            shape((rows, width), BF),
            shape((rows, chosen), BF),
            shape((1, width), F32),
            shape((rows, query_width), F32),
        ]
        + [shape((rows, 2 * key_width), BF if d else F32) for d in range(count)],
        [ranks, cot, resid, both, xor(both, "mp", 1), ffn_gain_row, out_weight, attn_rows,
         log_sums, query_rot, position_row, *blocks],
        name="attention_backward",
        after=[down_sent],
    )
    grad_resid, grad_resid_b, grad_select, ffn_gain_part, grad_query = outs[:5]
    terms = outs[5:]

    arrived = [xor(terms[2 * j + 1], "ctx", 1) for j in range(slots)]
    gate_kept, gate_sent = weight_grad(
        ranks,
        [(act_ffn, gate_there, gate_packet, gate_there, (chosen, chosen), hidden_width)],
        "gate_grad",
        after=[grad_query],
    )
    down_kept, down_arrived, back = halve(
        down_kept, xor(down_sent, "ctx", 2), "down_fold", after=[gate_sent]
    )
    shifted = []
    if 2 * slots < n_ctx:
        pairs = [(i, i - 2 * slots) for i in range(2 * slots, n_ctx) if i % 2 == 1]
        shifted.append(lax.ppermute(arrived[slots - 1], "ctx", pairs))
    for k in range(slots - 1, 0, -1):
        carried = [grad_up] if k == 1 else []
        total = launch(
            pair_sum_kernel,
            [shape(terms[0].shape, BF)],
            [ranks, terms[2 * k], arrived[k - 1], arrived[k]],
            name="pair_sum",
            after=[back],
            carry=carried,
        )
        if carried:
            grad_up = total[1]
        shifted.append(down(total[0], 2 * k))
    up_there = xor(grad_up, "ctx", 1)

    late, query_gain_part, query_partial = launch(
        query_backward_kernel,
        [
            shape((rows, chosen + query_width), BF),
            shape((1, query_width), F32),
            shape((rows, width), F32),
        ],
        [queries, query_gain_row, grad_query, cos, sin, query_weight, grad_select],
        name="query_backward",
        after=[grad_up],
    )
    late_there = xor(late, "ctx", 1)
    out_kept, out_sent = launch(
        down_kernel,
        [shape((half, width), F32), shape((half, width), BF)],
        [hidden, down_weight],
        name="down",
        after=[query_partial],
    )
    up_kept, up_sent = weight_grad(
        ranks, [(act_ffn, gate_there, grad_up, up_there, (0, 0), hidden_width)], "up_grad",
        after=[out_sent],
    )
    pair_b, gains, kept, sent = launch(
        key_backward_kernel,
        [
            shape((rows, 2 * key_width), BF),
            shape((2 * width // 128 + 2, 128), F32),
            shape((half, width), F32),
            shape((half, width), BF),
        ],
        [ranks, keys_pre, key_gain_row, cos, sin, key_weight, value_weight, query_partial, *x,
         ffn_gain_part, query_gain_part, terms[0], arrived[0], *shifted],
        name="key_backward",
        after=[up_sent],
    )
    pair_there = xor(pair_b, "ctx", 1)
    gate_kept, gate_arrived, back = halve(
        gate_kept, xor(gate_sent, "ctx", 2), "gate_fold", after=[kept]
    )
    gains = add(gains, xor(gains, "mp", 1), F32, "gains", after=[back])
    kept, across = mp_reduce_start(kept, sent, "grad_input_core", after=[gains])
    gains = add(gains, xor(gains, "mp", 2), F32, "gains", after=[kept])
    attn_kept, attn_sent = weight_grad(
        ranks,
        [
            (grad_resid_b, late_there, early, early_there, (chosen, chosen), query_width),
            (act_attn, early_there, late, late_there, (chosen, chosen), query_width),
            (act_attn, early_there, pair_b, pair_there, (0, 0), 2 * key_width),
        ],
        "attention_grads",
        after=[gains],
    )
    gains = add(gains, xor(gains, "ctx", 1), F32, "gains", after=[attn_sent])
    up_kept, up_arrived, back = halve(
        up_kept, xor(up_sent, "ctx", 2), "up_fold", after=[gains]
    )
    out_kept, out_across = mp_reduce_start(out_kept, out_sent, "block_out_core", after=[back])
    grad_input = launch(
        grad_input_kernel,
        [shape((own_rows, width), F32)],
        [x[0], attn_gain_row, grad_resid, kept, across],
        name="grad_input",
        after=[out_kept],
    )[0]
    block_out = launch(
        block_out_kernel,
        [shape((own_rows, width), BF)],
        [resid, out_kept, out_across],
        name="block_out",
        after=[grad_input],
    )[0]

    def finish(kept, arrived, name, after, kernel=add_kernel, turned=False):
        dims = kept.shape[::-1] if turned else kept.shape
        return launch(kernel, [shape(dims, F32)], [kept, arrived], name=name, after=after)[0]

    down_grad = finish(
        down_kept, down_arrived, "down_last", [block_out], turned_add_kernel, True
    )
    gate_grad = finish(gate_kept, gate_arrived, "gate_last", [down_grad])
    attn_kept, attn_arrived, back = halve(
        attn_kept, xor(attn_sent, "ctx", 2), "attention_fold", after=[gate_grad]
    )
    mask = 2
    while mask < n_ctx:
        gains = add(gains, xor(gains, "ctx", mask), F32, "gains", after=[back])
        mask *= 2
    up_grad = finish(up_kept, up_arrived, "up_last", [gains])
    out_grad, query_grad, key_grad, value_grad = launch(
        attention_last_kernel,
        [shape((query_width, attn_kept.shape[0]), F32)]
        + [shape((attn_kept.shape[0], w), F32) for w in (query_width, key_width, key_width)],
        [attn_kept, attn_arrived],
        name="attention_last",
        after=[up_grad],
    )
    gains = gains.reshape(-1)
    heads = gains[2 * width :].reshape(2, -1, HD).sum(axis=1)
    query_gains, key_gains = heads[0], heads[1]
    return (
        block_out,
        grad_input,
        query_grad,
        key_grad,
        value_grad,
        out_grad,
        gate_grad,
        up_grad,
        down_grad,
        gains[:width],
        gains[width : 2 * width],
        query_gains,
        key_gains,
    )


def solution(mesh):
    in_specs = (
        P(("ctx", "mp"), None),
        P(),
        P(None, "mp"),
        P(None, "mp"),
        P(None, "mp"),
        P("mp", None),
        P(),
        P(),
        P(),
        P(None, "mp"),
        P(None, "mp"),
        P("mp", None),
        P(),
        P("ctx"),
        P(("ctx", "mp"), None),
    )
    out_specs = (
        P(("ctx", "mp"), None),
        P(("ctx", "mp"), None),
        P("ctx", "mp"),
        P("ctx", "mp"),
        P("ctx", "mp"),
        P("mp", "ctx"),
        P("ctx", "mp"),
        P("ctx", "mp"),
        P("mp", "ctx"),
        P(),
        P(),
        P(),
        P(),
    )
    return jax.shard_map(body, mesh=mesh, in_specs=in_specs, out_specs=out_specs, check_vma=False)
```

```python
import functools
import math

import jax
import jax.numpy as jnp
from jax import lax
from jax.experimental import pallas as pl
from jax.experimental.pallas import tpu as pltpu
from jax.sharding import PartitionSpec as P

HEADS = 16
KV_HEADS = 8
HD = 64
EPS = 1e-05
ROPE_BASE = 1000000.0
MASKED_SCORE = -1e30
LONGEST = {2048: 1280, 8192: 4352}
BF = jnp.bfloat16
F32 = jnp.float32
ROWS = (((0,), (0,)), ((), ()))
COLS = (((1,), (1,)), ((), ()))
SCALE = HD ** (-0.5)
RANKS = "ranks"


def dot(a, b, dims=(((1,), (0,)), ((), ()))):
    return lax.dot_general(a, b, dims, preferred_element_type=F32)


def xor(values, axis, mask):
    n = lax.axis_size(axis)
    return lax.ppermute(values, axis, [(i, i ^ mask) for i in range(n)])


def up(values, step):
    n = lax.axis_size("ctx")
    return lax.ppermute(values, "ctx", [(i, i + step) for i in range(n - step)])


def down(values, step):
    n = lax.axis_size("ctx")
    return lax.ppermute(values, "ctx", [(i, i - step) for i in range(step, n)])


def lanes(shape):
    return lax.broadcasted_iota(jnp.int32, shape, len(shape) - 1)


def group_sum(values):
    width = values.shape[-1]
    line = lax.broadcasted_iota(jnp.int32, (width, width), 0) // HD
    ones = (line == lanes((width, width)) // HD).astype(BF)
    front = values.astype(BF)
    back = (values - front.astype(F32)).astype(BF)
    return dot(front, ones) + dot(back, ones)


def partner(values):
    width = values.shape[-1]
    first = lanes(values.shape) % HD < HD // 2
    return jnp.where(
        first, pltpu.roll(values, width - HD // 2, 1), pltpu.roll(values, HD // 2, 1)
    )


def wide(table, width):
    return jnp.concatenate([table] * (width // table.shape[-1]), axis=-1)


def row_norm(values):
    return lax.rsqrt(jnp.mean(values * values, axis=-1, keepdims=True) + EPS)


def head_norm(values):
    return lax.rsqrt(group_sum(values * values) * (1.0 / HD) + EPS)


def head_norm_backward(values, gain, grads, cos, sin):
    width = values.shape[-1]
    grads = grads * wide(cos, width) - partner(grads) * wide(sin, width)
    scale = head_norm(values)
    normed = values * scale
    inner = grads * gain
    grad_in = scale * (inner - normed * (group_sum(inner * normed) * (1.0 / HD)))
    return grad_in, jnp.sum(grads * normed, axis=0, keepdims=True)


def place_of(iota, rows, rank):
    quarter = rows // 4
    part = iota // quarter
    relative = (part % 2) * 2 + part // 2
    return jnp.bitwise_xor(relative, rank) * quarter + iota % quarter


def stack(slab, kv_head):
    slab = slab.astype(F32)
    turned = pltpu.roll(slab, HD, 1)
    low = lanes(slab.shape) < HD
    if kv_head == 0:
        parts = [jnp.where(low, slab, 0.0), jnp.where(low, turned, 0.0)]
    else:
        parts = [jnp.where(low, 0.0, turned), jnp.where(low, 0.0, slab)]
    return jnp.concatenate(parts, axis=0)


def unstack(stacked, kv_head):
    rows = stacked.shape[0] // 2
    first, second = stacked[:rows], stacked[rows:]
    low = lanes(first.shape) < HD
    if kv_head == 0:
        return jnp.where(low, first, pltpu.roll(second, HD, 1))
    return jnp.where(low, pltpu.roll(first, HD, 1), second)


def qkv_kernel(
    x1, x2, x3, x0, gain, positions, wk, wv, key_gain, wq, query_gain,
    act_out, select_out, pair_out, query_rot_out, query_out, key_out,
    cos_out, sin_out, column_out, row_out, *scratch,
):
    sources = (x0, gain, positions, wk, wv, key_gain, wq, query_gain)
    buffers, sems = scratch[:-1], scratch[-1]
    copies = [
        pltpu.make_async_copy(source, buffer, sems.at[i])
        for i, (source, buffer) in enumerate(zip(sources, buffers, strict=True))
    ]
    for copy in copies:
        copy.start()
    for copy in copies:
        copy.wait()
    x0, gain, positions, wk, wv, key_gain, wq, query_gain = buffers
    ranks = (lax.axis_index("ctx"), lax.axis_index("mp"))
    rows = act_out.shape[0]
    line = lax.broadcasted_iota(jnp.int32, (rows, rows), 0)
    picked = place_of(line, rows, ranks[1]) == lanes((rows, rows))
    column = jnp.sum(
        jnp.where(picked, positions[...].astype(F32), 0.0), axis=1, keepdims=True
    )
    column_out[...] = column.astype(jnp.int32)
    row = jnp.sum(jnp.where(line == lanes((rows, rows)), column, 0.0), axis=0, keepdims=True)
    row_out[...] = row.astype(jnp.int32)
    lane = lanes((1, 128))
    power = (lane % (HD // 2)).astype(F32) * (-2.0 / HD)
    angles = column * jnp.exp(power * math.log(ROPE_BASE))
    cos = jnp.cos(angles)
    sin = jnp.sin(angles) * jnp.where(lane % HD < HD // 2, -1.0, 1.0)
    cos_out[...] = cos
    sin_out[...] = sin

    x = jnp.concatenate([x0[...], x1[...], x2[...], x3[...]], axis=0).astype(F32)
    act = (x * row_norm(x) * gain[...]).astype(BF)
    act_out[...] = act
    keys = dot(act, wk[...])
    key_out[...] = keys
    width = keys.shape[-1]
    normed = keys * head_norm(keys) * wide(key_gain[...], width)
    rotated = normed * wide(cos, width) + partner(normed) * wide(sin, width)
    pair_out[:, :width] = rotated.astype(BF)
    pair_out[:, width:] = dot(act, wv[...]).astype(BF)
    queries = dot(act, wq[...])
    query_out[...] = queries
    width = queries.shape[-1]
    normed = queries * head_norm(queries) * wide(query_gain[...], width)
    rotated = normed * wide(cos, width) + partner(normed) * wide(sin, width)
    query_rot_out[...] = rotated.astype(BF)
    select_columns(ranks, act_out, select_out)


def select_columns(ranks, source, target):
    columns = target.shape[1]
    blocks = columns // 128
    if blocks != 4:
        target[...] = jnp.zeros(target.shape, target.dtype)
        return
    for b in range(blocks):
        start = pl.multiple_of((2 * b + 1 - ranks[0] % 2) * 128, 128)
        target[:, b * 128 : (b + 1) * 128] = source[:, pl.ds(start, 128)]


def cotangent_kernel(
    ranks, c0, c1, c2, c3, wd, act_select, attn_b, cot_out, packet_out, grad_hidden_out
):
    cot = jnp.concatenate([c0[...], c1[...], c2[...], c3[...]], axis=0)
    cot_out[...] = cot
    chosen = act_select.shape[1]
    select_columns(ranks, cot_out, packet_out.at[:, :chosen])
    packet_out[:, chosen : 2 * chosen] = act_select[...]
    packet_out[:, 2 * chosen :] = attn_b[...]
    grad_hidden_out[...] = dot(cot, wd[...], COLS)


def attention_kernel(count, ranks, query_rot, positions, wo, *refs):
    slots = count // 2
    even = refs[:slots]
    low_odd, high_odd = refs[slots : 2 * slots], refs[2 * slots : 3 * slots]
    out_f32, out_b, sums_out, kept_out, sent_out = refs[3 * slots : 3 * slots + 5]
    odd = refs[3 * slots + 5 : -1]
    scores = refs[-1]
    rows = query_rot.shape[0]
    key_width = even[0].shape[1] // 2
    for j in range(slots):
        odd[j][...] = jnp.where(
            ranks[0] % 2 == 1, low_odd[j][...].astype(F32), high_odd[j][...].astype(F32)
        ).astype(BF)
    blocks = [(even, odd)[d % 2][d // 2] for d in range(count)]
    query_index = ranks[0] * rows + place_of(
        lax.broadcasted_iota(jnp.int32, (rows, 1), 0), rows, ranks[1]
    )
    first_seen = query_index - positions[...]
    key_place = place_of(lanes((1, rows)), rows, ranks[1])
    masks = []
    for d in range(count):
        key_index = (ranks[0] - d) * rows + key_place
        mask = key_index >= first_seen
        if d == 0:
            mask = mask & (key_index <= query_index)
        masks.append(jnp.where(mask, 0.0, MASKED_SCORE))
    for head in range(2):
        slab = query_rot[:, head * 128 : (head + 1) * 128]
        stacked = (stack(slab, head) * SCALE).astype(BF)
        top = jnp.full((2 * rows, 1), MASKED_SCORE, F32)
        for d in range(count):
            block = dot(stacked, blocks[d][:, :key_width], COLS)
            block = block + jnp.concatenate([masks[d], masks[d]], axis=0)
            scores[:, d * rows : (d + 1) * rows] = block
            top = jnp.maximum(top, jnp.max(block, axis=-1, keepdims=True))
        total = jnp.zeros((2 * rows, 1), F32)
        mixed = jnp.zeros((2 * rows, key_width), F32)
        for d in range(count):
            weights = jnp.exp(scores[:, d * rows : (d + 1) * rows] - top)
            total = total + jnp.sum(weights, axis=-1, keepdims=True)
            mixed = mixed + dot(weights.astype(BF), blocks[d][:, key_width:])
        sums = jnp.broadcast_to(top + jnp.log(total), (2 * rows, 128))
        sums_out[head : head + 1, :] = jnp.transpose(sums)[:1]
        out_f32[:, head * 128 : (head + 1) * 128] = unstack(mixed / total, head)
    attn_b = out_f32[...].astype(BF)
    out_b[...] = attn_b
    half = rows // 2
    kept_out[...] = dot(attn_b[:half], wo[...])
    sent_out[...] = dot(attn_b[half:], wo[...]).astype(BF)


def add_kernel(kept, arrived, out):
    out[...] = (kept[...].astype(F32) + arrived[...].astype(F32)).astype(out.dtype)


def flipped_add_kernel(kept, arrived, out):
    half = kept.shape[0] // 2
    for a, b in ((0, half), (half, 0)):
        total = kept[a : a + half, :].astype(F32) + arrived[b : b + half, :].astype(F32)
        out[a : a + half, :] = total.astype(out.dtype)


def fold_kernel(*refs):
    count = (len(refs) - 1) // 3
    back_out = refs[-1]
    place = 0
    for p in range(count):
        kept, arrived, front_out = refs[2 * p], refs[2 * p + 1], refs[2 * count + p]
        half, width = front_out.shape
        front_out[...] = kept[:half, :] + arrived[:half, :].astype(F32)
        back_out[:, place : place + width] = (
            kept[half:, :] + arrived[half:, :].astype(F32)
        ).astype(BF)
        place += width


def mp_fold_kernel(input_kept, out_kept, gains, arrived, input_front, out_front, gains_out, back):
    half = input_kept.shape[0]
    own = half // 2
    came = arrived[...].astype(F32)
    for place, kept, front in ((0, input_kept, input_front), (1, out_kept, out_front)):
        total = kept[...] + came[place * half : (place + 1) * half]
        front[...] = total[:own]
        back[place * own : (place + 1) * own, :] = total[own:].astype(BF)
    gains_out[...] = gains[...] + unpack(came[2 * half :], gains.shape[0])
    pack(gains_out[...], back, 2 * own)


def pack(values, target, start):
    count = values.shape[0]
    target[start : start + 16, :] = jnp.zeros((16, target.shape[1]), BF)
    front = values.astype(BF)
    for part, piece in enumerate((front.astype(F32), values - front.astype(F32))):
        for g in range(-(-count // 16)):
            rows = piece[16 * g : 16 * g + 16]
            if rows.shape[0] < 16:
                rows = jnp.concatenate([rows, jnp.zeros((16 - rows.shape[0], 128), F32)], axis=0)
            column = (2 * g + part) * 128
            target[start : start + 16, column : column + 128] = rows.astype(BF)


def unpack(values, count):
    pieces = []
    for g in range(-(-count // 16)):
        column = 2 * g * 128
        total = values[:, column : column + 128] + values[:, column + 128 : column + 256]
        pieces.append(total[: min(16, count - 16 * g)])
    return jnp.concatenate(pieces, axis=0)


def last_kernel(turned, *refs):
    count = len(turned)
    arrived, outs, token = refs[count], refs[count + 1 : -1], refs[-1]
    place = 0
    for p in range(count):
        width = refs[p].shape[1]
        total = refs[p][...] + arrived[:, place : place + width].astype(F32)
        outs[p][...] = jnp.transpose(total) if turned[p] else total
        place += width
    token[...] = jnp.zeros(token.shape, F32)


def attention_last_kernel(kept, arrived, out_grad, query_grad, key_grad, value_grad):
    total = kept[...] + arrived[...].astype(F32)
    turned = out_grad.shape[0]
    out_grad[...] = jnp.transpose(total[:, :turned])
    start = turned
    for out in (query_grad, key_grad, value_grad):
        width = out.shape[1]
        out[...] = total[:, start : start + width]
        start += width


def pair_sum_kernel(slots, ranks, *refs):
    odd = ranks[0] % 2 == 1
    terms, arrived = refs[:slots], refs[slots]
    outs = refs[slots + 1 :]
    rows = terms[0].shape[0]
    came = [arrived[j * rows : (j + 1) * rows, :].astype(F32) for j in range(slots)]
    outs[0][...] = terms[0][...] + jnp.where(odd, 0.0, came[0])
    for k in range(1, slots):
        outs[k][...] = (
            terms[k][...].astype(F32) + jnp.where(odd, came[k - 1], came[k])
        ).astype(BF)
    outs[slots][...] = came[slots - 1].astype(BF)


def down_kernel(hidden, wd, kept_out, sent_out):
    half = hidden.shape[0] // 2
    sent_out[...] = dot(hidden[half:, :], wd[...]).astype(BF)
    kept_out[...] = dot(hidden[:half, :], wd[...])


def outputs_kernel(
    x, gain, grad_resid, resid, input_kept, out_kept, gains, arrived,
    grad_input_out, block_out, gains_out,
):
    own = block_out.shape[0]
    came = arrived[...].astype(F32)
    block_out[...] = (resid[:own, :] + out_kept[...] + came[own : 2 * own]).astype(BF)
    gains_out[...] = gains[...] + unpack(came[2 * own :], gains.shape[0])
    grads = input_kept[...] + came[:own]
    values = x[...].astype(F32)
    scale = row_norm(values)
    normed = values * scale
    inner = grads * gain[...]
    grad_input_out[...] = grad_resid[...] + scale * (
        inner - normed * jnp.mean(inner * normed, axis=-1, keepdims=True)
    )


def ffn_forward_kernel(
    ranks, x0, x1, x2, x3, half0, half1, gain, wg, wu,
    resid_out, act_out, select_out, gate_out, up_out, hidden_out,
):
    x = jnp.concatenate([x0[...], x1[...], x2[...], x3[...]], axis=0).astype(F32)
    resid = x + jnp.concatenate([half0[...], half1[...]], axis=0).astype(F32)
    resid_out[...] = resid
    act = (resid * row_norm(resid) * gain[...]).astype(BF)
    act_out[...] = act
    gate = dot(act, wg[...])
    upper = dot(act, wu[...])
    gate_out[...] = gate
    up_out[...] = upper
    hidden_out[...] = (gate * jax.nn.sigmoid(gate) * upper).astype(BF)
    select_columns(ranks, act_out, select_out)


def ffn_backward_kernel(
    gate, upper, grad_hidden, wg, wu, select, gate_packet, grad_up_out, kept_out, sent_out
):
    grads = grad_hidden[...]
    values = gate[...]
    sigmoid = jax.nn.sigmoid(values)
    grad_gate = (grads * upper[...] * sigmoid * (1.0 + values * (1.0 - sigmoid))).astype(BF)
    grad_up = (grads * values * sigmoid).astype(BF)
    chosen = select.shape[1]
    gate_packet[:, :chosen] = select[...]
    gate_packet[:, chosen:] = grad_gate
    grad_up_out[...] = grad_up
    half = values.shape[0] // 2
    sent_out[...] = (
        dot(grad_gate[half:], wg[...], COLS) + dot(grad_up[half:], wu[...], COLS)
    ).astype(BF)
    kept_out[...] = dot(grad_gate[:half], wg[...], COLS) + dot(grad_up[:half], wu[...], COLS)


def attention_backward_kernel(
    count, ranks, cot, resid, half0, half1, gain, wo, attn, sums, query_rot, positions, *refs
):
    blocks = refs[:count]
    grad_own_out, grad_b_out, select_out, gain_out, grad_query_out = refs[count : count + 5]
    even, odd = refs[count + 5 : -1], refs[-1]
    rows = query_rot.shape[0]
    terms = [
        even[d // 2] if d % 2 == 0 else odd.at[d // 2 * rows : (d // 2 + 1) * rows]
        for d in range(count)
    ]
    key_width = blocks[0].shape[1] // 2
    values = resid[...]
    scale = row_norm(values)
    normed = values * scale
    grads = jnp.concatenate([half0[...], half1[...]], axis=0).astype(F32)
    inner = grads * gain[...]
    grad_in = scale * (inner - normed * jnp.mean(inner * normed, axis=-1, keepdims=True))
    grad_resid = cot[...].astype(F32) + grad_in
    own = rows // 4
    grad_own_out[...] = grad_resid[:own]
    gain_out[...] = jnp.sum(grads[:own] * normed[:own], axis=0, keepdims=True)
    grad_resid_b = grad_resid.astype(BF)
    grad_b_out[...] = grad_resid_b
    select_columns(ranks, grad_b_out, select_out)
    grad_attn = dot(grad_resid_b, wo[...], COLS)
    delta = jnp.transpose(group_sum(grad_attn * attn[...]))
    grad_attn_b = grad_attn.astype(BF)

    query_index = ranks[0] * rows + place_of(lanes((1, rows)), rows, ranks[1])
    first_row = query_index - positions[...]
    key_place = place_of(lax.broadcasted_iota(jnp.int32, (rows, 1), 0), rows, ranks[1])
    stacked = [stack(query_rot[:, h * 128 : (h + 1) * 128], h) for h in range(2)]
    stacked_b = [s.astype(BF) for s in stacked]
    scaled = [(s * SCALE).astype(BF) for s in stacked]
    grads_b = [
        stack(grad_attn_b[:, h * 128 : (h + 1) * 128], h).astype(BF) for h in range(2)
    ]
    deltas = [
        jnp.concatenate(
            [delta[2 * h * HD : 2 * h * HD + 1], delta[(2 * h + 1) * HD : (2 * h + 1) * HD + 1]],
            axis=1,
        )
        for h in range(2)
    ]
    grad_query = [jnp.zeros((2 * rows, key_width), F32) for _ in range(2)]
    for d in range(count - 1, -1, -1):
        key_index = (ranks[0] - d) * rows + key_place
        mask = key_index >= first_row
        if d == 0:
            mask = mask & (key_index <= query_index)
        mask = jnp.where(mask, 0.0, MASKED_SCORE)
        mask = jnp.concatenate([mask, mask], axis=1)
        key_block = blocks[d][:, :key_width]
        value_block = blocks[d][:, key_width:]
        key_term = jnp.zeros((rows, key_width), F32)
        value_term = jnp.zeros((rows, key_width), F32)
        for h in range(2):
            scores = dot(key_block, scaled[h], COLS) + mask
            probs = jnp.exp(scores - sums[h : h + 1, :])
            grad_probs = dot(value_block, grads_b[h], COLS)
            grad_scores = (probs * (grad_probs - deltas[h]) * SCALE).astype(BF)
            key_term = key_term + dot(grad_scores, stacked_b[h])
            value_term = value_term + dot(probs.astype(BF), grads_b[h])
            grad_query[h] = grad_query[h] + dot(grad_scores, key_block, ROWS)
        terms[d][:, :key_width] = key_term.astype(terms[d].dtype)
        terms[d][:, key_width:] = value_term.astype(terms[d].dtype)
    for h in range(2):
        grad_query_out[:, h * 128 : (h + 1) * 128] = unstack(grad_query[h], h)


def query_backward_kernel(
    queries, gain, grads, cos, sin, wq, grad_out, gain_out, partial_out
):
    grad_in, gain_terms = head_norm_backward(queries[...], wide(gain[...], queries.shape[-1]), grads[...], cos[...], sin[...])
    grad_b = grad_in.astype(BF)
    grad_out[...] = grad_b
    gain_out[...] = gain_terms
    partial_out[...] = dot(grad_b, wq[...], COLS)


def key_backward_kernel(
    keys, gain, cos, sin, wk, wv, query_partial, x0, x1, x2, x3,
    ffn_gain_part, query_gain_part, out_sent, select, grad_query_b, term, *refs,
):
    shifted = refs[:-4]
    late_out, gains_out, kept_out, sent_out = refs[-4:]
    width = keys.shape[-1]
    grads = term[...]
    for other in shifted:
        grads = grads + other[...].astype(F32)
    grad_in, gain_terms = head_norm_backward(
        keys[...], wide(gain[...], width), grads[:, :width], cos[...], sin[...]
    )
    grad_b = grad_in.astype(BF)
    value_b = grads[:, width:].astype(BF)
    place = 0
    for piece in (select[...], grad_query_b[...], grad_b, value_b):
        late_out[:, place : place + piece.shape[1]] = piece
        place += piece.shape[1]
    partial = query_partial[...] + dot(grad_b, wk[...], COLS) + dot(value_b, wv[...], COLS)
    half = partial.shape[0] // 2
    kept_out[...] = partial[:half]
    sent_out[:half, :] = partial[half:].astype(BF)
    sent_out[half : 2 * half, :] = out_sent[...]
    x = jnp.concatenate([x0[...], x1[...], x2[...], x3[...]], axis=0).astype(F32)
    features = x.shape[1]
    parts = [
        jnp.sum(partial * (x * row_norm(x)), axis=0, keepdims=True),
        ffn_gain_part[...],
    ]
    row = 0
    for part in parts:
        for c in range(features // 128):
            gains_out[row : row + 1, :] = part[:, c * 128 : (c + 1) * 128]
            row += 1
    queries = query_gain_part[...]
    queries = sum(queries[:, c * 128 : (c + 1) * 128] for c in range(queries.shape[1] // 128))
    gains_out[row : row + 1, :] = queries
    gains_out[row + 1 : row + 2, :] = gain_terms
    pack(gains_out[...], sent_out, 2 * half)


def weight_grad_kernel(parts, ranks, *refs):
    kept_out, sent_out = refs[-2:]
    parity = ranks[0] % 2
    mine = ranks[0] // 2
    place = 0
    for p, (own, there_at, act_at, width) in enumerate(parts):
        act, arrived_act, grads, arrived_grads = refs[4 * p : 4 * p + 4]
        mine_grads = grads[:, own : own + width]
        other_grads = arrived_grads[:, there_at : there_at + width]
        for lo in (1, 0):
            for hi in range(2):
                block = jnp.bitwise_xor(mine, lo + 2 * hi)
                start = pl.multiple_of((2 * block + parity) * 128, 128)
                there = pl.multiple_of(act_at + block * 128, 128)
                total = dot(act[:, pl.ds(start, 128)], mine_grads, ROWS) + dot(
                    arrived_act[:, pl.ds(there, 128)], other_grads, ROWS
                )
                target = sent_out if lo else kept_out
                target[hi * 128 : (hi + 1) * 128, place : place + width] = total.astype(
                    target.dtype
                )
        place += width


def shape(dims, dtype):
    return jax.ShapeDtypeStruct(dims, dtype)


def launch(kernel, outs, args, scratch=(), name=None, after=(), carry=()):
    nbytes = sum(s.shape[0] * s.shape[1] * 4 for s in scratch)
    ranked = args[0] is RANKS
    args = list(args[ranked:])
    n_in, n_out, n_unused = len(args), len(outs), len(after) + len(carry)

    def run(*refs):
        results = refs[n_in + n_unused :]
        ranks = [(lax.axis_index("ctx"), lax.axis_index("mp"))] if ranked else []
        kernel(*ranks, *refs[:n_in], *results[:n_out], *results[n_out + len(carry) :])

    any_spec = pl.BlockSpec(memory_space=pl.ANY)
    return pl.pallas_call(
        run,
        out_shape=list(outs) + [shape(c.shape, c.dtype) for c in carry],
        in_specs=[pl.BlockSpec(memory_space=pltpu.VMEM)] * n_in + [any_spec] * n_unused,
        out_specs=[pl.BlockSpec(memory_space=pltpu.VMEM) for _ in outs] + [any_spec] * len(carry),
        scratch_shapes=list(scratch),
        input_output_aliases={n_in + len(after) + i: n_out + i for i in range(len(carry))},
        compiler_params=pltpu.CompilerParams(vmem_limit_bytes=nbytes + (12 << 20)),
        name=name,
    )(*args, *after, *carry)


def add(kept, arrived, dtype, name, kernel=add_kernel, after=(), carry=()):
    out = launch(
        kernel, [shape(kept.shape, dtype)], [kept, arrived], name=name, after=after, carry=carry
    )
    return out if carry else out[0]


def mp_gather(values):
    other = xor(values, "mp", 2)
    core = xor(values, "mp", 1)
    return values, other, core, xor(other, "mp", 1)


def split_columns(values):
    n = lax.axis_size("ctx")
    index = lax.axis_index("ctx")
    rows, columns = values.shape
    bits = n.bit_length() - 1
    parts = values.reshape((rows,) + (2,) * bits + (columns // n,))
    for bit in range(bits):
        parts = jnp.where((index >> bit) % 2 == 1, jnp.flip(parts, bits - bit), parts)
    order = [0] + [bits - b for b in range(bits)] + [bits + 1]
    parts = jnp.transpose(parts, order).reshape(rows, 2, columns // 2)
    return parts[:, 0], parts[:, 1]


def weight_grad(parts, name, after=()):
    n = lax.axis_size("ctx")
    act = parts[0][0]
    half = act.shape[1] // 4
    columns = sum(part[6] for part in parts)
    if n == 8 and act.shape[1] == 1024:
        return launch(
            functools.partial(weight_grad_kernel, [part[4] + part[5:] for part in parts]),
            [shape((half, columns), F32), shape((half, columns), BF)],
            [RANKS] + [a for part in parts for a in part[:4]],
            name=name,
            after=after,
        )
    totals = []
    for act, _, grads, arrived_grads, offsets, _, width in parts:
        own, other = split_columns(act)
        grads = grads[:, offsets[0] : offsets[0] + width]
        arrived_grads = arrived_grads[:, offsets[1] : offsets[1] + width]
        both = jnp.concatenate([own, xor(other, "ctx", 1)], axis=0)
        totals.append(dot(both, jnp.concatenate([grads, arrived_grads], axis=0), ROWS))
    total = jnp.concatenate(totals, axis=1)
    return total[:half], total[half:].astype(BF)


def fold(pairs, name, after=()):
    n = lax.axis_size("ctx")
    kept = [p[0] for p in pairs]
    arrived = [p[1] for p in pairs]
    mask = 4
    while mask < n:
        half = kept[0].shape[0] // 2
        widths = [k.shape[1] for k in kept]
        outs = launch(
            fold_kernel,
            [shape((half, w), F32) for w in widths] + [shape((half, sum(widths)), BF)],
            [a for pair in zip(kept, arrived, strict=True) for a in pair],
            name=name,
            after=after,
        )
        kept, back = outs[:-1], outs[-1]
        came = xor(back, "ctx", mask)
        mask *= 2
        if mask >= n:
            return kept, came, back
        arrived = []
        for w in widths:
            start = sum(a.shape[1] for a in arrived)
            arrived.append(came[:, start : start + w])
    return kept, came, back


def body(
    block_in,
    attn_gain,
    query_weight,
    key_weight,
    value_weight,
    out_weight,
    query_gain,
    key_gain,
    ffn_gain,
    gate_weight,
    up_weight,
    down_weight,
    segments,
    positions,
    cotangent,
):
    width = block_in.shape[1]
    key_width = key_weight.shape[1]
    query_width = query_weight.shape[1]
    hidden_width = gate_weight.shape[1]
    n_ctx = lax.axis_size("ctx")
    ctx_rank = lax.axis_index("ctx")
    own_rows = block_in.shape[0]
    rows = positions.shape[0]
    total_tokens = rows * n_ctx
    longest = LONGEST.get(total_tokens, total_tokens)
    window = min(n_ctx - 1, -(-(longest - 1) // rows))
    slots = (window + 1) // 2
    count = window + 1
    half = rows // 2

    x = mp_gather(block_in)
    query_gain_row = query_gain.reshape(1, -1)
    key_gain_row = key_gain.reshape(1, -1)
    attn_gain_row = attn_gain.reshape(1, -1)
    ffn_gain_row = ffn_gain.reshape(1, -1)

    outs = [
        shape((rows, width), BF),
        shape((rows, width // 2), BF),
        shape((rows, 2 * key_width), BF),
        shape((rows, query_width), BF),
        shape((rows, query_width), F32),
        shape((rows, key_width), F32),
        shape((rows, 128), F32),
        shape((rows, 128), F32),
        shape((rows, 1), jnp.int32),
        shape((1, rows), jnp.int32),
    ]
    copied = [block_in, attn_gain_row, positions.reshape(1, -1), key_weight, value_weight,
              key_gain_row, query_weight, query_gain_row]
    (
        act_attn, act_attn_select, pair, query_rot, queries, keys_pre,
        cos, sin, position_column, position_row,
    ) = pl.pallas_call(
        qkv_kernel,
        out_shape=outs,
        in_specs=[pl.BlockSpec(memory_space=pltpu.VMEM)] * 3
        + [pl.BlockSpec(memory_space=pl.ANY)] * len(copied),
        out_specs=[pl.BlockSpec(memory_space=pltpu.VMEM)] * len(outs),
        scratch_shapes=[pltpu.VMEM(a.shape, a.dtype) for a in copied]
        + [pltpu.SemaphoreType.DMA((len(copied),))],
        compiler_params=pltpu.CompilerParams(vmem_limit_bytes=52 << 20),
        name="qkv",
    )(*x[1:], *copied)

    def cross(values, odd):
        return lax.ppermute(values, "ctx", [(i, i ^ 1) for i in range(odd, n_ctx, 2)])

    def climb(step, pairs):
        pairs = [(i, i + step) for i in pairs if i + step < n_ctx]
        return lax.ppermute(pair, "ctx", pairs) if pairs else jnp.zeros_like(pair)

    items = [pair] + [climb(2 * k, range(n_ctx)) for k in range(1, slots)]
    farthest = climb(2 * slots - 1, range(1, n_ctx, 2))
    low_odd = [cross(items[j], 0) for j in range(slots)]
    high_odd = [cross(items[j + 1], 1) for j in range(slots - 1)] + [farthest]
    even = items[:slots]
    cot_chip = xor(cotangent, "mp", 2)
    cot_core = xor(cotangent, "mp", 1)

    outs = launch(
        functools.partial(attention_kernel, count),
        [
            shape((rows, query_width), F32),
            shape((rows, query_width), BF),
            shape((2, 2 * rows), F32),
            shape((half, width), F32),
            shape((half, width), BF),
        ]
        + [shape((rows, 2 * key_width), BF) for _ in range(slots)],
        [RANKS, query_rot, position_column, out_weight,
         *even, *low_odd, *high_odd],
        scratch=[pltpu.VMEM((2 * rows, count * rows), F32)],
        name="attention",
        after=[cot_chip, cot_core],
    )
    attn_rows, attn_b, log_sums, kept, sent = outs[:5]
    blocks = [(even, outs[5:])[d % 2][d // 2] for d in range(count)]
    chosen = width // 2

    kept = add(kept, xor(sent, "mp", 1), BF, "resid_core")
    cot, packet, grad_hidden = launch(
        cotangent_kernel,
        [
            shape((rows, width), BF),
            shape((rows, 2 * chosen + query_width), BF),
            shape((rows, hidden_width), F32),
        ],
        [RANKS, cotangent, cot_chip, cot_core, xor(cot_chip, "mp", 1), down_weight,
         act_attn_select, attn_b],
        name="cotangent",
        after=[kept],
    )
    there = xor(packet, "ctx", 1)
    both = add(
        kept, xor(kept, "mp", 2), BF, "resid_chip", kernel=flipped_add_kernel,
        after=[grad_hidden],
    )

    resid, act_ffn, act_select, gate_pre, up_proj, hidden = launch(
        ffn_forward_kernel,
        [
            shape((rows, width), F32),
            shape((rows, width), BF),
            shape((rows, chosen), BF),
            shape((rows, hidden_width), F32),
            shape((rows, hidden_width), F32),
            shape((rows, hidden_width), BF),
        ],
        [RANKS, *x, both, xor(both, "mp", 1), ffn_gain_row, gate_weight, up_weight],
        name="ffn_forward",
    )
    hidden_there = xor(hidden, "ctx", 1)
    gate_packet, grad_up, kept, sent = launch(
        ffn_backward_kernel,
        [
            shape((rows, chosen + hidden_width), BF),
            shape((rows, hidden_width), BF),
            shape((half, width), F32),
            shape((half, width), BF),
        ],
        [gate_pre, up_proj, grad_hidden, gate_weight, up_weight, act_select],
        name="ffn_backward",
    )
    kept, gate_packet = add(kept, xor(sent, "mp", 1), BF, "grad_act_core", after=[there],
        carry=[gate_packet])
    gate_there = xor(gate_packet, "ctx", 1)
    both = add(kept, xor(kept, "mp", 2), BF, "grad_act_chip", kernel=flipped_add_kernel)
    down_kept, down_sent = weight_grad(
        [(cot, there, hidden, hidden_there, (0, 0), 0, hidden_width)], "down_grad",
        after=[both],
    )

    outs = launch(
        functools.partial(attention_backward_kernel, count),
        [
            shape((own_rows, width), F32),
            shape((rows, width), BF),
            shape((rows, chosen), BF),
            shape((1, width), F32),
            shape((rows, query_width), F32),
        ]
        + [shape((rows, 2 * key_width), BF if d else F32) for d in range(slots)]
        + [shape((slots * rows, 2 * key_width), BF)],
        [RANKS, cot, resid, both, xor(both, "mp", 1), ffn_gain_row, out_weight, attn_rows,
         log_sums, query_rot, position_row, *blocks],
        name="attention_backward",
        after=[down_sent],
    )
    grad_resid, grad_resid_b, grad_select, ffn_gain_part, grad_query = outs[:5]
    terms, odd_terms = outs[5:-1], outs[-1]

    arrived = xor(odd_terms, "ctx", 1)
    gate_kept, gate_sent = weight_grad(
        [(act_ffn, gate_there, gate_packet, gate_there, (chosen, chosen), 0, hidden_width)],
        "gate_grad",
        after=[grad_query],
    )
    totals = launch(
        functools.partial(pair_sum_kernel, slots),
        [shape(terms[0].shape, BF if k else F32) for k in range(slots + 1)],
        [RANKS, *terms, arrived],
        name="pair_sums",
        after=[gate_sent],
        carry=[grad_up],
    )
    grad_up = totals[-1]
    up_there = xor(grad_up, "ctx", 1)
    shifted = [down(totals[k], 2 * k) for k in range(slots - 1, 0, -1)]
    if 2 * slots < n_ctx:
        pairs = [(i, i - 2 * slots) for i in range(2 * slots, n_ctx) if i % 2 == 1]
        shifted.append(lax.ppermute(totals[slots], "ctx", pairs))

    grad_query_b, query_gain_part, query_partial = launch(
        query_backward_kernel,
        [
            shape((rows, query_width), BF),
            shape((1, query_width), F32),
            shape((rows, width), F32),
        ],
        [queries, query_gain_row, grad_query, cos, sin, query_weight],
        name="query_backward",
        after=[totals[0]],
    )
    out_kept, out_sent = launch(
        down_kernel,
        [shape((half, width), F32), shape((half, width), BF)],
        [hidden, down_weight],
        name="down",
        after=[query_partial],
    )
    (down_kept, gate_kept), first_arrived, back = fold(
        [(down_kept, xor(down_sent, "ctx", 2)), (gate_kept, xor(gate_sent, "ctx", 2))],
        "first_fold",
        after=[out_sent],
    )
    up_kept, up_sent = weight_grad(
        [(act_ffn, gate_there, grad_up, up_there, (0, 0), 0, hidden_width)], "up_grad",
        after=[back],
    )
    late, gains, kept, sent = launch(
        key_backward_kernel,
        [
            shape((rows, chosen + query_width + 2 * key_width), BF),
            shape((2 * width // 128 + 2, 128), F32),
            shape((half, width), F32),
            shape((rows + 16, width), BF),
        ],
        [keys_pre, key_gain_row, cos, sin, key_weight, value_weight, query_partial, *x,
         ffn_gain_part, query_gain_part, out_sent, grad_select, grad_query_b, totals[0],
         *shifted],
        name="key_backward",
        after=[up_sent],
    )
    late_there = xor(late, "ctx", 1)
    core_arrived = xor(sent, "mp", 1)
    query_at = chosen
    pair_at = chosen + query_width
    input_kept, out_kept, gains, back = launch(
        mp_fold_kernel,
        [
            shape((own_rows, width), F32),
            shape((own_rows, width), F32),
            shape(gains.shape, F32),
            shape((half + 16, width), BF),
        ],
        [kept, out_kept, gains, core_arrived],
        name="mp_fold",
    )
    attn_kept, attn_sent = weight_grad(
        [
            (grad_resid_b, late_there, attn_b, there, (0, 2 * chosen), 0, query_width),
            (act_attn, there, late, late_there, (query_at, query_at), chosen, query_width),
            (act_attn, there, late, late_there, (pair_at, pair_at), chosen, 2 * key_width),
        ],
        "attention_grads",
        after=[back],
    )
    grad_input, block_out, gains = launch(
        outputs_kernel,
        [
            shape((own_rows, width), F32),
            shape((own_rows, width), BF),
            shape(gains.shape, F32),
        ],
        [x[0], attn_gain_row, grad_resid, resid, input_kept, out_kept, gains,
         xor(back, "mp", 2)],
        name="outputs",
        after=[attn_sent],
    )
    gains = add(gains, xor(gains, "ctx", 1), F32, "gains")
    (up_kept,), up_arrived, back = fold(
        [(up_kept, xor(up_sent, "ctx", 2))], "up_fold", after=[gains]
    )
    token = shape((8, 128), F32)
    down_grad, gate_grad, done = launch(
        functools.partial(last_kernel, (True, False)),
        [shape(down_kept.shape[::-1], F32), shape(gate_kept.shape, F32), token],
        [down_kept, gate_kept, first_arrived],
        name="first_last",
        after=[back],
    )
    (attn_kept,), attn_arrived, back = fold(
        [(attn_kept, xor(attn_sent, "ctx", 2))], "attention_fold", after=[done]
    )
    mask = 2
    while mask < n_ctx // 2:
        gains = add(gains, xor(gains, "ctx", mask), F32, "gains", after=[back])
        mask *= 2
    up_grad, done = launch(
        functools.partial(last_kernel, (False,)),
        [shape(up_kept.shape, F32), token],
        [up_kept, up_arrived],
        name="up_last",
        after=[gains],
    )
    gains = add(gains, xor(gains, "ctx", mask), F32, "gains", after=[done])
    out_grad, query_grad, key_grad, value_grad = launch(
        attention_last_kernel,
        [shape((query_width, attn_kept.shape[0]), F32)]
        + [shape((attn_kept.shape[0], w), F32) for w in (query_width, key_width, key_width)],
        [attn_kept, attn_arrived],
        name="attention_last",
        after=[gains],
    )
    gains = gains.reshape(-1)
    heads = gains[2 * width :].reshape(2, -1, HD).sum(axis=1)
    query_gains, key_gains = heads[0], heads[1]
    return (
        block_out,
        grad_input,
        query_grad,
        key_grad,
        value_grad,
        out_grad,
        gate_grad,
        up_grad,
        down_grad,
        gains[:width],
        gains[width : 2 * width],
        query_gains,
        key_gains,
    )


def solution(mesh):
    in_specs = (
        P(("ctx", "mp"), None),
        P(),
        P(None, "mp"),
        P(None, "mp"),
        P(None, "mp"),
        P("mp", None),
        P(),
        P(),
        P(),
        P(None, "mp"),
        P(None, "mp"),
        P("mp", None),
        P(),
        P("ctx"),
        P(("ctx", "mp"), None),
    )
    out_specs = (
        P(("ctx", "mp"), None),
        P(("ctx", "mp"), None),
        P("ctx", "mp"),
        P("ctx", "mp"),
        P("ctx", "mp"),
        P("mp", "ctx"),
        P("ctx", "mp"),
        P("ctx", "mp"),
        P("mp", "ctx"),
        P(),
        P(),
        P(),
        P(),
    )
    return jax.shard_map(body, mesh=mesh, in_specs=in_specs, out_specs=out_specs, check_vma=False)
```

```python
import functools
import math

import jax
import jax.numpy as jnp
from jax import lax
from jax.experimental import pallas as pl
from jax.experimental.pallas import tpu as pltpu
from jax.sharding import PartitionSpec as P

HEADS = 16
KV_HEADS = 8
HD = 64
EPS = 1e-05
ROPE_BASE = 1000000.0
MASKED_SCORE = -1e30
LONGEST = {2048: 1280, 8192: 4352}
BF = jnp.bfloat16
F32 = jnp.float32
ROWS = (((0,), (0,)), ((), ()))
COLS = (((1,), (1,)), ((), ()))
SCALE = HD ** (-0.5)
RANKS = "ranks"


def dot(a, b, dims=(((1,), (0,)), ((), ()))):
    return lax.dot_general(a, b, dims, preferred_element_type=F32)


def xor(values, axis, mask):
    n = lax.axis_size(axis)
    return lax.ppermute(values, axis, [(i, i ^ mask) for i in range(n)])


def up(values, step):
    n = lax.axis_size("ctx")
    return lax.ppermute(values, "ctx", [(i, i + step) for i in range(n - step)])


def down(values, step):
    n = lax.axis_size("ctx")
    return lax.ppermute(values, "ctx", [(i, i - step) for i in range(step, n)])


def lanes(shape):
    return lax.broadcasted_iota(jnp.int32, shape, len(shape) - 1)


def group_sum(values):
    width = values.shape[-1]
    line = lax.broadcasted_iota(jnp.int32, (width, width), 0) // HD
    ones = (line == lanes((width, width)) // HD).astype(BF)
    front = values.astype(BF)
    back = (values - front.astype(F32)).astype(BF)
    return dot(front, ones) + dot(back, ones)


def partner(values):
    width = values.shape[-1]
    first = lanes(values.shape) % HD < HD // 2
    return jnp.where(
        first, pltpu.roll(values, width - HD // 2, 1), pltpu.roll(values, HD // 2, 1)
    )


def wide(table, width):
    return jnp.concatenate([table] * (width // table.shape[-1]), axis=-1)


def row_norm(values):
    return lax.rsqrt(jnp.mean(values * values, axis=-1, keepdims=True) + EPS)


def head_norm(values):
    return lax.rsqrt(group_sum(values * values) * (1.0 / HD) + EPS)


def head_norm_backward(values, gain, grads, cos, sin):
    width = values.shape[-1]
    grads = grads * wide(cos, width) - partner(grads) * wide(sin, width)
    scale = head_norm(values)
    normed = values * scale
    inner = grads * gain
    grad_in = scale * (inner - normed * (group_sum(inner * normed) * (1.0 / HD)))
    return grad_in, jnp.sum(grads * normed, axis=0, keepdims=True)


def place_of(iota, rows, rank):
    quarter = rows // 4
    part = iota // quarter
    relative = (part % 2) * 2 + part // 2
    return jnp.bitwise_xor(relative, rank) * quarter + iota % quarter


def stack(slab, kv_head):
    slab = slab.astype(F32)
    turned = pltpu.roll(slab, HD, 1)
    low = lanes(slab.shape) < HD
    if kv_head == 0:
        parts = [jnp.where(low, slab, 0.0), jnp.where(low, turned, 0.0)]
    else:
        parts = [jnp.where(low, 0.0, turned), jnp.where(low, 0.0, slab)]
    return jnp.concatenate(parts, axis=0)


def unstack(stacked, kv_head):
    rows = stacked.shape[0] // 2
    first, second = stacked[:rows], stacked[rows:]
    low = lanes(first.shape) < HD
    if kv_head == 0:
        return jnp.where(low, first, pltpu.roll(second, HD, 1))
    return jnp.where(low, pltpu.roll(first, HD, 1), second)


def qkv_kernel(
    x1, x2, x3, x0, gain, positions, wk, wv, key_gain, wq, query_gain,
    act_out, select_out, pair_out, query_rot_out, query_out, key_out,
    cos_out, sin_out, column_out, row_out, *scratch,
):
    sources = (x0, gain, positions, wk, wv, key_gain, wq, query_gain)
    buffers, sems = scratch[:-1], scratch[-1]
    copies = [
        pltpu.make_async_copy(source, buffer, sems.at[i])
        for i, (source, buffer) in enumerate(zip(sources, buffers, strict=True))
    ]
    for copy in copies:
        copy.start()
    for copy in copies:
        copy.wait()
    x0, gain, positions, wk, wv, key_gain, wq, query_gain = buffers
    ranks = (lax.axis_index("ctx"), lax.axis_index("mp"))
    rows = act_out.shape[0]
    line = lax.broadcasted_iota(jnp.int32, (rows, rows), 0)
    picked = place_of(line, rows, ranks[1]) == lanes((rows, rows))
    column = jnp.sum(
        jnp.where(picked, positions[...].astype(F32), 0.0), axis=1, keepdims=True
    )
    column_out[...] = column.astype(jnp.int32)
    row = jnp.sum(jnp.where(line == lanes((rows, rows)), column, 0.0), axis=0, keepdims=True)
    row_out[...] = row.astype(jnp.int32)
    lane = lanes((1, 128))
    power = (lane % (HD // 2)).astype(F32) * (-2.0 / HD)
    angles = column * jnp.exp(power * math.log(ROPE_BASE))
    cos = jnp.cos(angles)
    sin = jnp.sin(angles) * jnp.where(lane % HD < HD // 2, -1.0, 1.0)
    cos_out[...] = cos
    sin_out[...] = sin

    x = jnp.concatenate([x0[...], x1[...], x2[...], x3[...]], axis=0).astype(F32)
    act = (x * row_norm(x) * gain[...]).astype(BF)
    act_out[...] = act
    keys = dot(act, wk[...])
    key_out[...] = keys
    width = keys.shape[-1]
    normed = keys * head_norm(keys) * wide(key_gain[...], width)
    rotated = normed * wide(cos, width) + partner(normed) * wide(sin, width)
    pair_out[:, :width] = rotated.astype(BF)
    pair_out[:, width:] = dot(act, wv[...]).astype(BF)
    queries = dot(act, wq[...])
    query_out[...] = queries
    width = queries.shape[-1]
    normed = queries * head_norm(queries) * wide(query_gain[...], width)
    rotated = normed * wide(cos, width) + partner(normed) * wide(sin, width)
    query_rot_out[...] = rotated.astype(BF)
    select_columns(ranks, act_out, select_out)


def pack_kernel(cot, there_cot, packet_out):
    packet_out[:, : cot.shape[1]] = cot[...]
    packet_out[:, cot.shape[1] :] = there_cot[...]


def select_columns(ranks, source, target):
    columns = target.shape[1]
    blocks = columns // 128
    if blocks != 4:
        target[...] = jnp.zeros(target.shape, target.dtype)
        return
    for b in range(blocks):
        start = pl.multiple_of((2 * b + 1 - ranks[0] % 2) * 128, 128)
        target[:, b * 128 : (b + 1) * 128] = source[:, pl.ds(start, 128)]


def cotangent_kernel(ranks, p0, p1, p2, p3, wd, cot_out, there_out, grad_hidden_out):
    packet = jnp.concatenate([p0[...], p1[...], p2[...], p3[...]], axis=0)
    width = cot_out.shape[1]
    cot = packet[:, :width]
    cot_out[...] = cot
    grad_hidden_out[...] = dot(cot, wd[...], COLS)
    if width // lax.axis_size("ctx") != 128:
        there_out[...] = jnp.zeros(there_out.shape, BF)
        return
    source = packet[:, width:].astype(F32)
    for b in range(width // 256):
        low = source[:, 256 * b : 256 * b + 128]
        high = source[:, 256 * b + 128 : 256 * b + 256]
        there_out[:, 128 * b : 128 * (b + 1)] = jnp.where(ranks[0] % 2 == 1, high, low).astype(BF)


def attention_kernel(count, ranks, query_rot, positions, wo, act_select, *refs):
    slots = count // 2
    even = refs[:slots]
    crossed = refs[slots : 2 * slots]
    out_f32, out_b, sums_out, kept_out, sent_out = refs[2 * slots : 2 * slots + 5]
    odd = refs[2 * slots + 5 : -1]
    scores = refs[-1]
    rows = query_rot.shape[0]
    key_width = even[0].shape[1] // 2
    for j in range(slots):
        odd[j][...] = jnp.where(
            ranks[0] % 2 == 1,
            crossed[j][...].astype(F32),
            crossed[(j + 1) % slots][...].astype(F32),
        ).astype(BF)
    blocks = [(even, odd)[d % 2][d // 2] for d in range(count)]
    query_index = ranks[0] * rows + place_of(
        lax.broadcasted_iota(jnp.int32, (rows, 1), 0), rows, ranks[1]
    )
    first_seen = query_index - positions[...]
    key_place = place_of(lanes((1, rows)), rows, ranks[1])
    masks = []
    for d in range(count):
        key_index = (ranks[0] - d) * rows + key_place
        mask = key_index >= first_seen
        if d == 0:
            mask = mask & (key_index <= query_index)
        masks.append(jnp.where(mask, 0.0, MASKED_SCORE))
    for head in range(2):
        slab = query_rot[:, head * 128 : (head + 1) * 128]
        stacked = (stack(slab, head) * SCALE).astype(BF)
        top = jnp.full((2 * rows, 1), MASKED_SCORE, F32)
        for d in range(count):
            block = dot(stacked, blocks[d][:, :key_width], COLS)
            block = block + jnp.concatenate([masks[d], masks[d]], axis=0)
            scores[:, d * rows : (d + 1) * rows] = block
            top = jnp.maximum(top, jnp.max(block, axis=-1, keepdims=True))
        total = jnp.zeros((2 * rows, 1), F32)
        mixed = jnp.zeros((2 * rows, key_width), F32)
        for d in range(count):
            weights = jnp.exp(scores[:, d * rows : (d + 1) * rows] - top)
            total = total + jnp.sum(weights, axis=-1, keepdims=True)
            mixed = mixed + dot(weights.astype(BF), blocks[d][:, key_width:])
        sums = jnp.broadcast_to(top + jnp.log(total), (2 * rows, 128))
        sums_out[head : head + 1, :] = jnp.transpose(sums)[:1]
        out_f32[:, head * 128 : (head + 1) * 128] = unstack(mixed / total, head)
    attn_b = out_f32[...].astype(BF)
    chosen = act_select.shape[1]
    out_b[:, :chosen] = act_select[...]
    out_b[:, chosen:] = attn_b
    half = rows // 2
    kept_out[...] = dot(attn_b[:half], wo[...])
    sent_out[...] = dot(attn_b[half:], wo[...]).astype(BF)


def add_kernel(kept, arrived, out):
    out[...] = (kept[...].astype(F32) + arrived[...].astype(F32)).astype(out.dtype)


def flipped_add_kernel(kept, arrived, out):
    half = kept.shape[0] // 2
    for a, b in ((0, half), (half, 0)):
        total = kept[a : a + half, :].astype(F32) + arrived[b : b + half, :].astype(F32)
        out[a : a + half, :] = total.astype(out.dtype)


def fold_kernel(*refs):
    count = (len(refs) - 1) // 3
    back_out = refs[-1]
    place = 0
    for p in range(count):
        kept, arrived, front_out = refs[2 * p], refs[2 * p + 1], refs[2 * count + p]
        half, width = front_out.shape
        front_out[...] = kept[:half, :] + arrived[:half, :].astype(F32)
        back_out[:, place : place + width] = (
            kept[half:, :] + arrived[half:, :].astype(F32)
        ).astype(BF)
        place += width


def mp_fold_kernel(input_kept, out_kept, gains, arrived, input_front, out_front, gains_out, back):
    half = input_kept.shape[0]
    own = half // 2
    came = arrived[...].astype(F32)
    for place, kept, front in ((0, input_kept, input_front), (1, out_kept, out_front)):
        total = kept[...] + came[place * half : (place + 1) * half]
        front[...] = total[:own]
        back[place * own : (place + 1) * own, :] = total[own:].astype(BF)
    gains_out[...] = gains[...] + unpack(came[2 * half :], gains.shape[0])
    pack(gains_out[...], back, 2 * own)


def pack(values, target, start):
    count = values.shape[0]
    target[start : start + 16, :] = jnp.zeros((16, target.shape[1]), BF)
    front = values.astype(BF)
    for part, piece in enumerate((front.astype(F32), values - front.astype(F32))):
        for g in range(-(-count // 16)):
            rows = piece[16 * g : 16 * g + 16]
            if rows.shape[0] < 16:
                rows = jnp.concatenate([rows, jnp.zeros((16 - rows.shape[0], 128), F32)], axis=0)
            column = (2 * g + part) * 128
            target[start : start + 16, column : column + 128] = rows.astype(BF)


def unpack(values, count):
    pieces = []
    for g in range(-(-count // 16)):
        column = 2 * g * 128
        total = values[:, column : column + 128] + values[:, column + 128 : column + 256]
        pieces.append(total[: min(16, count - 16 * g)])
    return jnp.concatenate(pieces, axis=0)


def last_kernel(turned, *refs):
    count = len(turned)
    arrived, outs, token = refs[count], refs[count + 1 : -1], refs[-1]
    place = 0
    for p in range(count):
        width = refs[p].shape[1]
        total = refs[p][...] + arrived[:, place : place + width].astype(F32)
        outs[p][...] = jnp.transpose(total) if turned[p] else total
        place += width
    token[...] = jnp.zeros(token.shape, F32)


def attention_last_kernel(kept, arrived, out_grad, query_grad, key_grad, value_grad):
    total = kept[...] + arrived[...].astype(F32)
    turned = out_grad.shape[0]
    out_grad[...] = jnp.transpose(total[:, :turned])
    start = turned
    for out in (query_grad, key_grad, value_grad):
        width = out.shape[1]
        out[...] = total[:, start : start + width]
        start += width


def pair_sum_kernel(slots, ranks, *refs):
    odd = ranks[0] % 2 == 1
    terms, arrived = refs[:slots], refs[slots]
    outs = refs[slots + 1 :]
    rows = terms[0].shape[0]
    came = [arrived[j * rows : (j + 1) * rows, :].astype(F32) for j in range(slots)]
    outs[0][...] = terms[0][...] + jnp.where(odd, 0.0, came[0])
    for k in range(1, slots):
        outs[k][...] = (
            terms[k][...].astype(F32) + jnp.where(odd, came[k - 1], came[k])
        ).astype(BF)
    outs[slots][...] = came[slots - 1].astype(BF)


def down_kernel(hidden, wd, kept_out, sent_out):
    half = hidden.shape[0] // 2
    sent_out[...] = dot(hidden[half:, :], wd[...]).astype(BF)
    kept_out[...] = dot(hidden[:half, :], wd[...])


def outputs_kernel(
    x, gain, grad_resid, resid, input_kept, out_kept, gains, arrived,
    grad_input_out, block_out, gains_out,
):
    own = block_out.shape[0]
    came = arrived[...].astype(F32)
    block_out[...] = (resid[:own, :] + out_kept[...] + came[own : 2 * own]).astype(BF)
    gains_out[...] = gains[...] + unpack(came[2 * own :], gains.shape[0])
    grads = input_kept[...] + came[:own]
    values = x[...].astype(F32)
    scale = row_norm(values)
    normed = values * scale
    inner = grads * gain[...]
    grad_input_out[...] = grad_resid[...] + scale * (
        inner - normed * jnp.mean(inner * normed, axis=-1, keepdims=True)
    )


def ffn_kernel(
    ranks, x0, x1, x2, x3, half0, half1, gain, wg, wu, grad_hidden,
    resid_out, act_out, hidden_out, gate_packet, grad_up_out, kept_out, sent_out,
):
    x = jnp.concatenate([x0[...], x1[...], x2[...], x3[...]], axis=0).astype(F32)
    resid = x + jnp.concatenate([half0[...], half1[...]], axis=0).astype(F32)
    resid_out[...] = resid
    act = (resid * row_norm(resid) * gain[...]).astype(BF)
    act_out[...] = act
    values = dot(act, wg[...])
    upper = dot(act, wu[...])
    sigmoid = jax.nn.sigmoid(values)
    hidden_out[...] = (values * sigmoid * upper).astype(BF)
    grads = grad_hidden[...]
    grad_gate = (grads * upper * sigmoid * (1.0 + values * (1.0 - sigmoid))).astype(BF)
    grad_up = (grads * values * sigmoid).astype(BF)
    chosen = act.shape[1] // 2
    select_columns(ranks, act_out, gate_packet.at[:, :chosen])
    gate_packet[:, chosen:] = grad_gate
    grad_up_out[...] = grad_up
    half = resid.shape[0] // 2
    sent_out[...] = (
        dot(grad_gate[half:], wg[...], COLS) + dot(grad_up[half:], wu[...], COLS)
    ).astype(BF)
    kept_out[...] = dot(grad_gate[:half], wg[...], COLS) + dot(grad_up[:half], wu[...], COLS)


def attention_backward_kernel(
    count, ranks, cot, resid, half0, half1, gain, wo, attn, sums, query_rot, positions, *refs
):
    blocks = refs[:count]
    grad_own_out, grad_b_out, select_out, gain_out, grad_query_out = refs[count : count + 5]
    even, odd = refs[count + 5 : -1], refs[-1]
    rows = query_rot.shape[0]
    terms = [
        even[d // 2] if d % 2 == 0 else odd.at[d // 2 * rows : (d // 2 + 1) * rows]
        for d in range(count)
    ]
    key_width = blocks[0].shape[1] // 2
    values = resid[...]
    scale = row_norm(values)
    normed = values * scale
    grads = jnp.concatenate([half0[...], half1[...]], axis=0).astype(F32)
    inner = grads * gain[...]
    grad_in = scale * (inner - normed * jnp.mean(inner * normed, axis=-1, keepdims=True))
    grad_resid = cot[...].astype(F32) + grad_in
    own = rows // 4
    grad_own_out[...] = grad_resid[:own]
    gain_out[...] = jnp.sum(grads[:own] * normed[:own], axis=0, keepdims=True)
    grad_resid_b = grad_resid.astype(BF)
    grad_b_out[...] = grad_resid_b
    select_columns(ranks, grad_b_out, select_out)
    grad_attn = dot(grad_resid_b, wo[...], COLS)
    delta = jnp.transpose(group_sum(grad_attn * attn[...]))
    grad_attn_b = grad_attn.astype(BF)

    query_index = ranks[0] * rows + place_of(lanes((1, rows)), rows, ranks[1])
    first_row = query_index - positions[...]
    key_place = place_of(lax.broadcasted_iota(jnp.int32, (rows, 1), 0), rows, ranks[1])
    stacked = [stack(query_rot[:, h * 128 : (h + 1) * 128], h) for h in range(2)]
    stacked_b = [s.astype(BF) for s in stacked]
    scaled = [(s * SCALE).astype(BF) for s in stacked]
    grads_b = [
        stack(grad_attn_b[:, h * 128 : (h + 1) * 128], h).astype(BF) for h in range(2)
    ]
    deltas = [
        jnp.concatenate(
            [delta[2 * h * HD : 2 * h * HD + 1], delta[(2 * h + 1) * HD : (2 * h + 1) * HD + 1]],
            axis=1,
        )
        for h in range(2)
    ]
    grad_query = [jnp.zeros((2 * rows, key_width), F32) for _ in range(2)]
    for d in range(count - 1, -1, -1):
        key_index = (ranks[0] - d) * rows + key_place
        mask = key_index >= first_row
        if d == 0:
            mask = mask & (key_index <= query_index)
        mask = jnp.where(mask, 0.0, MASKED_SCORE)
        mask = jnp.concatenate([mask, mask], axis=1)
        key_block = blocks[d][:, :key_width]
        value_block = blocks[d][:, key_width:]
        key_term = jnp.zeros((rows, key_width), F32)
        value_term = jnp.zeros((rows, key_width), F32)
        for h in range(2):
            scores = dot(key_block, scaled[h], COLS) + mask
            probs = jnp.exp(scores - sums[h : h + 1, :])
            grad_probs = dot(value_block, grads_b[h], COLS)
            grad_scores = (probs * (grad_probs - deltas[h]) * SCALE).astype(BF)
            key_term = key_term + dot(grad_scores, stacked_b[h])
            value_term = value_term + dot(probs.astype(BF), grads_b[h])
            grad_query[h] = grad_query[h] + dot(grad_scores, key_block, ROWS)
        terms[d][:, :key_width] = key_term.astype(terms[d].dtype)
        terms[d][:, key_width:] = value_term.astype(terms[d].dtype)
    for h in range(2):
        grad_query_out[:, h * 128 : (h + 1) * 128] = unstack(grad_query[h], h)


def query_backward_kernel(
    queries, gain, grads, cos, sin, wq, grad_out, gain_out, partial_out
):
    grad_in, gain_terms = head_norm_backward(queries[...], wide(gain[...], queries.shape[-1]), grads[...], cos[...], sin[...])
    grad_b = grad_in.astype(BF)
    grad_out[...] = grad_b
    gain_out[...] = gain_terms
    partial_out[...] = dot(grad_b, wq[...], COLS)


def key_backward_kernel(
    keys, gain, cos, sin, wk, wv, query_partial, x0, x1, x2, x3,
    ffn_gain_part, query_gain_part, out_sent, select, grad_query_b, term, *refs,
):
    shifted = refs[:-4]
    late_out, gains_out, kept_out, sent_out = refs[-4:]
    width = keys.shape[-1]
    grads = term[...]
    for other in shifted:
        grads = grads + other[...].astype(F32)
    grad_in, gain_terms = head_norm_backward(
        keys[...], wide(gain[...], width), grads[:, :width], cos[...], sin[...]
    )
    grad_b = grad_in.astype(BF)
    value_b = grads[:, width:].astype(BF)
    place = 0
    for piece in (select[...], grad_query_b[...], grad_b, value_b):
        late_out[:, place : place + piece.shape[1]] = piece
        place += piece.shape[1]
    partial = query_partial[...] + dot(grad_b, wk[...], COLS) + dot(value_b, wv[...], COLS)
    half = partial.shape[0] // 2
    kept_out[...] = partial[:half]
    sent_out[:half, :] = partial[half:].astype(BF)
    sent_out[half : 2 * half, :] = out_sent[...]
    x = jnp.concatenate([x0[...], x1[...], x2[...], x3[...]], axis=0).astype(F32)
    features = x.shape[1]
    parts = [
        jnp.sum(partial * (x * row_norm(x)), axis=0, keepdims=True),
        ffn_gain_part[...],
    ]
    row = 0
    for part in parts:
        for c in range(features // 128):
            gains_out[row : row + 1, :] = part[:, c * 128 : (c + 1) * 128]
            row += 1
    queries = query_gain_part[...]
    queries = sum(queries[:, c * 128 : (c + 1) * 128] for c in range(queries.shape[1] // 128))
    gains_out[row : row + 1, :] = queries
    gains_out[row + 1 : row + 2, :] = gain_terms
    pack(gains_out[...], sent_out, 2 * half)


def weight_grad_kernel(parts, ranks, *refs):
    kept_out, sent_out = refs[-2:]
    parity = ranks[0] % 2
    mine = ranks[0] // 2
    place = 0
    for p, (own, there_at, act_at, width) in enumerate(parts):
        act, arrived_act, grads, arrived_grads = refs[4 * p : 4 * p + 4]
        mine_grads = grads[:, own : own + width]
        other_grads = arrived_grads[:, there_at : there_at + width]
        for lo in (1, 0):
            for hi in range(2):
                block = jnp.bitwise_xor(mine, lo + 2 * hi)
                start = pl.multiple_of((2 * block + parity) * 128, 128)
                there = pl.multiple_of(act_at + block * 128, 128)
                total = dot(act[:, pl.ds(start, 128)], mine_grads, ROWS) + dot(
                    arrived_act[:, pl.ds(there, 128)], other_grads, ROWS
                )
                target = sent_out if lo else kept_out
                target[hi * 128 : (hi + 1) * 128, place : place + width] = total.astype(
                    target.dtype
                )
        place += width


def shape(dims, dtype):
    return jax.ShapeDtypeStruct(dims, dtype)


def launch(kernel, outs, args, scratch=(), name=None, after=(), carry=()):
    nbytes = sum(s.shape[0] * s.shape[1] * 4 for s in scratch)
    ranked = args[0] is RANKS
    args = list(args[ranked:])
    n_in, n_out, n_unused = len(args), len(outs), len(after) + len(carry)

    def run(*refs):
        results = refs[n_in + n_unused :]
        ranks = [(lax.axis_index("ctx"), lax.axis_index("mp"))] if ranked else []
        kernel(*ranks, *refs[:n_in], *results[:n_out], *results[n_out + len(carry) :])

    any_spec = pl.BlockSpec(memory_space=pl.ANY)
    return pl.pallas_call(
        run,
        out_shape=list(outs) + [shape(c.shape, c.dtype) for c in carry],
        in_specs=[pl.BlockSpec(memory_space=pltpu.VMEM)] * n_in + [any_spec] * n_unused,
        out_specs=[pl.BlockSpec(memory_space=pltpu.VMEM) for _ in outs] + [any_spec] * len(carry),
        scratch_shapes=list(scratch),
        input_output_aliases={n_in + len(after) + i: n_out + i for i in range(len(carry))},
        compiler_params=pltpu.CompilerParams(vmem_limit_bytes=nbytes + (12 << 20)),
        name=name,
    )(*args, *after, *carry)


def add(kept, arrived, dtype, name, kernel=add_kernel, after=(), carry=()):
    out = launch(
        kernel, [shape(kept.shape, dtype)], [kept, arrived], name=name, after=after, carry=carry
    )
    return out if carry else out[0]


def mp_gather(values):
    other = xor(values, "mp", 2)
    core = xor(values, "mp", 1)
    return values, other, core, xor(other, "mp", 1)


def split_columns(values):
    n = lax.axis_size("ctx")
    index = lax.axis_index("ctx")
    rows, columns = values.shape
    bits = n.bit_length() - 1
    parts = values.reshape((rows,) + (2,) * bits + (columns // n,))
    for bit in range(bits):
        parts = jnp.where((index >> bit) % 2 == 1, jnp.flip(parts, bits - bit), parts)
    order = [0] + [bits - b for b in range(bits)] + [bits + 1]
    parts = jnp.transpose(parts, order).reshape(rows, 2, columns // 2)
    return parts[:, 0], parts[:, 1]


def weight_grad(parts, name, after=()):
    n = lax.axis_size("ctx")
    act = parts[0][0]
    half = act.shape[1] // 4
    columns = sum(part[6] for part in parts)
    if n == 8 and act.shape[1] == 1024:
        return launch(
            functools.partial(weight_grad_kernel, [part[4] + part[5:] for part in parts]),
            [shape((half, columns), F32), shape((half, columns), BF)],
            [RANKS] + [a for part in parts for a in part[:4]],
            name=name,
            after=after,
        )
    totals = []
    for act, _, grads, arrived_grads, offsets, _, width in parts:
        own, other = split_columns(act)
        grads = grads[:, offsets[0] : offsets[0] + width]
        arrived_grads = arrived_grads[:, offsets[1] : offsets[1] + width]
        both = jnp.concatenate([own, xor(other, "ctx", 1)], axis=0)
        totals.append(dot(both, jnp.concatenate([grads, arrived_grads], axis=0), ROWS))
    total = jnp.concatenate(totals, axis=1)
    return total[:half], total[half:].astype(BF)


def fold(pairs, name, after=()):
    n = lax.axis_size("ctx")
    kept = [p[0] for p in pairs]
    arrived = [p[1] for p in pairs]
    mask = 4
    while mask < n:
        half = kept[0].shape[0] // 2
        widths = [k.shape[1] for k in kept]
        outs = launch(
            fold_kernel,
            [shape((half, w), F32) for w in widths] + [shape((half, sum(widths)), BF)],
            [a for pair in zip(kept, arrived, strict=True) for a in pair],
            name=name,
            after=after,
        )
        kept, back = outs[:-1], outs[-1]
        came = xor(back, "ctx", mask)
        mask *= 2
        if mask >= n:
            return kept, came, back
        arrived = []
        for w in widths:
            start = sum(a.shape[1] for a in arrived)
            arrived.append(came[:, start : start + w])
    return kept, came, back


def body(
    block_in,
    attn_gain,
    query_weight,
    key_weight,
    value_weight,
    out_weight,
    query_gain,
    key_gain,
    ffn_gain,
    gate_weight,
    up_weight,
    down_weight,
    segments,
    positions,
    cotangent,
):
    width = block_in.shape[1]
    key_width = key_weight.shape[1]
    query_width = query_weight.shape[1]
    hidden_width = gate_weight.shape[1]
    n_ctx = lax.axis_size("ctx")
    ctx_rank = lax.axis_index("ctx")
    own_rows = block_in.shape[0]
    rows = positions.shape[0]
    total_tokens = rows * n_ctx
    longest = LONGEST.get(total_tokens, total_tokens)
    window = min(n_ctx - 1, -(-(longest - 1) // rows))
    slots = (window + 1) // 2
    count = window + 1
    half = rows // 2

    x = mp_gather(block_in)
    query_gain_row = query_gain.reshape(1, -1)
    key_gain_row = key_gain.reshape(1, -1)
    attn_gain_row = attn_gain.reshape(1, -1)
    ffn_gain_row = ffn_gain.reshape(1, -1)

    outs = [
        shape((rows, width), BF),
        shape((rows, width // 2), BF),
        shape((rows, 2 * key_width), BF),
        shape((rows, query_width), BF),
        shape((rows, query_width), F32),
        shape((rows, key_width), F32),
        shape((rows, 128), F32),
        shape((rows, 128), F32),
        shape((rows, 1), jnp.int32),
        shape((1, rows), jnp.int32),
    ]
    copied = [block_in, attn_gain_row, positions.reshape(1, -1), key_weight, value_weight,
              key_gain_row, query_weight, query_gain_row]
    (
        act_attn, act_attn_select, pair, query_rot, queries, keys_pre,
        cos, sin, position_column, position_row,
    ) = pl.pallas_call(
        qkv_kernel,
        out_shape=outs,
        in_specs=[pl.BlockSpec(memory_space=pltpu.VMEM)] * 3
        + [pl.BlockSpec(memory_space=pl.ANY)] * len(copied),
        out_specs=[pl.BlockSpec(memory_space=pltpu.VMEM)] * len(outs),
        scratch_shapes=[pltpu.VMEM(a.shape, a.dtype) for a in copied]
        + [pltpu.SemaphoreType.DMA((len(copied),))],
        compiler_params=pltpu.CompilerParams(vmem_limit_bytes=52 << 20),
        name="qkv",
    )(*x[1:], *copied)

    def climb(step):
        pairs = [(i, i + step) for i in range(n_ctx - step)]
        return lax.ppermute(pair, "ctx", pairs) if pairs else jnp.zeros_like(pair)

    even = [pair] + [climb(2 * k) for k in range(1, slots)]
    farthest = 2 * slots - 1
    pairs = [(i, i + 1) for i in range(0, n_ctx, 2)]
    pairs += [(i, i + farthest) for i in range(1, n_ctx - farthest, 2)]
    crossed = [lax.ppermute(pair, "ctx", pairs)] + [xor(e, "ctx", 1) for e in even[1:]]
    packet = launch(
        pack_kernel,
        [shape((own_rows, 2 * width), BF)],
        [cotangent, xor(cotangent, "ctx", 1)],
        name="pack",
        after=[pair],
    )[0]
    packets = mp_gather(packet)

    outs = launch(
        functools.partial(attention_kernel, count),
        [
            shape((rows, query_width), F32),
            shape((rows, width // 2 + query_width), BF),
            shape((2, 2 * rows), F32),
            shape((half, width), F32),
            shape((half, width), BF),
        ]
        + [shape((rows, 2 * key_width), BF) for _ in range(slots)],
        [RANKS, query_rot, position_column, out_weight, act_attn_select,
         *even, *crossed],
        scratch=[pltpu.VMEM((2 * rows, count * rows), F32)],
        name="attention",
        after=packets[1:3],
    )
    attn_rows, early, log_sums, kept, sent = outs[:5]
    blocks = [(even, outs[5:])[d % 2][d // 2] for d in range(count)]
    chosen = width // 2

    kept = add(kept, xor(sent, "mp", 1), BF, "resid_core")
    cot, cot_there, grad_hidden = launch(
        cotangent_kernel,
        [
            shape((rows, width), BF),
            shape((rows, chosen), BF),
            shape((rows, hidden_width), F32),
        ],
        [RANKS, *packets, down_weight],
        name="cotangent",
        after=[kept],
    )
    early_there = xor(early, "ctx", 1)
    both = add(
        kept, xor(kept, "mp", 2), BF, "resid_chip", kernel=flipped_add_kernel,
        after=[grad_hidden],
    )

    resid, act_ffn, hidden, gate_packet, grad_up, kept, sent = launch(
        ffn_kernel,
        [
            shape((rows, width), F32),
            shape((rows, width), BF),
            shape((rows, hidden_width), BF),
            shape((rows, chosen + hidden_width), BF),
            shape((rows, hidden_width), BF),
            shape((half, width), F32),
            shape((half, width), BF),
        ],
        [RANKS, *x, both, xor(both, "mp", 1), ffn_gain_row, gate_weight, up_weight, grad_hidden],
        name="ffn",
    )
    hidden_there = xor(hidden, "ctx", 1)
    kept, gate_packet = add(kept, xor(sent, "mp", 1), BF, "grad_act_core", carry=[gate_packet])
    gate_there = xor(gate_packet, "ctx", 1)
    both = add(kept, xor(kept, "mp", 2), BF, "grad_act_chip", kernel=flipped_add_kernel)
    down_kept, down_sent = weight_grad(
        [(cot, cot_there, hidden, hidden_there, (0, 0), 0, hidden_width)], "down_grad",
        after=[both],
    )

    outs = launch(
        functools.partial(attention_backward_kernel, count),
        [
            shape((own_rows, width), F32),
            shape((rows, width), BF),
            shape((rows, chosen), BF),
            shape((1, width), F32),
            shape((rows, query_width), F32),
        ]
        + [shape((rows, 2 * key_width), BF if d else F32) for d in range(slots)]
        + [shape((slots * rows, 2 * key_width), BF)],
        [RANKS, cot, resid, both, xor(both, "mp", 1), ffn_gain_row, out_weight, attn_rows,
         log_sums, query_rot, position_row, *blocks],
        name="attention_backward",
        after=[down_sent],
    )
    grad_resid, grad_resid_b, grad_select, ffn_gain_part, grad_query = outs[:5]
    terms, odd_terms = outs[5:-1], outs[-1]

    arrived = xor(odd_terms, "ctx", 1)
    down_arrived = xor(down_sent, "ctx", 2)
    gate_kept, gate_sent = weight_grad(
        [(act_ffn, gate_there, gate_packet, gate_there, (chosen, chosen), 0, hidden_width)],
        "gate_grad",
        after=[grad_query, down_arrived],
    )
    totals = launch(
        functools.partial(pair_sum_kernel, slots),
        [shape(terms[0].shape, BF if k else F32) for k in range(slots + 1)],
        [RANKS, *terms, arrived],
        name="pair_sums",
        after=[gate_sent],
        carry=[grad_up],
    )
    grad_up = totals[-1]
    up_there = xor(grad_up, "ctx", 1)
    shifted = [down(totals[k], 2 * k) for k in range(slots - 1, 0, -1)]
    if 2 * slots < n_ctx:
        pairs = [(i, i - 2 * slots) for i in range(2 * slots, n_ctx) if i % 2 == 1]
        shifted.append(lax.ppermute(totals[slots], "ctx", pairs))

    grad_query_b, query_gain_part, query_partial = launch(
        query_backward_kernel,
        [
            shape((rows, query_width), BF),
            shape((1, query_width), F32),
            shape((rows, width), F32),
        ],
        [queries, query_gain_row, grad_query, cos, sin, query_weight],
        name="query_backward",
        after=[totals[0]],
    )
    out_kept, out_sent = launch(
        down_kernel,
        [shape((half, width), F32), shape((half, width), BF)],
        [hidden, down_weight],
        name="down",
        after=[query_partial],
    )
    (down_kept, gate_kept), first_arrived, back = fold(
        [(down_kept, down_arrived), (gate_kept, xor(gate_sent, "ctx", 2))],
        "first_fold",
        after=[out_sent],
    )
    up_kept, up_sent = weight_grad(
        [(act_ffn, gate_there, grad_up, up_there, (0, 0), 0, hidden_width)], "up_grad",
        after=[back],
    )
    late, gains, kept, sent = launch(
        key_backward_kernel,
        [
            shape((rows, chosen + query_width + 2 * key_width), BF),
            shape((2 * width // 128 + 2, 128), F32),
            shape((half, width), F32),
            shape((rows + 16, width), BF),
        ],
        [keys_pre, key_gain_row, cos, sin, key_weight, value_weight, query_partial, *x,
         ffn_gain_part, query_gain_part, out_sent, grad_select, grad_query_b, totals[0],
         *shifted],
        name="key_backward",
        after=[up_sent],
    )
    late_there = xor(late, "ctx", 1)
    core_arrived = xor(sent, "mp", 1)
    query_at = chosen
    pair_at = chosen + query_width
    input_kept, out_kept, gains, back = launch(
        mp_fold_kernel,
        [
            shape((own_rows, width), F32),
            shape((own_rows, width), F32),
            shape(gains.shape, F32),
            shape((half + 16, width), BF),
        ],
        [kept, out_kept, gains, core_arrived],
        name="mp_fold",
    )
    grad_input, block_out, gains = launch(
        outputs_kernel,
        [
            shape((own_rows, width), F32),
            shape((own_rows, width), BF),
            shape(gains.shape, F32),
        ],
        [x[0], attn_gain_row, grad_resid, resid, input_kept, out_kept, gains,
         xor(back, "mp", 2)],
        name="outputs",
        after=[early_there],
    )
    attn_kept, attn_sent = weight_grad(
        [
            (grad_resid_b, late_there, early, early_there, (chosen, chosen), 0, query_width),
            (act_attn, early_there, late, late_there, (query_at, query_at), 0, query_width),
            (act_attn, early_there, late, late_there, (pair_at, pair_at), 0, 2 * key_width),
        ],
        "attention_grads",
        after=[gains],
    )
    gains = add(gains, xor(gains, "ctx", 1), F32, "gains", after=[attn_sent])
    (up_kept,), up_arrived, back = fold(
        [(up_kept, xor(up_sent, "ctx", 2))], "up_fold", after=[gains]
    )
    token = shape((8, 128), F32)
    down_grad, gate_grad, done = launch(
        functools.partial(last_kernel, (True, False)),
        [shape(down_kept.shape[::-1], F32), shape(gate_kept.shape, F32), token],
        [down_kept, gate_kept, first_arrived],
        name="first_last",
        after=[back],
    )
    mask = 2
    while mask < n_ctx // 2:
        gains = add(gains, xor(gains, "ctx", mask), F32, "gains", after=[done])
        mask *= 2
    (attn_kept,), attn_arrived, back = fold(
        [(attn_kept, xor(attn_sent, "ctx", 2))], "attention_fold", after=[done]
    )
    up_grad, done = launch(
        functools.partial(last_kernel, (False,)),
        [shape(up_kept.shape, F32), token],
        [up_kept, up_arrived],
        name="up_last",
        after=[back],
    )
    gains = add(gains, xor(gains, "ctx", mask), F32, "gains", after=[done])
    out_grad, query_grad, key_grad, value_grad = launch(
        attention_last_kernel,
        [shape((query_width, attn_kept.shape[0]), F32)]
        + [shape((attn_kept.shape[0], w), F32) for w in (query_width, key_width, key_width)],
        [attn_kept, attn_arrived],
        name="attention_last",
        after=[gains],
    )
    gains = gains.reshape(-1)
    heads = gains[2 * width :].reshape(2, -1, HD).sum(axis=1)
    query_gains, key_gains = heads[0], heads[1]
    return (
        block_out,
        grad_input,
        query_grad,
        key_grad,
        value_grad,
        out_grad,
        gate_grad,
        up_grad,
        down_grad,
        gains[:width],
        gains[width : 2 * width],
        query_gains,
        key_gains,
    )


def solution(mesh):
    in_specs = (
        P(("ctx", "mp"), None),
        P(),
        P(None, "mp"),
        P(None, "mp"),
        P(None, "mp"),
        P("mp", None),
        P(),
        P(),
        P(),
        P(None, "mp"),
        P(None, "mp"),
        P("mp", None),
        P(),
        P("ctx"),
        P(("ctx", "mp"), None),
    )
    out_specs = (
        P(("ctx", "mp"), None),
        P(("ctx", "mp"), None),
        P("ctx", "mp"),
        P("ctx", "mp"),
        P("ctx", "mp"),
        P("mp", "ctx"),
        P("ctx", "mp"),
        P("ctx", "mp"),
        P("mp", "ctx"),
        P(),
        P(),
        P(),
        P(),
    )
    return jax.shard_map(body, mesh=mesh, in_specs=in_specs, out_specs=out_specs, check_vma=False)
```

```python
import functools
import math

import jax
import jax.numpy as jnp
from jax import lax
from jax.experimental import pallas as pl
from jax.experimental.pallas import tpu as pltpu
from jax.sharding import PartitionSpec as P

HEADS = 16
KV_HEADS = 8
HD = 64
EPS = 1e-05
ROPE_BASE = 1000000.0
MASKED_SCORE = -1e30
LONGEST = {2048: 1280, 8192: 4352}
BF = jnp.bfloat16
F32 = jnp.float32
ROWS = (((0,), (0,)), ((), ()))
COLS = (((1,), (1,)), ((), ()))
SCALE = HD ** (-0.5)
RANKS = "ranks"


def dot(a, b, dims=(((1,), (0,)), ((), ()))):
    return lax.dot_general(a, b, dims, preferred_element_type=F32)


def xor(values, axis, mask):
    n = lax.axis_size(axis)
    return lax.ppermute(values, axis, [(i, i ^ mask) for i in range(n)])


def up(values, step):
    n = lax.axis_size("ctx")
    return lax.ppermute(values, "ctx", [(i, i + step) for i in range(n - step)])


def down(values, step):
    n = lax.axis_size("ctx")
    return lax.ppermute(values, "ctx", [(i, i - step) for i in range(step, n)])


def lanes(shape):
    return lax.broadcasted_iota(jnp.int32, shape, len(shape) - 1)


def group_sum(values):
    width = values.shape[-1]
    line = lax.broadcasted_iota(jnp.int32, (width, width), 0) // HD
    ones = (line == lanes((width, width)) // HD).astype(BF)
    front = values.astype(BF)
    back = (values - front.astype(F32)).astype(BF)
    return dot(front, ones) + dot(back, ones)


def partner(values):
    width = values.shape[-1]
    first = lanes(values.shape) % HD < HD // 2
    return jnp.where(
        first, pltpu.roll(values, width - HD // 2, 1), pltpu.roll(values, HD // 2, 1)
    )


def wide(table, width):
    return jnp.concatenate([table] * (width // table.shape[-1]), axis=-1)


def row_norm(values):
    return lax.rsqrt(jnp.mean(values * values, axis=-1, keepdims=True) + EPS)


def head_norm(values):
    return lax.rsqrt(group_sum(values * values) * (1.0 / HD) + EPS)


def head_norm_backward(values, gain, grads, cos, sin):
    width = values.shape[-1]
    grads = grads * wide(cos, width) - partner(grads) * wide(sin, width)
    scale = head_norm(values)
    normed = values * scale
    inner = grads * gain
    grad_in = scale * (inner - normed * (group_sum(inner * normed) * (1.0 / HD)))
    return grad_in, jnp.sum(grads * normed, axis=0, keepdims=True)


def place_of(iota, rows, rank):
    quarter = rows // 4
    part = iota // quarter
    relative = (part % 2) * 2 + part // 2
    return jnp.bitwise_xor(relative, rank) * quarter + iota % quarter


def stack(slab, kv_head):
    slab = slab.astype(F32)
    turned = pltpu.roll(slab, HD, 1)
    low = lanes(slab.shape) < HD
    if kv_head == 0:
        parts = [jnp.where(low, slab, 0.0), jnp.where(low, turned, 0.0)]
    else:
        parts = [jnp.where(low, 0.0, turned), jnp.where(low, 0.0, slab)]
    return jnp.concatenate(parts, axis=0)


def unstack(stacked, kv_head):
    rows = stacked.shape[0] // 2
    first, second = stacked[:rows], stacked[rows:]
    low = lanes(first.shape) < HD
    if kv_head == 0:
        return jnp.where(low, first, pltpu.roll(second, HD, 1))
    return jnp.where(low, pltpu.roll(first, HD, 1), second)


def qkv_kernel(
    x1, x2, x3, x0, gain, positions, wk, wv, key_gain, wq, query_gain,
    act_out, select_out, pair_out, query_rot_out, query_out, key_out,
    cos_out, sin_out, column_out, row_out, *scratch,
):
    sources = (x0, gain, positions, wk, wv, key_gain, wq, query_gain)
    buffers, sems = scratch[:-1], scratch[-1]
    copies = [
        pltpu.make_async_copy(source, buffer, sems.at[i])
        for i, (source, buffer) in enumerate(zip(sources, buffers, strict=True))
    ]
    for copy in copies:
        copy.start()
    for copy in copies:
        copy.wait()
    x0, gain, positions, wk, wv, key_gain, wq, query_gain = buffers
    ranks = (lax.axis_index("ctx"), lax.axis_index("mp"))
    rows = act_out.shape[0]
    line = lax.broadcasted_iota(jnp.int32, (rows, rows), 0)
    picked = place_of(line, rows, ranks[1]) == lanes((rows, rows))
    column = jnp.sum(
        jnp.where(picked, positions[...].astype(F32), 0.0), axis=1, keepdims=True
    )
    column_out[...] = column.astype(jnp.int32)
    row = jnp.sum(jnp.where(line == lanes((rows, rows)), column, 0.0), axis=0, keepdims=True)
    row_out[...] = row.astype(jnp.int32)
    lane = lanes((1, 128))
    power = (lane % (HD // 2)).astype(F32) * (-2.0 / HD)
    angles = column * jnp.exp(power * math.log(ROPE_BASE))
    cos = jnp.cos(angles)
    sin = jnp.sin(angles) * jnp.where(lane % HD < HD // 2, -1.0, 1.0)
    cos_out[...] = cos
    sin_out[...] = sin

    x = jnp.concatenate([x0[...], x1[...], x2[...], x3[...]], axis=0).astype(F32)
    act = (x * row_norm(x) * gain[...]).astype(BF)
    act_out[...] = act
    keys = dot(act, wk[...])
    key_out[...] = keys
    width = keys.shape[-1]
    normed = keys * head_norm(keys) * wide(key_gain[...], width)
    rotated = normed * wide(cos, width) + partner(normed) * wide(sin, width)
    pair_out[:, :width] = rotated.astype(BF)
    pair_out[:, width:] = dot(act, wv[...]).astype(BF)
    queries = dot(act, wq[...])
    query_out[...] = queries
    width = queries.shape[-1]
    normed = queries * head_norm(queries) * wide(query_gain[...], width)
    rotated = normed * wide(cos, width) + partner(normed) * wide(sin, width)
    query_rot_out[...] = rotated.astype(BF)
    select_columns(ranks, act_out, select_out)


def pack_kernel(cot, there_cot, packet_out):
    packet_out[:, : cot.shape[1]] = cot[...]
    packet_out[:, cot.shape[1] :] = there_cot[...]


def select_columns(ranks, source, target):
    columns = target.shape[1]
    blocks = columns // 128
    if blocks != 4:
        target[...] = jnp.zeros(target.shape, target.dtype)
        return
    for b in range(blocks):
        start = pl.multiple_of((2 * b + 1 - ranks[0] % 2) * 128, 128)
        target[:, b * 128 : (b + 1) * 128] = source[:, pl.ds(start, 128)]


def cotangent_kernel(ranks, p0, p1, p2, p3, wd, cot_out, there_out, grad_hidden_out):
    packet = jnp.concatenate([p0[...], p1[...], p2[...], p3[...]], axis=0)
    width = cot_out.shape[1]
    cot = packet[:, :width]
    cot_out[...] = cot
    grad_hidden_out[...] = dot(cot, wd[...], COLS)
    if width // lax.axis_size("ctx") != 128:
        there_out[...] = jnp.zeros(there_out.shape, BF)
        return
    source = packet[:, width:].astype(F32)
    for b in range(width // 256):
        low = source[:, 256 * b : 256 * b + 128]
        high = source[:, 256 * b + 128 : 256 * b + 256]
        there_out[:, 128 * b : 128 * (b + 1)] = jnp.where(ranks[0] % 2 == 1, high, low).astype(BF)


def attention_kernel(count, ranks, query_rot, positions, wo, act_select, *refs):
    slots = count // 2
    even = refs[:slots]
    crossed = refs[slots : 2 * slots]
    out_f32, out_b, sums_out, kept_out, sent_out = refs[2 * slots : 2 * slots + 5]
    odd = refs[2 * slots + 5 : -1]
    scores = refs[-1]
    rows = query_rot.shape[0]
    key_width = even[0].shape[1] // 2
    for j in range(slots):
        odd[j][...] = jnp.where(
            ranks[0] % 2 == 1,
            crossed[j][...].astype(F32),
            crossed[(j + 1) % slots][...].astype(F32),
        ).astype(BF)
    blocks = [(even, odd)[d % 2][d // 2] for d in range(count)]
    query_index = ranks[0] * rows + place_of(
        lax.broadcasted_iota(jnp.int32, (rows, 1), 0), rows, ranks[1]
    )
    first_seen = query_index - positions[...]
    key_place = place_of(lanes((1, rows)), rows, ranks[1])
    masks = []
    for d in range(count):
        key_index = (ranks[0] - d) * rows + key_place
        mask = key_index >= first_seen
        if d == 0:
            mask = mask & (key_index <= query_index)
        masks.append(jnp.where(mask, 0.0, MASKED_SCORE))
    for head in range(2):
        slab = query_rot[:, head * 128 : (head + 1) * 128]
        stacked = (stack(slab, head) * SCALE).astype(BF)
        top = jnp.full((2 * rows, 1), MASKED_SCORE, F32)
        for d in range(count):
            block = dot(stacked, blocks[d][:, :key_width], COLS)
            block = block + jnp.concatenate([masks[d], masks[d]], axis=0)
            scores[:, d * rows : (d + 1) * rows] = block
            top = jnp.maximum(top, jnp.max(block, axis=-1, keepdims=True))
        total = jnp.zeros((2 * rows, 1), F32)
        mixed = jnp.zeros((2 * rows, key_width), F32)
        for d in range(count):
            weights = jnp.exp(scores[:, d * rows : (d + 1) * rows] - top)
            total = total + jnp.sum(weights, axis=-1, keepdims=True)
            mixed = mixed + dot(weights.astype(BF), blocks[d][:, key_width:])
        sums = jnp.broadcast_to(top + jnp.log(total), (2 * rows, 128))
        sums_out[head : head + 1, :] = jnp.transpose(sums)[:1]
        out_f32[:, head * 128 : (head + 1) * 128] = unstack(mixed / total, head)
    attn_b = out_f32[...].astype(BF)
    chosen = act_select.shape[1]
    out_b[:, :chosen] = act_select[...]
    out_b[:, chosen:] = attn_b
    half = rows // 2
    kept_out[...] = dot(attn_b[:half], wo[...])
    sent_out[...] = dot(attn_b[half:], wo[...]).astype(BF)


def piece_kernel(packet, out):
    out[...] = packet[:, packet.shape[1] - 128 :]


def join_kernel(p0, p1, p2, p3, out):
    own = p0.shape[0] // 4
    for quarter, piece in enumerate((p0, p1, p2, p3)):
        for b in range(4):
            out[quarter * own : (quarter + 1) * own, 128 * b : 128 * (b + 1)] = piece[
                b * own : (b + 1) * own, :
            ]


def add_kernel(kept, arrived, out):
    out[...] = (kept[...].astype(F32) + arrived[...].astype(F32)).astype(out.dtype)


def flipped_add_kernel(kept, arrived, out):
    half = kept.shape[0] // 2
    for a, b in ((0, half), (half, 0)):
        total = kept[a : a + half, :].astype(F32) + arrived[b : b + half, :].astype(F32)
        out[a : a + half, :] = total.astype(out.dtype)


def fold_kernel(*refs):
    count = (len(refs) - 1) // 3
    back_out = refs[-1]
    place = 0
    for p in range(count):
        kept, arrived, front_out = refs[2 * p], refs[2 * p + 1], refs[2 * count + p]
        half, width = front_out.shape
        front_out[...] = kept[:half, :] + arrived[:half, :].astype(F32)
        back_out[:, place : place + width] = (
            kept[half:, :] + arrived[half:, :].astype(F32)
        ).astype(BF)
        place += width


def mp_fold_kernel(input_kept, out_kept, gains, arrived, input_front, out_front, gains_out, back):
    half = input_kept.shape[0]
    own = half // 2
    came = arrived[...].astype(F32)
    for place, kept, front in ((0, input_kept, input_front), (1, out_kept, out_front)):
        total = kept[...] + came[place * half : (place + 1) * half]
        front[...] = total[:own]
        back[place * own : (place + 1) * own, :] = total[own:].astype(BF)
    gains_out[...] = gains[...] + unpack(came[2 * half :], gains.shape[0])
    pack(gains_out[...], back, 2 * own)


def pack(values, target, start):
    count = values.shape[0]
    target[start : start + 16, :] = jnp.zeros((16, target.shape[1]), BF)
    front = values.astype(BF)
    for part, piece in enumerate((front.astype(F32), values - front.astype(F32))):
        for g in range(-(-count // 16)):
            rows = piece[16 * g : 16 * g + 16]
            if rows.shape[0] < 16:
                rows = jnp.concatenate([rows, jnp.zeros((16 - rows.shape[0], 128), F32)], axis=0)
            column = (2 * g + part) * 128
            target[start : start + 16, column : column + 128] = rows.astype(BF)


def unpack(values, count):
    pieces = []
    for g in range(-(-count // 16)):
        column = 2 * g * 128
        total = values[:, column : column + 128] + values[:, column + 128 : column + 256]
        pieces.append(total[: min(16, count - 16 * g)])
    return jnp.concatenate(pieces, axis=0)


def last_kernel(turned, *refs):
    count = len(turned)
    arrived, outs, token = refs[count], refs[count + 1 : -1], refs[-1]
    place = 0
    for p in range(count):
        width = refs[p].shape[1]
        total = refs[p][...] + arrived[:, place : place + width].astype(F32)
        outs[p][...] = jnp.transpose(total) if turned[p] else total
        place += width
    token[...] = jnp.zeros(token.shape, F32)


def attention_last_kernel(kept, arrived, out_grad, query_grad, key_grad, value_grad):
    total = kept[...] + arrived[...].astype(F32)
    turned = out_grad.shape[0]
    out_grad[...] = jnp.transpose(total[:, :turned])
    start = turned
    for out in (query_grad, key_grad, value_grad):
        width = out.shape[1]
        out[...] = total[:, start : start + width]
        start += width


def pair_sum_kernel(slots, ranks, *refs):
    odd = ranks[0] % 2 == 1
    terms, arrived = refs[:slots], refs[slots]
    outs = refs[slots + 1 :]
    rows = terms[0].shape[0]
    came = [arrived[j * rows : (j + 1) * rows, :].astype(F32) for j in range(slots)]
    outs[0][...] = terms[0][...] + jnp.where(odd, 0.0, came[0])
    for k in range(1, slots):
        outs[k][...] = (
            terms[k][...].astype(F32) + jnp.where(odd, came[k - 1], came[k])
        ).astype(BF)
    outs[slots][...] = came[slots - 1].astype(BF)


def down_kernel(hidden, wd, kept_out, sent_out):
    half = hidden.shape[0] // 2
    columns = wd.shape[0]
    sent_out[...] = dot(hidden[half:, :columns], wd[...]).astype(BF)
    kept_out[...] = dot(hidden[:half, :columns], wd[...])


def outputs_kernel(
    x, gain, grad_resid, resid, input_kept, out_kept, gains, arrived,
    grad_input_out, block_out, gains_out,
):
    own = block_out.shape[0]
    came = arrived[...].astype(F32)
    block_out[...] = (resid[:own, :] + out_kept[...] + came[own : 2 * own]).astype(BF)
    gains_out[...] = gains[...] + unpack(came[2 * own :], gains.shape[0])
    grads = input_kept[...] + came[:own]
    values = x[...].astype(F32)
    scale = row_norm(values)
    normed = values * scale
    inner = grads * gain[...]
    grad_input_out[...] = grad_resid[...] + scale * (
        inner - normed * jnp.mean(inner * normed, axis=-1, keepdims=True)
    )


def ffn_kernel(
    ranks, x0, x1, x2, x3, half0, half1, gain, wg, wu, grad_hidden,
    resid_out, act_out, hidden_out, grad_gate_out, grad_up_out, kept_out, sent_out, select,
):
    x = jnp.concatenate([x0[...], x1[...], x2[...], x3[...]], axis=0).astype(F32)
    resid = x + jnp.concatenate([half0[...], half1[...]], axis=0).astype(F32)
    resid_out[...] = resid
    act = (resid * row_norm(resid) * gain[...]).astype(BF)
    act_out[...] = act
    values = dot(act, wg[...])
    upper = dot(act, wu[...])
    sigmoid = jax.nn.sigmoid(values)
    columns = values.shape[1]
    hidden_out[:, :columns] = (values * sigmoid * upper).astype(BF)
    grads = grad_hidden[...]
    grad_gate = (grads * upper * sigmoid * (1.0 + values * (1.0 - sigmoid))).astype(BF)
    grad_up = (grads * values * sigmoid).astype(BF)
    own = select.shape[0]
    select_columns(ranks, act_out.at[:own, :], select)
    for b in range(4):
        hidden_out[b * own : (b + 1) * own, columns:] = select[:, 128 * b : 128 * (b + 1)]
    grad_gate_out[...] = grad_gate
    grad_up_out[...] = grad_up
    half = resid.shape[0] // 2
    sent_out[...] = (
        dot(grad_gate[half:], wg[...], COLS) + dot(grad_up[half:], wu[...], COLS)
    ).astype(BF)
    kept_out[...] = dot(grad_gate[:half], wg[...], COLS) + dot(grad_up[:half], wu[...], COLS)


def attention_backward_kernel(
    count, ranks, cot, resid, half0, half1, gain, wo, attn, sums, query_rot, positions, *refs
):
    blocks = refs[:count]
    grad_own_out, grad_b_out, select_out, gain_out, grad_query_out = refs[count : count + 5]
    even, odd = refs[count + 5 : -1], refs[-1]
    rows = query_rot.shape[0]
    terms = [
        even[d // 2] if d % 2 == 0 else odd.at[d // 2 * rows : (d // 2 + 1) * rows]
        for d in range(count)
    ]
    key_width = blocks[0].shape[1] // 2
    values = resid[...]
    scale = row_norm(values)
    normed = values * scale
    grads = jnp.concatenate([half0[...], half1[...]], axis=0).astype(F32)
    inner = grads * gain[...]
    grad_in = scale * (inner - normed * jnp.mean(inner * normed, axis=-1, keepdims=True))
    grad_resid = cot[...].astype(F32) + grad_in
    own = rows // 4
    grad_own_out[...] = grad_resid[:own]
    gain_out[...] = jnp.sum(grads[:own] * normed[:own], axis=0, keepdims=True)
    grad_resid_b = grad_resid.astype(BF)
    grad_b_out[...] = grad_resid_b
    select_columns(ranks, grad_b_out, select_out)
    grad_attn = dot(grad_resid_b, wo[...], COLS)
    delta = jnp.transpose(group_sum(grad_attn * attn[...]))
    grad_attn_b = grad_attn.astype(BF)

    query_index = ranks[0] * rows + place_of(lanes((1, rows)), rows, ranks[1])
    first_row = query_index - positions[...]
    key_place = place_of(lax.broadcasted_iota(jnp.int32, (rows, 1), 0), rows, ranks[1])
    stacked = [stack(query_rot[:, h * 128 : (h + 1) * 128], h) for h in range(2)]
    stacked_b = [s.astype(BF) for s in stacked]
    scaled = [(s * SCALE).astype(BF) for s in stacked]
    grads_b = [
        stack(grad_attn_b[:, h * 128 : (h + 1) * 128], h).astype(BF) for h in range(2)
    ]
    deltas = [
        jnp.concatenate(
            [delta[2 * h * HD : 2 * h * HD + 1], delta[(2 * h + 1) * HD : (2 * h + 1) * HD + 1]],
            axis=1,
        )
        for h in range(2)
    ]
    grad_query = [jnp.zeros((2 * rows, key_width), F32) for _ in range(2)]
    for d in range(count - 1, -1, -1):
        key_index = (ranks[0] - d) * rows + key_place
        mask = key_index >= first_row
        if d == 0:
            mask = mask & (key_index <= query_index)
        mask = jnp.where(mask, 0.0, MASKED_SCORE)
        mask = jnp.concatenate([mask, mask], axis=1)
        key_block = blocks[d][:, :key_width]
        value_block = blocks[d][:, key_width:]
        key_term = jnp.zeros((rows, key_width), F32)
        value_term = jnp.zeros((rows, key_width), F32)
        for h in range(2):
            scores = dot(key_block, scaled[h], COLS) + mask
            probs = jnp.exp(scores - sums[h : h + 1, :])
            grad_probs = dot(value_block, grads_b[h], COLS)
            grad_scores = (probs * (grad_probs - deltas[h]) * SCALE).astype(BF)
            key_term = key_term + dot(grad_scores, stacked_b[h])
            value_term = value_term + dot(probs.astype(BF), grads_b[h])
            grad_query[h] = grad_query[h] + dot(grad_scores, key_block, ROWS)
        terms[d][:, :key_width] = key_term.astype(terms[d].dtype)
        terms[d][:, key_width:] = value_term.astype(terms[d].dtype)
    for h in range(2):
        grad_query_out[:, h * 128 : (h + 1) * 128] = unstack(grad_query[h], h)


def query_backward_kernel(
    queries, gain, grads, cos, sin, wq, grad_out, gain_out, partial_out
):
    grad_in, gain_terms = head_norm_backward(queries[...], wide(gain[...], queries.shape[-1]), grads[...], cos[...], sin[...])
    grad_b = grad_in.astype(BF)
    grad_out[...] = grad_b
    gain_out[...] = gain_terms
    partial_out[...] = dot(grad_b, wq[...], COLS)


def key_backward_kernel(
    keys, gain, cos, sin, wk, wv, query_partial, x0, x1, x2, x3,
    ffn_gain_part, query_gain_part, out_sent, select, grad_query_b, term, *refs,
):
    shifted = refs[:-4]
    late_out, gains_out, kept_out, sent_out = refs[-4:]
    width = keys.shape[-1]
    grads = term[...]
    for other in shifted:
        grads = grads + other[...].astype(F32)
    grad_in, gain_terms = head_norm_backward(
        keys[...], wide(gain[...], width), grads[:, :width], cos[...], sin[...]
    )
    grad_b = grad_in.astype(BF)
    value_b = grads[:, width:].astype(BF)
    place = 0
    for piece in (select[...], grad_query_b[...], grad_b, value_b):
        late_out[:, place : place + piece.shape[1]] = piece
        place += piece.shape[1]
    partial = query_partial[...] + dot(grad_b, wk[...], COLS) + dot(value_b, wv[...], COLS)
    half = partial.shape[0] // 2
    kept_out[...] = partial[:half]
    sent_out[:half, :] = partial[half:].astype(BF)
    sent_out[half : 2 * half, :] = out_sent[...]
    x = jnp.concatenate([x0[...], x1[...], x2[...], x3[...]], axis=0).astype(F32)
    features = x.shape[1]
    parts = [
        jnp.sum(partial * (x * row_norm(x)), axis=0, keepdims=True),
        ffn_gain_part[...],
    ]
    row = 0
    for part in parts:
        for c in range(features // 128):
            gains_out[row : row + 1, :] = part[:, c * 128 : (c + 1) * 128]
            row += 1
    queries = query_gain_part[...]
    queries = sum(queries[:, c * 128 : (c + 1) * 128] for c in range(queries.shape[1] // 128))
    gains_out[row : row + 1, :] = queries
    gains_out[row + 1 : row + 2, :] = gain_terms
    pack(gains_out[...], sent_out, 2 * half)


def weight_grad_kernel(parts, ranks, *refs):
    kept_out, sent_out = refs[-2:]
    parity = ranks[0] % 2
    mine = ranks[0] // 2
    place = 0
    for p, (own, there_at, act_at, width) in enumerate(parts):
        act, arrived_act, grads, arrived_grads = refs[4 * p : 4 * p + 4]
        mine_grads = grads[:, own : own + width]
        other_grads = arrived_grads[:, there_at : there_at + width]
        for lo in (1, 0):
            for hi in range(2):
                block = jnp.bitwise_xor(mine, lo + 2 * hi)
                start = pl.multiple_of((2 * block + parity) * 128, 128)
                there = pl.multiple_of(act_at + block * 128, 128)
                total = dot(act[:, pl.ds(start, 128)], mine_grads, ROWS) + dot(
                    arrived_act[:, pl.ds(there, 128)], other_grads, ROWS
                )
                target = sent_out if lo else kept_out
                target[hi * 128 : (hi + 1) * 128, place : place + width] = total.astype(
                    target.dtype
                )
        place += width


def shape(dims, dtype):
    return jax.ShapeDtypeStruct(dims, dtype)


def launch(kernel, outs, args, scratch=(), name=None, after=(), carry=()):
    nbytes = sum(s.shape[0] * s.shape[1] * 4 for s in scratch)
    ranked = args[0] is RANKS
    args = list(args[ranked:])
    n_in, n_out, n_unused = len(args), len(outs), len(after) + len(carry)

    def run(*refs):
        results = refs[n_in + n_unused :]
        ranks = [(lax.axis_index("ctx"), lax.axis_index("mp"))] if ranked else []
        kernel(*ranks, *refs[:n_in], *results[:n_out], *results[n_out + len(carry) :])

    any_spec = pl.BlockSpec(memory_space=pl.ANY)
    return pl.pallas_call(
        run,
        out_shape=list(outs) + [shape(c.shape, c.dtype) for c in carry],
        in_specs=[pl.BlockSpec(memory_space=pltpu.VMEM)] * n_in + [any_spec] * n_unused,
        out_specs=[pl.BlockSpec(memory_space=pltpu.VMEM) for _ in outs] + [any_spec] * len(carry),
        scratch_shapes=list(scratch),
        input_output_aliases={n_in + len(after) + i: n_out + i for i in range(len(carry))},
        compiler_params=pltpu.CompilerParams(vmem_limit_bytes=nbytes + (12 << 20)),
        name=name,
    )(*args, *after, *carry)


def add(kept, arrived, dtype, name, kernel=add_kernel, after=(), carry=()):
    out = launch(
        kernel, [shape(kept.shape, dtype)], [kept, arrived], name=name, after=after, carry=carry
    )
    return out if carry else out[0]


def mp_gather(values):
    other = xor(values, "mp", 2)
    core = xor(values, "mp", 1)
    return values, other, core, xor(other, "mp", 1)


def split_columns(values):
    n = lax.axis_size("ctx")
    index = lax.axis_index("ctx")
    rows, columns = values.shape
    bits = n.bit_length() - 1
    parts = values.reshape((rows,) + (2,) * bits + (columns // n,))
    for bit in range(bits):
        parts = jnp.where((index >> bit) % 2 == 1, jnp.flip(parts, bits - bit), parts)
    order = [0] + [bits - b for b in range(bits)] + [bits + 1]
    parts = jnp.transpose(parts, order).reshape(rows, 2, columns // 2)
    return parts[:, 0], parts[:, 1]


def weight_grad(parts, name, after=()):
    n = lax.axis_size("ctx")
    act = parts[0][0]
    half = act.shape[1] // 4
    columns = sum(part[6] for part in parts)
    if n == 8 and act.shape[1] == 1024:
        return launch(
            functools.partial(weight_grad_kernel, [part[4] + part[5:] for part in parts]),
            [shape((half, columns), F32), shape((half, columns), BF)],
            [RANKS] + [a for part in parts for a in part[:4]],
            name=name,
            after=after,
        )
    totals = []
    for act, _, grads, arrived_grads, offsets, _, width in parts:
        own, other = split_columns(act)
        grads = grads[:, offsets[0] : offsets[0] + width]
        arrived_grads = arrived_grads[:, offsets[1] : offsets[1] + width]
        both = jnp.concatenate([own, xor(other, "ctx", 1)], axis=0)
        totals.append(dot(both, jnp.concatenate([grads, arrived_grads], axis=0), ROWS))
    total = jnp.concatenate(totals, axis=1)
    return total[:half], total[half:].astype(BF)


def fold(pairs, name, after=()):
    n = lax.axis_size("ctx")
    kept = [p[0] for p in pairs]
    arrived = [p[1] for p in pairs]
    mask = 4
    while mask < n:
        half = kept[0].shape[0] // 2
        widths = [k.shape[1] for k in kept]
        outs = launch(
            fold_kernel,
            [shape((half, w), F32) for w in widths] + [shape((half, sum(widths)), BF)],
            [a for pair in zip(kept, arrived, strict=True) for a in pair],
            name=name,
            after=after,
        )
        kept, back = outs[:-1], outs[-1]
        came = xor(back, "ctx", mask)
        mask *= 2
        if mask >= n:
            return kept, came, back
        arrived = []
        for w in widths:
            start = sum(a.shape[1] for a in arrived)
            arrived.append(came[:, start : start + w])
    return kept, came, back


def body(
    block_in,
    attn_gain,
    query_weight,
    key_weight,
    value_weight,
    out_weight,
    query_gain,
    key_gain,
    ffn_gain,
    gate_weight,
    up_weight,
    down_weight,
    segments,
    positions,
    cotangent,
):
    width = block_in.shape[1]
    key_width = key_weight.shape[1]
    query_width = query_weight.shape[1]
    hidden_width = gate_weight.shape[1]
    n_ctx = lax.axis_size("ctx")
    ctx_rank = lax.axis_index("ctx")
    own_rows = block_in.shape[0]
    rows = positions.shape[0]
    total_tokens = rows * n_ctx
    longest = LONGEST.get(total_tokens, total_tokens)
    window = min(n_ctx - 1, -(-(longest - 1) // rows))
    slots = (window + 1) // 2
    count = window + 1
    half = rows // 2

    x = mp_gather(block_in)
    query_gain_row = query_gain.reshape(1, -1)
    key_gain_row = key_gain.reshape(1, -1)
    attn_gain_row = attn_gain.reshape(1, -1)
    ffn_gain_row = ffn_gain.reshape(1, -1)

    outs = [
        shape((rows, width), BF),
        shape((rows, width // 2), BF),
        shape((rows, 2 * key_width), BF),
        shape((rows, query_width), BF),
        shape((rows, query_width), F32),
        shape((rows, key_width), F32),
        shape((rows, 128), F32),
        shape((rows, 128), F32),
        shape((rows, 1), jnp.int32),
        shape((1, rows), jnp.int32),
    ]
    copied = [block_in, attn_gain_row, positions.reshape(1, -1), key_weight, value_weight,
              key_gain_row, query_weight, query_gain_row]
    (
        act_attn, act_attn_select, pair, query_rot, queries, keys_pre,
        cos, sin, position_column, position_row,
    ) = pl.pallas_call(
        qkv_kernel,
        out_shape=outs,
        in_specs=[pl.BlockSpec(memory_space=pltpu.VMEM)] * 3
        + [pl.BlockSpec(memory_space=pl.ANY)] * len(copied),
        out_specs=[pl.BlockSpec(memory_space=pltpu.VMEM)] * len(outs),
        scratch_shapes=[pltpu.VMEM(a.shape, a.dtype) for a in copied]
        + [pltpu.SemaphoreType.DMA((len(copied),))],
        compiler_params=pltpu.CompilerParams(vmem_limit_bytes=52 << 20),
        name="qkv",
    )(*x[1:], *copied)

    def climb(step):
        pairs = [(i, i + step) for i in range(n_ctx - step)]
        return lax.ppermute(pair, "ctx", pairs) if pairs else jnp.zeros_like(pair)

    even = [pair] + [climb(2 * k) for k in range(1, slots)]
    farthest = 2 * slots - 1
    pairs = [(i, i + 1) for i in range(0, n_ctx, 2)]
    pairs += [(i, i + farthest) for i in range(1, n_ctx - farthest, 2)]
    crossed = [lax.ppermute(pair, "ctx", pairs)] + [xor(e, "ctx", 1) for e in even[1:]]
    packet = launch(
        pack_kernel,
        [shape((own_rows, 2 * width), BF)],
        [cotangent, xor(cotangent, "ctx", 1)],
        name="pack",
        after=[pair],
    )[0]
    packets = mp_gather(packet)

    outs = launch(
        functools.partial(attention_kernel, count),
        [
            shape((rows, query_width), F32),
            shape((rows, width // 2 + query_width), BF),
            shape((2, 2 * rows), F32),
            shape((half, width), F32),
            shape((half, width), BF),
        ]
        + [shape((rows, 2 * key_width), BF) for _ in range(slots)],
        [RANKS, query_rot, position_column, out_weight, act_attn_select,
         *even, *crossed],
        scratch=[pltpu.VMEM((2 * rows, count * rows), F32)],
        name="attention",
        after=packets[1:3],
    )
    attn_rows, early, log_sums, kept, sent = outs[:5]
    blocks = [(even, outs[5:])[d % 2][d // 2] for d in range(count)]
    chosen = width // 2

    kept = add(kept, xor(sent, "mp", 1), BF, "resid_core")
    cot, cot_there, grad_hidden = launch(
        cotangent_kernel,
        [
            shape((rows, width), BF),
            shape((rows, chosen), BF),
            shape((rows, hidden_width), F32),
        ],
        [RANKS, *packets, down_weight],
        name="cotangent",
        after=[kept],
    )
    early_there = xor(early, "ctx", 1)
    both = add(
        kept, xor(kept, "mp", 2), BF, "resid_chip", kernel=flipped_add_kernel,
        after=[grad_hidden],
    )

    resid, act_ffn, hidden, grad_gate, grad_up, kept, sent = launch(
        ffn_kernel,
        [
            shape((rows, width), F32),
            shape((rows, width), BF),
            shape((rows, hidden_width + 128), BF),
            shape((rows, hidden_width), BF),
            shape((rows, hidden_width), BF),
            shape((half, width), F32),
            shape((half, width), BF),
        ],
        [RANKS, *x, both, xor(both, "mp", 1), ffn_gain_row, gate_weight, up_weight, grad_hidden],
        scratch=[pltpu.VMEM((own_rows, chosen), BF)],
        name="ffn",
    )
    hidden_there = xor(hidden, "ctx", 1)
    kept, grad_gate = add(kept, xor(sent, "mp", 1), BF, "grad_act_core", carry=[grad_gate])
    gate_there = xor(grad_gate, "ctx", 1)
    both = add(kept, xor(kept, "mp", 2), BF, "grad_act_chip", kernel=flipped_add_kernel)
    act_piece = launch(
        piece_kernel, [shape((rows, 128), BF)], [hidden_there], name="piece", after=[both]
    )[0]
    down_kept, down_sent = weight_grad(
        [(cot, cot_there, hidden, hidden_there, (0, 0), 0, hidden_width)], "down_grad",
        after=[act_piece],
    )

    outs = launch(
        functools.partial(attention_backward_kernel, count),
        [
            shape((own_rows, width), F32),
            shape((rows, width), BF),
            shape((rows, chosen), BF),
            shape((1, width), F32),
            shape((rows, query_width), F32),
        ]
        + [shape((rows, 2 * key_width), BF if d else F32) for d in range(slots)]
        + [shape((slots * rows, 2 * key_width), BF)],
        [RANKS, cot, resid, both, xor(both, "mp", 1), ffn_gain_row, out_weight, attn_rows,
         log_sums, query_rot, position_row, *blocks],
        name="attention_backward",
        after=[down_sent],
    )
    grad_resid, grad_resid_b, grad_select, ffn_gain_part, grad_query = outs[:5]
    terms, odd_terms = outs[5:-1], outs[-1]

    arrived = xor(odd_terms, "ctx", 1)
    down_arrived = xor(down_sent, "ctx", 2)
    act_there = launch(
        join_kernel,
        [shape((rows, chosen), BF)],
        mp_gather(act_piece),
        name="join",
        after=[grad_query],
    )[0]
    gate_kept, gate_sent = weight_grad(
        [(act_ffn, act_there, grad_gate, gate_there, (0, 0), 0, hidden_width)],
        "gate_grad",
        after=[grad_query, down_arrived],
    )
    totals = launch(
        functools.partial(pair_sum_kernel, slots),
        [shape(terms[0].shape, BF if k else F32) for k in range(slots + 1)],
        [RANKS, *terms, arrived],
        name="pair_sums",
        after=[gate_sent],
        carry=[grad_up],
    )
    grad_up = totals[-1]
    up_there = xor(grad_up, "ctx", 1)
    shifted = [down(totals[k], 2 * k) for k in range(slots - 1, 0, -1)]
    if 2 * slots < n_ctx:
        pairs = [(i, i - 2 * slots) for i in range(2 * slots, n_ctx) if i % 2 == 1]
        shifted.append(lax.ppermute(totals[slots], "ctx", pairs))

    grad_query_b, query_gain_part, query_partial = launch(
        query_backward_kernel,
        [
            shape((rows, query_width), BF),
            shape((1, query_width), F32),
            shape((rows, width), F32),
        ],
        [queries, query_gain_row, grad_query, cos, sin, query_weight],
        name="query_backward",
        after=[totals[0]],
    )
    out_kept, out_sent = launch(
        down_kernel,
        [shape((half, width), F32), shape((half, width), BF)],
        [hidden, down_weight],
        name="down",
        after=[query_partial],
    )
    (down_kept, gate_kept), first_arrived, back = fold(
        [(down_kept, down_arrived), (gate_kept, xor(gate_sent, "ctx", 2))],
        "first_fold",
        after=[out_sent],
    )
    up_kept, up_sent = weight_grad(
        [(act_ffn, act_there, grad_up, up_there, (0, 0), 0, hidden_width)], "up_grad",
        after=[back],
    )
    late, gains, kept, sent = launch(
        key_backward_kernel,
        [
            shape((rows, chosen + query_width + 2 * key_width), BF),
            shape((2 * width // 128 + 2, 128), F32),
            shape((half, width), F32),
            shape((rows + 16, width), BF),
        ],
        [keys_pre, key_gain_row, cos, sin, key_weight, value_weight, query_partial, *x,
         ffn_gain_part, query_gain_part, out_sent, grad_select, grad_query_b, totals[0],
         *shifted],
        name="key_backward",
        after=[up_sent],
    )
    late_there = xor(late, "ctx", 1)
    core_arrived = xor(sent, "mp", 1)
    query_at = chosen
    pair_at = chosen + query_width
    input_kept, out_kept, gains, back = launch(
        mp_fold_kernel,
        [
            shape((own_rows, width), F32),
            shape((own_rows, width), F32),
            shape(gains.shape, F32),
            shape((half + 16, width), BF),
        ],
        [kept, out_kept, gains, core_arrived],
        name="mp_fold",
    )
    grad_input, block_out, gains = launch(
        outputs_kernel,
        [
            shape((own_rows, width), F32),
            shape((own_rows, width), BF),
            shape(gains.shape, F32),
        ],
        [x[0], attn_gain_row, grad_resid, resid, input_kept, out_kept, gains,
         xor(back, "mp", 2)],
        name="outputs",
        after=[early_there],
    )
    attn_kept, attn_sent = weight_grad(
        [
            (grad_resid_b, late_there, early, early_there, (chosen, chosen), 0, query_width),
            (act_attn, early_there, late, late_there, (query_at, query_at), 0, query_width),
            (act_attn, early_there, late, late_there, (pair_at, pair_at), 0, 2 * key_width),
        ],
        "attention_grads",
        after=[gains],
    )
    gains = add(gains, xor(gains, "ctx", 1), F32, "gains", after=[attn_sent])
    (up_kept,), up_arrived, back = fold(
        [(up_kept, xor(up_sent, "ctx", 2))], "up_fold", after=[gains]
    )
    token = shape((8, 128), F32)
    down_grad, gate_grad, done = launch(
        functools.partial(last_kernel, (True, False)),
        [shape(down_kept.shape[::-1], F32), shape(gate_kept.shape, F32), token],
        [down_kept, gate_kept, first_arrived],
        name="first_last",
        after=[back],
    )
    mask = 2
    while mask < n_ctx // 2:
        gains = add(gains, xor(gains, "ctx", mask), F32, "gains", after=[done])
        mask *= 2
    (attn_kept,), attn_arrived, back = fold(
        [(attn_kept, xor(attn_sent, "ctx", 2))], "attention_fold", after=[done]
    )
    up_grad, done = launch(
        functools.partial(last_kernel, (False,)),
        [shape(up_kept.shape, F32), token],
        [up_kept, up_arrived],
        name="up_last",
        after=[back],
    )
    gains = add(gains, xor(gains, "ctx", mask), F32, "gains", after=[done])
    out_grad, query_grad, key_grad, value_grad = launch(
        attention_last_kernel,
        [shape((query_width, attn_kept.shape[0]), F32)]
        + [shape((attn_kept.shape[0], w), F32) for w in (query_width, key_width, key_width)],
        [attn_kept, attn_arrived],
        name="attention_last",
        after=[gains],
    )
    gains = gains.reshape(-1)
    heads = gains[2 * width :].reshape(2, -1, HD).sum(axis=1)
    query_gains, key_gains = heads[0], heads[1]
    return (
        block_out,
        grad_input,
        query_grad,
        key_grad,
        value_grad,
        out_grad,
        gate_grad,
        up_grad,
        down_grad,
        gains[:width],
        gains[width : 2 * width],
        query_gains,
        key_gains,
    )


def solution(mesh):
    in_specs = (
        P(("ctx", "mp"), None),
        P(),
        P(None, "mp"),
        P(None, "mp"),
        P(None, "mp"),
        P("mp", None),
        P(),
        P(),
        P(),
        P(None, "mp"),
        P(None, "mp"),
        P("mp", None),
        P(),
        P("ctx"),
        P(("ctx", "mp"), None),
    )
    out_specs = (
        P(("ctx", "mp"), None),
        P(("ctx", "mp"), None),
        P("ctx", "mp"),
        P("ctx", "mp"),
        P("ctx", "mp"),
        P("mp", "ctx"),
        P("ctx", "mp"),
        P("ctx", "mp"),
        P("mp", "ctx"),
        P(),
        P(),
        P(),
        P(),
    )
    return jax.shard_map(body, mesh=mesh, in_specs=in_specs, out_specs=out_specs, check_vma=False)
```
